32 devices in a mesh: seq: 16 (over z, y, core), batch: 2 (over x).
Axes of the slice: x: 2, y: 2, z: 4, core: 2. Of those that a mesh axis runs over, the one named last changes fastest.
Arguments:
- tokens: bfloat16 [4, 1024, 768], P('batch', 'seq'), may hold values from -6 to 6
- doc_lengths: int32 [4, 4], P('batch'), may hold values from 1 to 1021, as said below
- weights: bfloat16 [2, 9216, 768], P(None, ('seq', 'batch')), may hold values from -0.75 to 0.75
- norm_gain: float32 [2, 2, 768], replicated, may hold values from 0.25 to 1.75
- norm_bias: float32 [2, 2, 768], replicated, may hold values from -1.5 to 1.5
- fmap: float32 [2, 2, 64, 768], replicated, may hold values from -0.75 to 0.75
- cotangent: bfloat16 [4, 1024, 768], P('batch', 'seq'), may hold values from -33 to 33
Outputs:
- output: bfloat16 [4, 1024, 768], P('batch', 'seq')
- grad_tokens: float32 [4, 1024, 768], P('batch', 'seq')
- grad_weights: float32 [2, 9216, 768], P(None, ('seq', 'batch'))
- grad_gain: float32 [2, 2, 768], replicated
- grad_bias: float32 [2, 2, 768], replicated
- grad_fmap: float32 [2, 2, 64, 768], replicated
The draws below stay inside these ranges and needn't reach their ends.
Inputs may be any that keep to these rules, and one draw needn't show every extreme that they name: `doc_lengths`: each row's 4 lengths are positive and sum to 1024.
All inputs are finite; a program needn't handle non-finite values.
Results may differ from the reference program's by a relative error of at most 0.012.
Values may be sent and summed in bfloat16 or wider, within the bound.
No kernel may reach another device: no remote copies, remote signals or barrier semaphores. Data moves between devices by JAX's collectives and lax.ppermute only.
A program may use at most 320 MiB of HBM per device.

```python
import jax
import jax.numpy as jnp
from jax import lax

D = 768
H = 12
HD = 64
FEAT = 128
FF = 3072
LAYERS = 2
DOCS = 4
TOK_SEQ = 64
SEQS_DEV = 2
LENGTH = 1024
SEQUENCES = 4


def draw_doc_lengths(key, part):
    key = jax.random.fold_in(key, 5)
    cut_key, pick_key = jax.random.split(key)
    row_keys = jax.random.split(cut_key, SEQUENCES)

    def one_row(row_key):
        cuts = jax.random.choice(row_key, LENGTH - 1, (DOCS - 1,), replace=False) + 1
        cuts = jnp.sort(cuts).astype(jnp.int32)
        edges = jnp.concatenate([jnp.zeros((1,), jnp.int32), cuts, jnp.full((1,), LENGTH, jnp.int32)])
        return (edges[1:] - edges[:-1]).astype(jnp.int32)
    lengths = jax.vmap(one_row)(row_keys)
    picked = jax.random.randint(pick_key, (SEQUENCES // SEQS_DEV,), 0, SEQS_DEV)
    indices = jnp.arange(SEQUENCES)
    whole_row = indices % SEQS_DEV == picked[indices // SEQS_DEV]
    single = jnp.concatenate([jnp.full((1,), LENGTH - DOCS + 1, jnp.int32), jnp.ones((DOCS - 1,), jnp.int32)])
    return jnp.where(whole_row[:, None], single[None, :], lengths).astype(jnp.int32)


def draw_weights(key, part):
    key = jax.random.fold_in(key, 11)
    total_rows = 4 * D + 2 * FF
    base = jnp.clip(jax.random.normal(key, (LAYERS, total_rows, D), jnp.float32), -3.0, 3.0)
    index = jnp.arange(total_rows)
    scale = jnp.where(index < 3 * D, D ** (-0.5), jnp.where(index < 4 * D, max(D // 64, 1) ** (-0.5), jnp.where(index < 4 * D + FF, D ** (-0.5), FF ** (-0.5))))
    values = jnp.clip(base * scale[None, :, None].astype(jnp.float32), -0.75, 0.75)
    return values.astype(jnp.bfloat16)


def draw_cotangent(key, part):
    key = jax.random.fold_in(key, 17)
    base_key, rough_key = jax.random.split(key)
    shape = (SEQUENCES, LENGTH, D)
    base = jnp.clip(jax.random.normal(base_key, shape, jnp.float32), -4.0, 4.0)
    rise = 6.0
    rough = jax.random.uniform(rough_key, (SEQUENCES, LENGTH, 1), jnp.float32, 0.5, 1.5)
    position = jnp.exp(jnp.log(rise) * jnp.arange(LENGTH).astype(jnp.float32) / LENGTH)
    sequence = jnp.exp(jnp.log(3.0) * jnp.arange(SEQUENCES).astype(jnp.float32) / SEQUENCES)
    values = 0.3 * base * rough * position[None, :, None] * sequence[:, None, None]
    return jnp.clip(values, -33.0, 33.0).astype(jnp.bfloat16)


def levels(key, shape, cuts, smallest, largest):
    def one(axis_at, blocks):
        steps = jax.random.uniform(jax.random.fold_in(jax.random.fold_in(key, 6), axis_at), (blocks,), jnp.float32, smallest / len(cuts), largest / len(cuts))
        return jnp.repeat(jnp.exp(steps), shape[axis_at] // blocks).reshape((-1,) + (1,) * (len(shape) - axis_at - 1))

    loudness = one(*cuts[0])
    for cut in cuts[1:]:
        loudness = loudness * one(*cut)
    return loudness


def bell_draw(rng, dims, spread, reach, cuts=(), held_as=jnp.bfloat16):
    values = jax.random.normal(rng, dims, jnp.float32) * spread
    if len(cuts) > 0:
        values = levels(rng, dims, cuts, -0.22, 0.18) * values
    return jnp.clip(values, min=-reach, max=reach).astype(held_as)


def setup_inputs(seed: int = 0) -> dict:
    arg_keys = jax.random.split(jax.random.key(seed), 8)
    tokens = bell_draw(arg_keys[0], (SEQUENCES, LENGTH, D), 1.0, 6.0, ((0, 2), (1, 16)))
    doc_lengths = draw_doc_lengths(jax.random.fold_in(arg_keys[7], 71), 0)
    weights = draw_weights(jax.random.fold_in(arg_keys[7], 71), 0)
    norm_gain = jnp.clip(1.0 + 0.15 * jax.random.normal(arg_keys[3], (LAYERS, 2, D), jnp.float32), 0.25, 1.75)
    norm_bias = bell_draw(arg_keys[4], (LAYERS, 2, D), 0.3, 1.5, (), jnp.float32)
    fmap = bell_draw(arg_keys[5], (LAYERS, 2, HD, D), HD ** -0.5, 0.75, (), jnp.float32)
    cotangent = draw_cotangent(jax.random.fold_in(arg_keys[7], 71), 0)
    return {"tokens": tokens, "doc_lengths": doc_lengths, "weights": weights, "norm_gain": norm_gain, "norm_bias": norm_bias, "fmap": fmap, "cotangent": cotangent}


HIGH = lax.Precision.HIGHEST
EPSILON = 1e-05

@jax.custom_vjp
def low(v):
    return lax.optimization_barrier(v.astype(jnp.bfloat16)).astype(jnp.float32)

@jax.custom_vjp
def low_back(v):
    return v

def low_keep(v):
    return (low(v), None)

def low_pass(kept, grad):
    return (grad,)

def back_keep(v):
    return (v, None)

def back_low(kept, grad):
    return (low(grad),)
low.defvjp(low_keep, low_pass)
low_back.defvjp(back_keep, back_low)

def layer_norm(values, gain, bias):
    mean = lax.optimization_barrier(jnp.mean(values, axis=-1, keepdims=True))
    centred = values - mean
    variance = lax.optimization_barrier(jnp.mean(centred * centred, axis=-1, keepdims=True))
    return centred * lax.rsqrt(variance + EPSILON) * gain + bias

def feature_map(values, table):
    grid = table.reshape(HD, H, HD)
    before = jnp.einsum('thi,ihj->thj', values, grid, precision=HIGH)
    return jnp.concatenate([jax.nn.softmax(before, axis=-1), jax.nn.softmax(-before, axis=-1)], axis=-1)

def attend_block(carry, inputs):
    state, normaliser, previous = carry
    query_feat, key_feat, values, documents = inputs
    span = documents.shape[0]
    use_state = (documents == previous).astype(jnp.float32)
    places = jnp.arange(span)
    visible = ((places[:, None] >= places[None, :]) & (documents[:, None] == documents[None, :])).astype(jnp.float32)
    scores = low_back(jnp.einsum('thf,shf->hts', query_feat, key_feat, precision=HIGH) * visible[None])
    numerator = jnp.einsum('hts,she->the', low(scores), values, precision=HIGH)
    denominator = jnp.transpose(lax.optimization_barrier(jnp.sum(scores, axis=2)))
    numerator = numerator + use_state[:, None, None] * jnp.einsum('thf,hfe->the', query_feat, state, precision=HIGH)
    denominator = denominator + use_state[:, None] * jnp.einsum('thf,hf->th', query_feat, normaliser, precision=HIGH)
    output = numerator / denominator[:, :, None]
    last_doc = documents[span - 1]
    keeping = (previous == last_doc).astype(jnp.float32)
    chosen = (documents == last_doc).astype(jnp.float32)
    state = keeping * state + jnp.einsum('thf,the->hfe', key_feat * chosen[:, None, None], values, precision=HIGH)
    normaliser = keeping * normaliser + jnp.einsum('thf,t->hf', key_feat, chosen, precision=HIGH)
    return ((state, normaliser, last_doc), output)

def block_forward(residual, documents, flat, gains, biases, tables):
    qkv_weight = flat[:3 * D]
    out_weight = flat[3 * D:4 * D]
    up_weight = flat[4 * D:4 * D + FF]
    down_weight = flat[4 * D + FF:]
    hidden = low(layer_norm(residual, gains[0], biases[0]))
    projected = low(low_back(jnp.dot(hidden, qkv_weight.T, precision=HIGH)))
    queries = projected[:, :D].reshape(LENGTH, H, HD)
    keys = projected[:, D:2 * D].reshape(LENGTH, H, HD)
    values = projected[:, 2 * D:].reshape(LENGTH, H, HD)
    query_feat = low(feature_map(queries, tables[0]))
    key_feat = low(feature_map(keys, tables[1]))
    blocks = LENGTH // TOK_SEQ
    start = (jnp.zeros((H, FEAT, HD), jnp.float32), jnp.zeros((H, FEAT), jnp.float32), jnp.int32(-1))
    xs = (query_feat.reshape(blocks, TOK_SEQ, H, FEAT), key_feat.reshape(blocks, TOK_SEQ, H, FEAT), values.reshape(blocks, TOK_SEQ, H, HD), documents.reshape(blocks, TOK_SEQ))
    unused, outputs = lax.scan(jax.checkpoint(attend_block), start, xs)
    attended = low(low_back(outputs.reshape(LENGTH, D)))
    residual = residual + low_back(jnp.dot(attended, out_weight, precision=HIGH))
    hidden = low(layer_norm(residual, gains[1], biases[1]))
    up_proj = low_back(jnp.dot(hidden, up_weight.T, precision=HIGH))
    activated = low(jax.nn.gelu(up_proj, approximate=True))
    return residual + low_back(jnp.dot(activated, down_weight, precision=HIGH))

def row_forward(residual, lengths, flat, gains, biases, tables):
    ends = jnp.cumsum(lengths).astype(jnp.int32)
    places = jnp.arange(LENGTH).astype(jnp.int32)
    documents = lax.optimization_barrier(jnp.sum((places[:, None] >= ends[None, :]).astype(jnp.int32), axis=1)).astype(jnp.int32)
    for layer in range(LAYERS):
        residual = block_forward(residual, documents, flat[layer], gains[layer], biases[layer], tables[layer])
    return residual

def reference(tokens, doc_lengths, weights, norm_gain, norm_bias, fmap, cotangent):

    def forward(inputs, flat, gains, biases, tables):

        def one_row(row):
            return row_forward(row[0], row[1], flat, gains, biases, tables)
        return lax.map(jax.checkpoint(one_row), (inputs, doc_lengths))
    result, pull = jax.vjp(forward, tokens.astype(jnp.float32), weights.astype(jnp.float32), norm_gain, norm_bias, fmap)
    grads = pull(cotangent.astype(jnp.float32))
    return (result.astype(jnp.bfloat16), grads[0], grads[1], grads[2], grads[3], grads[4])
```

```python
import jax
import jax.numpy as jnp
from jax import lax
from jax.sharding import PartitionSpec as P

D = 768
H = 12
HD = 64
FF = 3072
LAYERS = 2


HIGH = lax.Precision.HIGHEST
EPSILON = 1e-05
LOWTYPE = jnp.bfloat16
WIDETYPE = jnp.float32


AXES = ("seq", "batch")


class Net:
    def __init__(self):
        self.nz = lax.axis_size("seq") // 4
        self.nb = lax.axis_size("batch")
        place = lax.axis_index("seq")
        self.z = place // 4
        self.y = (place // 2) % 2
        self.c = place % 2
        self.b = lax.axis_index("batch")

    def move(self, array, target):
        pairs = []
        for index in range(self.nz * 4 * self.nb):
            place = index // self.nb
            goal = target(place // 4, (place // 2) % 2, place % 2, index % self.nb)
            if goal is not None:
                z, y, c, b = goal
                pairs.append((index, ((z * 2 + y) * 2 + c) * self.nb + b))
        return lax.ppermute(array, AXES, pairs)

    def core(self, array):
        return self.move(array, lambda z, y, c, b: (z, y, 1 - c, b))

    def flip_y(self, array):
        return self.move(array, lambda z, y, c, b: (z, 1 - y, c, b))

    def turn_b(self, array, step):
        return self.move(array, lambda z, y, c, b: (z, y, c, (b + step) % self.nb))

    def shift_z(self, array, step):
        def target(z, y, c, b):
            return (z + step, y, c, b) if 0 <= z + step < self.nz else None

        return self.move(array, target)


def pick(array, index, axis=0):
    return lax.dynamic_index_in_dim(array, index, axis, False)


def last_docs(doc_lengths, span):
    ends = jnp.cumsum(doc_lengths, axis=1)

    def last_doc(block):
        found = jnp.sum(((block + 1) * span - 1 >= ends).astype(jnp.int32), axis=1)
        return jnp.where(block < 0, -1, found)

    return last_doc


def scan_states(net, packed, last_doc, reverse, low=LOWTYPE):
    wide = WIDETYPE
    base = 4 * net.z
    first = base + 2 * net.y

    def gate(a, b):
        same = (last_doc(a) == last_doc(b)).astype(wide)
        return pick(same, net.c)

    mine = pick(packed, net.c)
    theirs = net.core(pick(packed, 1 - net.c))
    zero = jnp.equal(net.c, 0)
    part0 = jnp.where(zero, mine, theirs).astype(wide)
    part1 = jnp.where(zero, theirs, mine).astype(wide)
    if reverse:
        chip = part0 + gate(first, first - 1) * part1
    else:
        chip = gate(first, first + 1) * part0 + part1
    chip = chip.astype(low)
    own = pick(chip, net.y)
    other = net.flip_y(pick(chip, 1 - net.y))
    down = jnp.equal(net.y, 0)
    row0 = jnp.where(down, own, other).astype(wide)
    row1 = jnp.where(down, other, own).astype(wide)
    if reverse:
        plane = row0 + gate(base + 1, base - 1) * row1
    else:
        plane = gate(base + 1, base + 3) * row0 + row1
    plane = plane.astype(low)
    entering = jnp.zeros(plane.shape, wide)
    for step in range(1, net.nz):
        if reverse:
            entering = entering + gate(4 * (net.z + step) - 1, base + 3) * net.shift_z(plane, -step)
        else:
            entering = entering + gate(4 * (net.z - step) + 3, base - 1) * net.shift_z(plane, step)
    if reverse:
        row1_in = entering
        row0_in = gate(base + 3, base + 1) * entering + row1
    else:
        row0_in = entering
        row1_in = gate(base - 1, base + 1) * entering + row0
    own_in = jnp.where(down, row0_in, row1_in)
    other_in = net.flip_y(jnp.where(down, row1_in, row0_in).astype(low)).astype(wide)
    chip_in = jnp.where(down, jnp.stack([own_in, other_in]), jnp.stack([other_in, own_in]))
    if reverse:
        core1_in = chip_in
        core0_in = gate(first + 1, first) * chip_in + part1
    else:
        core0_in = chip_in
        core1_in = gate(first - 1, first) * chip_in + part0
    core0_in = core0_in.astype(low)
    core1_in = core1_in.astype(low)
    kept = jnp.where(zero, core0_in, core1_in)
    sent = net.core(jnp.where(zero, core1_in, core0_in))
    return jnp.where(zero, jnp.stack([kept, sent]), jnp.stack([sent, kept]))


def scatter_planes(net, grads, first, last):
    planes = last - first
    wide = WIDETYPE
    low = LOWTYPE
    grads = grads.reshape(planes, 2, 2, net.nb, -1, D)
    kept = pick(grads, net.c, 2).astype(wide)
    summed = (kept + net.core(pick(grads, 1 - net.c, 2)).astype(wide)).astype(low)
    half = summed.shape[3] // 2

    def over_b(value, axis):
        total = pick(value, net.b, axis).astype(wide)
        for step in range(1, net.nb):
            total = total + net.turn_b(pick(value, (net.b + step) % net.nb, axis), step).astype(wide)
        return total.astype(low)

    def over_y(value):
        got = net.flip_y(pick(value, 1 - net.y, 1))
        return (pick(value, net.y, 1).astype(wide) + got.astype(wide)).astype(low)

    left = over_y(over_b(summed[:, :, :, :half], 2))
    right = over_b(over_y(summed[:, :, :, half:]), 1)
    rows = jnp.concatenate([left, right], axis=1)
    total = pick(rows, jnp.clip(net.z - first, 0, planes - 1)).astype(wide)
    for step in range(1, net.nz):
        goal = (net.z + step) % net.nz
        value = pick(rows, jnp.clip(goal - first, 0, planes - 1))

        def target(z, y, c, b, step=step):
            to = (z + step) % net.nz
            return (to, y, c, b) if first <= to < last else None

        total = total + net.move(value, target).astype(wide)
    return total


def sum_everywhere(net, array):
    wide = WIDETYPE

    def exchange(value, target):
        value = value.astype(LOWTYPE)
        return value.astype(wide) + net.move(value, target).astype(wide)

    array = exchange(array, lambda z, y, c, b: (z, y, 1 - c, b))
    array = exchange(array, lambda z, y, c, b: (z, 1 - y, c, b))
    step = 1
    while step < net.nb:
        array = exchange(array, lambda z, y, c, b, step=step: (z, y, c, b ^ step))
        step *= 2
    step = 1
    while step < net.nz:
        array = exchange(array, lambda z, y, c, b, step=step: (z ^ step, y, c, b))
        step *= 2
    return array


def layer_norm(values, gain, bias):
    mean = jnp.mean(values, axis=-1, keepdims=True)
    centred = values - mean
    variance = jnp.mean(centred * centred, axis=-1, keepdims=True)
    return centred * lax.rsqrt(variance + EPSILON) * gain + bias


def feature_map(values, table):
    grid = table.reshape(HD, H, HD)
    high = grid.astype(LOWTYPE)
    rest = (grid - high.astype(WIDETYPE)).astype(LOWTYPE)
    values = values.astype(LOWTYPE)
    before = jnp.einsum("sthi,ihj->sthj", values, high, preferred_element_type=WIDETYPE)
    before = before + jnp.einsum("sthi,ihj->sthj", values, rest, preferred_element_type=WIDETYPE)
    return jnp.concatenate(
        [jax.nn.softmax(before, axis=-1), jax.nn.softmax(-before, axis=-1)], axis=-1
    )


def gelu_tanh(values):
    return jax.nn.gelu(values, approximate=True)


def split_flat(flat):
    return (flat[: 3 * D], flat[3 * D : 4 * D], flat[4 * D : 4 * D + FF], flat[4 * D + FF :])


def doc_layout(doc_lengths, start, span):
    ends = jnp.cumsum(doc_lengths, axis=1)
    places = start + jnp.arange(span, dtype=jnp.int32)
    documents = jnp.sum((places[None, :, None] >= ends[:, None, :]).astype(jnp.int32), axis=2)
    before = jnp.sum((start - 1 >= ends).astype(jnp.int32), axis=1)
    previous = jnp.where(start > 0, before, -1)
    last_doc = documents[:, span - 1]
    keeping = (previous == last_doc).astype(WIDETYPE)
    use_state = (documents == previous[:, None]).astype(WIDETYPE)
    chosen = (documents == last_doc[:, None]).astype(WIDETYPE)
    lower = jnp.arange(span)[:, None] >= jnp.arange(span)[None, :]
    visible = (lower[None] & (documents[:, :, None] == documents[:, None, :])).astype(WIDETYPE)
    return (keeping, use_state, chosen, visible)


def pack(state, normaliser, LOWTYPE=LOWTYPE):
    groups = state.shape[0]
    rows = state.astype(LOWTYPE).reshape(groups, 2, H // 2 * HD, -1)
    tail = normaliser.astype(LOWTYPE).reshape(groups, 2, H // 2, -1)
    tail = jnp.pad(tail, ((0, 0), (0, 0), (0, 10), (0, 0)))
    return jnp.concatenate([rows, tail], axis=2)


def unpack(packed):
    groups = packed.shape[0]
    cut = H // 2 * HD
    state = packed[:, :, :cut].reshape(groups, H, HD, -1)
    normaliser = packed[:, :, cut : cut + H // 2].reshape(groups, H, -1)
    return (state, normaliser.astype(WIDETYPE))


def local_state(key_feat, values, chosen):
    picked = key_feat * chosen[:, :, None, None].astype(LOWTYPE)
    state = jnp.einsum("sthf,sthe->shef", picked, values, preferred_element_type=WIDETYPE)
    normaliser = jnp.sum(picked.astype(WIDETYPE), axis=1)
    return pack(state, normaliser, WIDETYPE)


def attend(query_feat, key_feat, values, state_in, norm_in, use_state, visible):
    scores = (
        jnp.einsum("sthf,suhf->shtu", query_feat, key_feat, preferred_element_type=WIDETYPE)
        * visible[:, None]
    )
    numerator = jnp.einsum(
        "shtu,suhe->sthe", scores.astype(LOWTYPE), values, preferred_element_type=WIDETYPE
    )
    denominator = jnp.transpose(jnp.sum(scores, axis=3), (0, 2, 1))
    query_wide = query_feat.astype(WIDETYPE)
    numerator = numerator + use_state[:, :, None, None] * jnp.einsum(
        "sthf,shef->sthe", query_wide, state_in, precision=HIGH
    )
    denominator = denominator + use_state[:, :, None] * jnp.sum(
        query_wide * norm_in[:, None], axis=3
    )
    return (numerator / denominator[:, :, :, None], denominator)


def forward_layer(net, residual, flat, gains, biases, tables, layout, last_doc):
    keeping, use_state, chosen, visible = layout
    sequences = keeping.shape[0]
    span = visible.shape[1]
    rows = residual.shape[0]
    qkv_weight, out_weight, up_weight, down_weight = split_flat(flat)
    hidden_one = layer_norm(residual, gains[0], biases[0]).astype(LOWTYPE)
    projected = lax.dot_general(
        hidden_one, qkv_weight, (((1,), (1,)), ((), ())), preferred_element_type=WIDETYPE
    ).astype(LOWTYPE)
    shaped = projected.reshape(sequences, span, 3, H, HD)
    queries = shaped[:, :, 0]
    keys = shaped[:, :, 1]
    values = shaped[:, :, 2]
    query_feat = feature_map(queries.astype(WIDETYPE), tables[0]).astype(LOWTYPE)
    key_feat = feature_map(keys.astype(WIDETYPE), tables[1]).astype(LOWTYPE)
    scanned = scan_states(net, local_state(key_feat, values, chosen), last_doc, False, WIDETYPE)
    state_in, norm_in = unpack(scanned)
    output, denominator = attend(
        query_feat, key_feat, values, state_in, norm_in, use_state, visible
    )
    attended = output.reshape(rows, D).astype(LOWTYPE)
    residual_mid = residual + jnp.dot(attended, out_weight, preferred_element_type=WIDETYPE)
    hidden_two = layer_norm(residual_mid, gains[1], biases[1]).astype(LOWTYPE)
    up_proj = lax.dot_general(
        hidden_two, up_weight, (((1,), (1,)), ((), ())), preferred_element_type=WIDETYPE
    )
    activated = gelu_tanh(up_proj).astype(LOWTYPE)
    result = residual_mid + jnp.dot(activated, down_weight, preferred_element_type=WIDETYPE)
    kept = (
        residual,
        residual_mid,
        hidden_one,
        queries,
        keys,
        values,
        query_feat,
        key_feat,
        state_in,
        norm_in,
        output,
        denominator,
        attended,
        hidden_two,
        up_proj,
        activated,
    )
    return (result, kept)


def backward_layer(net, upstream, flat, gains, biases, tables, layout, last_doc, kept):
    keeping, use_state, chosen, visible = layout
    (
        residual,
        residual_mid,
        hidden_one,
        queries,
        keys,
        values,
        query_feat,
        key_feat,
        state_in,
        norm_in,
        output,
        denominator,
        attended,
        hidden_two,
        up_proj,
        activated,
    ) = kept
    qkv_weight, out_weight, up_weight, down_weight = split_flat(flat)
    sequences = keeping.shape[0]
    span = visible.shape[1]
    rows = upstream.shape[0]
    branch_low = upstream.astype(LOWTYPE)
    grad_act = lax.dot_general(
        branch_low, down_weight, (((1,), (1,)), ((), ())), preferred_element_type=WIDETYPE
    )
    grad_up = jax.vjp(gelu_tanh, up_proj)[1](grad_act)[0].astype(LOWTYPE)
    grad_hidden = jnp.dot(grad_up, up_weight, preferred_element_type=WIDETYPE)
    norm_back = jax.vjp(layer_norm, residual_mid, gains[1], biases[1])[1](grad_hidden)
    grad_mid = upstream + norm_back[0]
    mid_low = grad_mid.astype(LOWTYPE)
    grad_att = lax.dot_general(
        mid_low, out_weight, (((1,), (1,)), ((), ())), preferred_element_type=WIDETYPE
    )
    grad_output = grad_att.astype(LOWTYPE).astype(WIDETYPE).reshape(sequences, span, H, HD)
    grad_numer = grad_output / denominator[:, :, :, None]
    grad_numer = grad_numer.astype(LOWTYPE).astype(WIDETYPE)
    grad_denom = -jnp.sum(grad_numer * output, axis=3)
    gated_numer = grad_numer * use_state[:, :, None, None]
    gated_denom = grad_denom * use_state[:, :, None]
    query_wide = query_feat.astype(WIDETYPE)
    numer_low = grad_numer.astype(LOWTYPE)
    gated_low = gated_numer.astype(LOWTYPE)
    local_grad = jnp.einsum(
        "sthf,sthe->shef", query_feat, gated_low, preferred_element_type=WIDETYPE
    )
    local_norm = jnp.sum(query_wide * gated_denom[:, :, :, None], axis=1)
    backward_sums = scan_states(net, pack(local_grad, local_norm, WIDETYPE), last_doc, True, WIDETYPE)
    state_grad, norm_grad = unpack(backward_sums)
    scores = (
        jnp.einsum("sthf,suhf->shtu", query_feat, key_feat, preferred_element_type=WIDETYPE)
        * visible[:, None]
    )
    grad_scores = (
        jnp.einsum("sthe,suhe->shtu", numer_low, values, preferred_element_type=WIDETYPE)
        + jnp.transpose(grad_denom, (0, 2, 1))[:, :, :, None]
    )
    grad_scores = grad_scores.astype(LOWTYPE) * visible[:, None].astype(LOWTYPE)
    grad_query = jnp.einsum(
        "shtu,suhf->sthf", grad_scores, key_feat, preferred_element_type=WIDETYPE
    )
    grad_query = (
        grad_query
        + jnp.einsum("sthe,shef->sthf", gated_low.astype(WIDETYPE), state_in, precision=HIGH)
        + gated_denom[:, :, :, None] * norm_in[:, None]
    )
    grad_key = jnp.einsum(
        "shtu,sthf->suhf", grad_scores, query_feat, preferred_element_type=WIDETYPE
    )
    grad_key = grad_key + chosen[:, :, None, None] * (
        jnp.einsum("shef,sthe->sthf", state_grad, values.astype(WIDETYPE), precision=HIGH) + norm_grad[:, None]
    )
    grad_value = jnp.einsum(
        "shtu,sthe->suhe", scores.astype(LOWTYPE), numer_low, preferred_element_type=WIDETYPE
    )
    grad_value = grad_value + chosen[:, :, None, None] * jnp.einsum(
        "shef,sthf->sthe", state_grad, key_feat.astype(WIDETYPE), precision=HIGH
    )
    query_back = jax.vjp(feature_map, queries.astype(WIDETYPE), tables[0])[1](grad_query)
    key_back = jax.vjp(feature_map, keys.astype(WIDETYPE), tables[1])[1](grad_key)
    grad_proj = (
        jnp.stack([query_back[0], key_back[0], grad_value], axis=2)
        .reshape(rows, 3 * D)
        .astype(LOWTYPE)
    )
    grad_hidden_one = jnp.dot(grad_proj, qkv_weight, preferred_element_type=WIDETYPE)
    first_back = jax.vjp(layer_norm, residual, gains[0], biases[0])[1](grad_hidden_one)
    grad_input = grad_mid + first_back[0]
    operands = (
        grad_proj,
        hidden_one,
        attended,
        mid_low,
        grad_up,
        hidden_two,
        activated,
        branch_low,
    )
    gain_grad = jnp.stack([first_back[1], norm_back[1]])
    bias_grad = jnp.stack([first_back[2], norm_back[2]])
    table_grad = jnp.stack([query_back[1], key_back[1]])
    return (grad_input, operands, gain_grad, bias_grad, table_grad)


def outer_rows(left, right):
    return lax.dot_general(left, right, (((0,), (0,)), ((), ())), preferred_element_type=WIDETYPE)


def scatter_layer(net, operands):
    grad_proj, hidden_one, attended, mid_low, grad_up, hidden_two, activated, branch_low = operands
    cut = net.nz * 3 * D // (4 * D + 2 * FF)
    rest = jnp.concatenate(
        [
            outer_rows(attended, mid_low).astype(LOWTYPE),
            outer_rows(grad_up, hidden_two).astype(LOWTYPE),
            outer_rows(activated, branch_low).astype(LOWTYPE),
        ],
        axis=0,
    )
    rest = scatter_planes(net, rest, cut, net.nz)
    head = scatter_planes(net, outer_rows(grad_proj, hidden_one).astype(LOWTYPE), 0, cut)
    return jnp.where(net.z < cut, head, rest)


def body(tokens, doc_lengths, weights, norm_gain, norm_bias, fmap, cotangent):
    net = Net()
    sequences, span = tokens.shape[:2]
    start = lax.axis_index("seq") * span
    gathered = [lax.all_gather(weights[layer], AXES, axis=0, tiled=True) for layer in range(LAYERS)]
    rows = sequences * span
    layout = doc_layout(doc_lengths, start, span)
    last_doc = last_docs(doc_lengths, span)
    residual = tokens.reshape(rows, D).astype(WIDETYPE)
    saved = []
    for layer in range(LAYERS):
        residual, kept = forward_layer(
            net, residual, gathered[layer], norm_gain[layer], norm_bias[layer], fmap[layer], layout, last_doc
        )
        saved.append(kept)
    result = residual.astype(LOWTYPE).reshape(tokens.shape)
    upstream = cotangent.reshape(rows, D).astype(WIDETYPE)
    shards = [None] * LAYERS
    small = [None] * LAYERS
    for layer in range(LAYERS - 1, -1, -1):
        upstream, operands, gain_grad, bias_grad, table_grad = backward_layer(
            net,
            upstream,
            gathered[layer],
            norm_gain[layer],
            norm_bias[layer],
            fmap[layer],
            layout,
            last_doc,
            saved[layer],
        )
        shards[layer] = scatter_layer(net, operands)
        packed = jnp.concatenate([table_grad.reshape(2 * HD, D), gain_grad, bias_grad], axis=0)
        small[layer] = sum_everywhere(net, packed)
    small = jnp.stack(small)
    cut = 2 * HD
    return (
        result,
        upstream.reshape(tokens.shape),
        jnp.stack(shards),
        small[:, cut : cut + 2],
        small[:, cut + 2 :],
        small[:, :cut].reshape(fmap.shape),
    )


def solution(mesh):
    in_specs = (
        P("batch", "seq", None),
        P("batch", None),
        P(None, ("seq", "batch"), None),
        P(),
        P(),
        P(),
        P("batch", "seq", None),
    )
    out_specs = (
        P("batch", "seq", None),
        P("batch", "seq", None),
        P(None, ("seq", "batch"), None),
        P(),
        P(),
        P(),
    )
    return jax.shard_map(body, mesh=mesh, in_specs=in_specs, out_specs=out_specs, check_vma=False)
```

```python
import jax
import jax.numpy as jnp
from jax import lax
from jax.experimental import pallas as pl
from jax.experimental.pallas import tpu as pltpu
from jax.sharding import PartitionSpec as P

D = 768
H = 12
HD = 64
FF = 3072
LAYERS = 2
DOCS = 4
EPSILON = 1e-05
F32 = jnp.float32
BF = jnp.bfloat16
PAIRS = H // 2
WIDE_LIMIT = 40 * 1024 * 1024


AXES = ("seq", "batch")


class Net:
    def __init__(self):
        self.nz = lax.axis_size("seq") // 4
        self.nb = lax.axis_size("batch")
        place = lax.axis_index("seq")
        self.z = place // 4
        self.y = (place // 2) % 2
        self.c = place % 2
        self.b = lax.axis_index("batch")

    def move(self, array, target):
        pairs = []
        for index in range(self.nz * 4 * self.nb):
            place = index // self.nb
            goal = target(place // 4, (place // 2) % 2, place % 2, index % self.nb)
            if goal is not None:
                z, y, c, b = goal
                pairs.append((index, ((z * 2 + y) * 2 + c) * self.nb + b))
        return lax.ppermute(array, AXES, pairs)

    def core(self, array):
        return self.move(array, lambda z, y, c, b: (z, y, 1 - c, b))

    def flip_y(self, array):
        return self.move(array, lambda z, y, c, b: (z, 1 - y, c, b))

    def turn_b(self, array, step):
        return self.move(array, lambda z, y, c, b: (z, y, c, (b + step) % self.nb))

    def shift_z(self, array, step):
        def target(z, y, c, b):
            return (z + step, y, c, b) if 0 <= z + step < self.nz else None

        return self.move(array, target)


def pick(array, index, axis=0):
    return lax.dynamic_index_in_dim(array, index, axis, False)


def last_docs(doc_lengths, span):
    ends = jnp.cumsum(doc_lengths, axis=1)

    def last_doc(block):
        found = jnp.sum(((block + 1) * span - 1 >= ends).astype(jnp.int32), axis=1)
        return jnp.where(block < 0, -1, found)

    return last_doc


def scan_states(net, packed, last_doc, reverse):
    wide = F32
    low = F32
    base = 4 * net.z
    first = base + 2 * net.y

    def gate(a, b):
        same = (last_doc(a) == last_doc(b)).astype(wide)
        return pick(same, net.c)

    mine = pick(packed, net.c)
    theirs = net.core(pick(packed, 1 - net.c))
    zero = jnp.equal(net.c, 0)
    part0 = jnp.where(zero, mine, theirs).astype(wide)
    part1 = jnp.where(zero, theirs, mine).astype(wide)
    if reverse:
        chip = part0 + gate(first, first - 1) * part1
    else:
        chip = gate(first, first + 1) * part0 + part1
    chip = chip.astype(low)
    own = pick(chip, net.y)
    other = net.flip_y(pick(chip, 1 - net.y))
    down = jnp.equal(net.y, 0)
    row0 = jnp.where(down, own, other).astype(wide)
    row1 = jnp.where(down, other, own).astype(wide)
    if reverse:
        plane = row0 + gate(base + 1, base - 1) * row1
    else:
        plane = gate(base + 1, base + 3) * row0 + row1
    plane = plane.astype(low)
    entering = jnp.zeros(plane.shape, wide)
    for step in range(1, net.nz):
        if reverse:
            entering = entering + gate(4 * (net.z + step) - 1, base + 3) * net.shift_z(plane, -step)
        else:
            entering = entering + gate(4 * (net.z - step) + 3, base - 1) * net.shift_z(plane, step)
    if reverse:
        row1_in = entering
        row0_in = gate(base + 3, base + 1) * entering + row1
    else:
        row0_in = entering
        row1_in = gate(base - 1, base + 1) * entering + row0
    own_in = jnp.where(down, row0_in, row1_in)
    other_in = net.flip_y(jnp.where(down, row1_in, row0_in).astype(low)).astype(wide)
    chip_in = jnp.where(down, jnp.stack([own_in, other_in]), jnp.stack([other_in, own_in]))
    if reverse:
        core1_in = chip_in
        core0_in = gate(first + 1, first) * chip_in + part1
    else:
        core0_in = chip_in
        core1_in = gate(first - 1, first) * chip_in + part0
    core0_in = core0_in.astype(low)
    core1_in = core1_in.astype(low)
    kept = jnp.where(zero, core0_in, core1_in)
    sent = net.core(jnp.where(zero, core1_in, core0_in))
    return jnp.where(zero, jnp.stack([kept, sent]), jnp.stack([sent, kept]))


def scatter_planes(net, grads, first, last):
    planes = last - first
    wide = F32
    low = BF
    grads = grads.reshape(planes, 2, 2, net.nb, -1, D)
    kept = pick(grads, net.c, 2).astype(wide)
    summed = (kept + net.core(pick(grads, 1 - net.c, 2)).astype(wide)).astype(low)
    half = summed.shape[3] // 2

    def over_b(value, axis):
        total = pick(value, net.b, axis).astype(wide)
        for step in range(1, net.nb):
            total = total + net.turn_b(pick(value, (net.b + step) % net.nb, axis), step).astype(wide)
        return total.astype(low)

    def over_y(value):
        got = net.flip_y(pick(value, 1 - net.y, 1))
        return (pick(value, net.y, 1).astype(wide) + got.astype(wide)).astype(low)

    left = over_y(over_b(summed[:, :, :, :half], 2))
    right = over_b(over_y(summed[:, :, :, half:]), 1)
    rows = jnp.concatenate([left, right], axis=1)
    total = pick(rows, jnp.clip(net.z - first, 0, planes - 1)).astype(wide)
    for step in range(1, net.nz):
        goal = (net.z + step) % net.nz
        value = pick(rows, jnp.clip(goal - first, 0, planes - 1))

        def target(z, y, c, b, step=step):
            to = (z + step) % net.nz
            return (to, y, c, b) if first <= to < last else None

        total = total + net.move(value, target).astype(wide)
    return total


def sum_everywhere(net, array):
    wide = F32

    def exchange(value, target):
        value = value.astype(BF)
        return value.astype(wide) + net.move(value, target).astype(wide)

    array = exchange(array, lambda z, y, c, b: (z, y, 1 - c, b))
    array = exchange(array, lambda z, y, c, b: (z, 1 - y, c, b))
    step = 1
    while step < net.nb:
        array = exchange(array, lambda z, y, c, b, step=step: (z, y, c, b ^ step))
        step *= 2
    step = 1
    while step < net.nz:
        array = exchange(array, lambda z, y, c, b, step=step: (z ^ step, y, c, b))
        step *= 2
    return array


def nn(a, b):
    return lax.dot_general(a, b, (((1,), (0,)), ((), ())), preferred_element_type=F32)


def nt(a, b):
    return lax.dot_general(a, b, (((1,), (1,)), ((), ())), preferred_element_type=F32)


def tn(a, b):
    return lax.dot_general(a, b, (((0,), (0,)), ((), ())), preferred_element_type=F32)


def two(a):
    high = a.astype(BF)
    return high, (a - high.astype(F32)).astype(BF)


def left_half(shape):
    return lax.broadcasted_iota(jnp.int32, shape, 1) < 64


def normed(values, gain, bias):
    mean = jnp.mean(values, axis=1, keepdims=True)
    centred = values - mean
    variance = jnp.mean(centred * centred, axis=1, keepdims=True)
    return centred * lax.rsqrt(variance + EPSILON) * gain + bias


def normed_back(values, gain, upstream):
    mean = jnp.mean(values, axis=1, keepdims=True)
    centred = values - mean
    variance = jnp.mean(centred * centred, axis=1, keepdims=True)
    scale = lax.rsqrt(variance + EPSILON)
    unit = centred * scale
    inner = upstream * gain
    grad = scale * (
        inner
        - jnp.mean(inner, axis=1, keepdims=True)
        - unit * jnp.mean(inner * unit, axis=1, keepdims=True)
    )
    return grad, jnp.sum(upstream * unit, axis=0, keepdims=True), jnp.sum(upstream, axis=0, keepdims=True)


def softmax_halves(values):
    left = left_half(values.shape)
    low = jnp.float32(-jnp.inf)
    top0 = jnp.max(jnp.where(left, values, low), axis=1, keepdims=True)
    top1 = jnp.max(jnp.where(left, low, values), axis=1, keepdims=True)
    raised = jnp.exp(values - jnp.where(left, top0, top1))
    sum0 = jnp.sum(jnp.where(left, raised, 0.0), axis=1, keepdims=True)
    sum1 = jnp.sum(jnp.where(left, 0.0, raised), axis=1, keepdims=True)
    return raised / jnp.where(left, sum0, sum1)


def softmax_halves_back(weights, upstream):
    left = left_half(weights.shape)
    product = weights * upstream
    sum0 = jnp.sum(jnp.where(left, product, 0.0), axis=1, keepdims=True)
    sum1 = jnp.sum(jnp.where(left, 0.0, product), axis=1, keepdims=True)
    return product - weights * jnp.where(left, sum0, sum1)


def lanes(ref, head):
    return ref[:, head * 128 : (head + 1) * 128]


def state_at(ref, seq, pair):
    start = pair % 3 * 128
    return ref[seq, pair // 3, start : start + 128, :]


def normaliser_at(ref, head):
    row = H // 2 * HD + head % 6
    parts = [ref[seq, head // 6, row : row + 1, :] for seq in range(2)]
    return jnp.concatenate([jnp.broadcast_to(part, (64, 128)) for part in parts], axis=0)


def store_state(ref, seq, pair, block, row):
    half = pair // 3
    start = pair % 3 * 128
    ref[seq, half, start : start + 64, :] = block[:64, :128]
    ref[seq, half, start + 64 : start + 128, :] = block[64:, 128:]
    tail = H // 2 * HD + pair % 3 * 2
    ref[seq, half, tail : tail + 1, :] = row[:, :128]
    ref[seq, half, tail + 1 : tail + 2, :] = row[:, 128:]


def clear_tail(ref):
    for seq in range(2):
        for half in range(2):
            ref[seq, half, 390:400, :] = jnp.zeros((10, 128), F32)


def head_kernel(x_ref, norm_ref, w_ref, map_ref, cols_ref, h_ref, proj_ref, fq_ref, fk_ref, state_ref):
    step = pl.program_id(0)

    @pl.when(step == 0)
    def _():
        h_ref[...] = normed(x_ref[...], norm_ref[0:1, :], norm_ref[1:2, :]).astype(BF)

    proj_ref[...] = nt(h_ref[...], w_ref[...]).astype(BF)

    def features(out_ref):
        for pair in range(PAIRS):
            part = lanes(proj_ref, pair)
            before = nn(jnp.concatenate([part, part], axis=1), map_ref[0, pair])
            for side in range(2):
                head = pair * 2 + side
                out_ref[:, head * 128 : (head + 1) * 128] = softmax_halves(
                    before[:, side * 128 : (side + 1) * 128]
                )

    @pl.when(step == 0)
    def _():
        features(fq_ref)

    @pl.when(step == 1)
    def _():
        features(fk_ref)

    @pl.when(step == 2)
    def _():
        clear_tail(state_ref)
        for seq in range(2):
            rows = slice(seq * 64, seq * 64 + 64)
            last = cols_ref[rows, 1:2]
            for pair in range(PAIRS):
                feats = fk_ref[rows, pair * 256 : (pair + 1) * 256].astype(BF).astype(F32) * last
                block = tn(proj_ref[rows, pair * 128 : (pair + 1) * 128], feats.astype(BF))
                store_state(state_ref, seq, pair, block, jnp.sum(feats, axis=0, keepdims=True))


def tail_kernel(
    x_ref, v_ref, fq_ref, fk_ref, state_ref, cols_ref, vis_ref, norm_ref, wo_ref, wu_ref, wd_ref,
    o_ref, rden_ref, att_ref, x1_ref, h2_ref, u_ref, g_ref, out_ref,
):
    @pl.when(pl.program_id(0) == 0)
    def _():
        visible = vis_ref[...]
        mark = cols_ref[:, 0:1]
        left = left_half((128, 128))
        for pair in range(PAIRS):
            value = lanes(v_ref, pair)
            nothing = jnp.zeros_like(value)
            state = [jnp.concatenate(two(state_at(state_ref, seq, pair)), axis=1) for seq in range(2)]
            weights = []
            totals = []
            carried = []
            for side in range(2):
                head = pair * 2 + side
                query = lanes(fq_ref, head).astype(BF)
                score = nt(query, lanes(fk_ref, head).astype(BF)) * visible
                weights.append(score.astype(BF))
                wide = query.astype(F32) * normaliser_at(state_ref, head) * mark
                totals.append(jnp.sum(score + wide, axis=1, keepdims=True))
                twice = jnp.concatenate([query, query], axis=1)
                carried.append(
                    jnp.concatenate([nt(twice[:64], state[0]), nt(twice[64:], state[1])], axis=0)
                )
            number = nn(
                jnp.concatenate(weights, axis=1),
                jnp.concatenate([jnp.where(left, value, nothing), jnp.where(left, nothing, value)], axis=0),
            )
            number = number + mark * jnp.where(left, carried[0], carried[1])
            inverse = 1.0 / jnp.where(left, totals[0], totals[1])
            output = number * inverse
            cut = slice(pair * 128, (pair + 1) * 128)
            o_ref[:, cut] = output
            rden_ref[:, cut] = inverse
            att_ref[:, cut] = output.astype(BF)
        x1 = x_ref[...] + nn(att_ref[...], wo_ref[...])
        x1_ref[...] = x1
        h2_ref[...] = normed(x1, norm_ref[0:1, :], norm_ref[1:2, :]).astype(BF)
        out_ref[...] = x1

    u = nt(h2_ref[...], wu_ref[...])
    u_ref[...] = u
    inner = jnp.tanh(0.7978845608028654 * (u + 0.044715 * (u * u * u)))
    g = (0.5 * u * (1.0 + inner)).astype(BF)
    g_ref[...] = g
    out_ref[...] += nn(g, wd_ref[...])


def back_kernel(
    e_ref, u_ref, x1_ref, norm_ref, wd_ref, wu_ref, wo_ref, o_ref, rden_ref, fq_ref, cols_ref,
    du_ref, dx1_ref, ebx_ref, dn_ref, dd_ref, state_ref, gn_ref, total,
):
    step = pl.program_id(0)
    dg = nt(e_ref[...].astype(BF), wd_ref[...])
    u = u_ref[...]
    inner = jnp.tanh(0.7978845608028654 * (u + 0.044715 * (u * u * u)))
    slope = 0.5 * (1.0 + inner) + (0.5 * u) * (1.0 - inner * inner) * (
        0.7978845608028654 * (1.0 + 0.134145 * (u * u))
    )
    du = (dg * slope).astype(BF)
    du_ref[...] = du
    part = nn(du, wu_ref[...])

    @pl.when(step == 0)
    def _():
        total[...] = part

    @pl.when(step > 0)
    def _():
        total[...] += part

    @pl.when(step == pl.num_programs(0) - 1)
    def _():
        grad, gain, bias = normed_back(x1_ref[...], norm_ref[0:1, :], total[...])
        gn_ref[0:1, :] = gain
        gn_ref[1:2, :] = bias
        dx1 = e_ref[...] + grad
        dx1_ref[...] = dx1
        low = dx1.astype(BF)
        ebx_ref[...] = low
        dn_ref[...] = nt(low, wo_ref[...]).astype(BF).astype(F32) * rden_ref[...]
        left = left_half((128, 128))
        lane = lax.broadcasted_iota(jnp.int32, (128, 128), 1)
        clear_tail(state_ref)
        columns = jnp.zeros((128, 128), F32)
        for pair in range(PAIRS):
            dn = lanes(dn_ref, pair)
            product = dn * lanes(o_ref, pair)
            d0 = -jnp.sum(jnp.where(left, product, 0.0), axis=1, keepdims=True)
            d1 = -jnp.sum(jnp.where(left, 0.0, product), axis=1, keepdims=True)
            columns = jnp.where(lane == pair * 2, d0, jnp.where(lane == pair * 2 + 1, d1, columns))
            for seq in range(2):
                rows = slice(seq * 64, seq * 64 + 64)
                mark = cols_ref[rows, 0:1]
                high, rest = two(dn[rows] * mark)
                feats = fq_ref[rows, pair * 256 : (pair + 1) * 256].astype(BF)
                block = tn(jnp.concatenate([high, rest], axis=0), jnp.concatenate([feats, feats], axis=0))
                wide = feats.astype(F32)
                row = jnp.concatenate(
                    [
                        jnp.sum(wide[:, :128] * (d0[rows] * mark), axis=0, keepdims=True),
                        jnp.sum(wide[:, 128:] * (d1[rows] * mark), axis=0, keepdims=True),
                    ],
                    axis=1,
                )
                store_state(state_ref, seq, pair, block, row)
        dd_ref[...] = columns


def fold_map(pair_weights, low_q):
    left = left_half((128, 128))
    folded = [weight - pltpu.roll(weight, 64, 1) for weight in pair_weights]
    grad = jnp.where(left, folded[0], pltpu.roll(folded[1], 64, 1))
    high, rest = two(grad)
    twice = jnp.concatenate([low_q, low_q], axis=0)
    table = tn(twice, jnp.concatenate([high, rest], axis=0))
    return jnp.where(left[:64], table[:64], table[64:])


def query_kernel(
    q_ref, v_ref, fq_ref, fk_ref, state_ref, dn_ref, dd_ref, cols_ref, vis_ref, map_ref,
    dq_ref, dmap_ref, dfk_ref, dv_ref,
):
    visible = vis_ref[...]
    low_visible = visible.astype(BF)
    mark = cols_ref[:, 0:1]
    left = left_half((128, 128))
    for pair in range(PAIRS):
        value = lanes(v_ref, pair)
        dn = lanes(dn_ref, pair)
        twice = jnp.concatenate([value, value], axis=1)
        state = [two(state_at(state_ref, seq, pair)) for seq in range(2)]
        weights = []
        shifts = []
        turned = []
        for side in range(2):
            head = pair * 2 + side
            wide = lanes(fq_ref, head)
            query = wide.astype(BF)
            key = lanes(fk_ref, head).astype(BF)
            score = (nt(query, key) * visible).astype(BF)
            mine = jnp.where(left, dn, 0.0) if side == 0 else jnp.where(left, 0.0, dn)
            high, rest = two(mine)
            dd = dd_ref[:, head : head + 1]
            shift = (nt(jnp.concatenate([high, rest], axis=1), twice) + dd).astype(BF) * low_visible
            carried = jnp.concatenate(
                [
                    nn(
                        jnp.concatenate([high[rows], high[rows], rest[rows]], axis=1),
                        jnp.concatenate([state[seq][0], state[seq][1], state[seq][0]], axis=0),
                    )
                    for seq, rows in ((0, slice(0, 64)), (1, slice(64, 128)))
                ],
                axis=0,
            )
            dfq = nn(shift, key) + mark * (carried + dd * normaliser_at(state_ref, head))
            dfk_ref[:, head * 128 : (head + 1) * 128] = tn(shift, query)
            weights.append(softmax_halves_back(wide, dfq))
            shifts.append(score)
            turned.append(high)
        cut = slice(pair * 128, (pair + 1) * 128)
        dv_ref[:, cut] = tn(jnp.concatenate(shifts, axis=0), jnp.concatenate(turned, axis=0))
        low = jnp.concatenate(weights, axis=1).astype(BF)
        dq_ref[:, cut] = nt(low, map_ref[0, pair, :128, :]).astype(BF)
        dmap_ref[:, cut] = fold_map(weights, lanes(q_ref, pair))


def key_kernel(
    k_ref, v_ref, fk_ref, state_ref, dfk_ref, dv_ref, dq_ref, cols_ref, map_ref, w_ref, x_ref, norm_ref, dx1_ref,
    dqkv_ref, dmap_ref, e_ref, gn_ref,
):
    last = cols_ref[:, 1:2]
    left = left_half((128, 128))
    dqkv_ref[:, :D] = dq_ref[...]
    for pair in range(PAIRS):
        value = lanes(v_ref, pair)
        nothing = jnp.zeros_like(value)
        state = [two(state_at(state_ref, seq, pair)) for seq in range(2)]
        weights = []
        grads = []
        for side in range(2):
            head = pair * 2 + side
            wide = lanes(fk_ref, head)
            key = wide.astype(BF)
            mine = jnp.where(left, value, nothing) if side == 0 else jnp.where(left, nothing, value)
            carried = []
            turned = []
            for seq, rows in ((0, slice(0, 64)), (1, slice(64, 128))):
                high, rest = state[seq]
                carried.append(
                    nn(
                        jnp.concatenate([mine[rows], mine[rows]], axis=1),
                        jnp.concatenate([high, rest], axis=0),
                    )
                )
                turned.append(nt(key[rows], high))
            carried = jnp.concatenate(carried, axis=0)
            dfk = lanes(dfk_ref, head) + last * (carried + normaliser_at(state_ref, head))
            weights.append(softmax_halves_back(wide, dfk))
            grads.append(jnp.concatenate(turned, axis=0))
        cut = slice(pair * 128, (pair + 1) * 128)
        dv = lanes(dv_ref, pair) + last * jnp.where(left, grads[0], grads[1])
        dqkv_ref[:, 2 * D + pair * 128 : 2 * D + (pair + 1) * 128] = dv.astype(BF)
        low = jnp.concatenate(weights, axis=1).astype(BF)
        dqkv_ref[:, D + pair * 128 : D + (pair + 1) * 128] = nt(low, map_ref[0, pair, :128, :]).astype(BF)
        dmap_ref[:, cut] = fold_map(weights, lanes(k_ref, pair))
    upstream = nn(dqkv_ref[...], w_ref[...])
    grad, gain, bias = normed_back(x_ref[...], norm_ref[0:1, :], upstream)
    gn_ref[0:1, :] = gain
    gn_ref[1:2, :] = bias
    e_ref[...] = dx1_ref[...] + grad


def rows_kernel(att_ref, ebx_ref, du_ref, h2_ref, g_ref, e_ref, out_ref):
    step = pl.program_id(0)

    @pl.when(step == 0)
    def _():
        out_ref[...] = tn(att_ref[...], ebx_ref[...]).astype(BF)

    @pl.when((step > 0) & (step < 5))
    def _():
        out_ref[...] = tn(du_ref[...], h2_ref[...]).astype(BF)

    @pl.when(step >= 5)
    def _():
        out_ref[...] = tn(g_ref[...], e_ref[...].astype(BF)).astype(BF)


def proj_rows_kernel(dqkv_ref, h_ref, out_ref):
    out_ref[...] = tn(dqkv_ref[...], h_ref[...]).astype(BF)


def whole(array):
    rank = array.ndim
    return pl.BlockSpec(array.shape, lambda *_: (0,) * rank)


def call(kernel, grid, operands, outputs, flops, scratch=()):
    arrays = []
    in_specs = []
    for operand in operands:
        if isinstance(operand, tuple):
            arrays.append(operand[0])
            in_specs.append(pl.BlockSpec(operand[1], operand[2]))
        else:
            arrays.append(operand)
            in_specs.append(whole(operand))
    shapes = [jax.ShapeDtypeStruct(out[0], out[1]) for out in outputs]
    out_specs = []
    for out, shape in zip(outputs, shapes):
        out_specs.append(pl.BlockSpec(out[2], out[3]) if len(out) > 2 else whole(shape))
    moved = sum(a.size * a.dtype.itemsize for a in shapes)
    for spec, a in zip(in_specs, arrays):
        moved += a.size * a.dtype.itemsize if a.shape[0] < 9000 else 4 * D * D
    return pl.pallas_call(
        kernel,
        grid=grid,
        in_specs=in_specs,
        out_specs=out_specs,
        out_shape=shapes,
        scratch_shapes=list(scratch),
        compiler_params=pltpu.CompilerParams(vmem_limit_bytes=WIDE_LIMIT),
        cost_estimate=pl.CostEstimate(flops=flops, bytes_accessed=moved, transcendentals=0),
    )(*arrays)


STATE = (2, 2, H // 2 * HD + 16, 128)
ROWS = 128
CHUNK = 512
CHUNKS = FF // CHUNK


def still(*index):
    return lambda i: index


def forward_layer(net, x, flat, norms, maps, cols, visible, last_doc):
    h1, proj, fq, fk, local = call(
        head_kernel,
        (3,),
        [
            x,
            norms[0],
            (flat, (D, D), lambda i: (i, 0)),
            (maps, (1, PAIRS, 256, 256), lambda i: (jnp.minimum(i, 1), 0, 0, 0)),
            cols,
        ],
        [
            ((ROWS, D), BF),
            ((ROWS, 3 * D), BF, (ROWS, D), lambda i: (0, i)),
            ((ROWS, H * 128), F32),
            ((ROWS, H * 128), F32),
            (STATE, F32),
        ],
        2 * ROWS * 3 * D * D,
    )
    state = scan_states(net, local, last_doc, False)
    o, rden, att, x1, h2, u, g, result = call(
        tail_kernel,
        (CHUNKS,),
        [
            x,
            (proj, (ROWS, D), still(0, 2)),
            fq,
            fk,
            state,
            cols,
            visible,
            norms[1],
            (flat, (D, D), still(3, 0)),
            (flat, (CHUNK, D), lambda i: (CHUNKS + i, 0)),
            (flat, (CHUNK, D), lambda i: (2 * CHUNKS + i, 0)),
        ],
        [
            ((ROWS, D), F32),
            ((ROWS, D), F32),
            ((ROWS, D), BF),
            ((ROWS, D), F32),
            ((ROWS, D), BF),
            ((ROWS, FF), F32, (ROWS, CHUNK), lambda i: (0, i)),
            ((ROWS, FF), BF, (ROWS, CHUNK), lambda i: (0, i)),
            ((ROWS, D), F32),
        ],
        2 * ROWS * 9 * D * D,
    )
    return result, (x, h1, proj, fq, fk, state, o, rden, att, x1, h2, u, g)


def backward_layer(net, e, flat, norms, maps, cols, visible, last_doc, kept):
    x, h1, proj, fq, fk, state, o, rden, att, x1, h2, u, g = kept
    du, dx1, ebx, dn, dd, local, norm_two = call(
        back_kernel,
        (CHUNKS,),
        [
            e,
            (u, (ROWS, CHUNK), lambda i: (0, i)),
            x1,
            norms[1],
            (flat, (CHUNK, D), lambda i: (2 * CHUNKS + i, 0)),
            (flat, (CHUNK, D), lambda i: (CHUNKS + i, 0)),
            (flat, (D, D), still(3, 0)),
            o,
            rden,
            fq,
            cols,
        ],
        [
            ((ROWS, FF), BF, (ROWS, CHUNK), lambda i: (0, i)),
            ((ROWS, D), F32),
            ((ROWS, D), BF),
            ((ROWS, D), F32),
            ((ROWS, 128), F32),
            (STATE, F32),
            ((2, D), F32),
        ],
        2 * ROWS * 9 * D * D,
        [pltpu.VMEM((ROWS, D), F32)],
    )
    state_grad = scan_states(net, local, last_doc, True)
    dq, query_map, dfk, dv = call(
        query_kernel,
        (1,),
        [
            (proj, (ROWS, D), still(0, 0)),
            (proj, (ROWS, D), still(0, 2)),
            fq,
            fk,
            state,
            dn,
            dd,
            cols,
            visible,
            (maps, (1, PAIRS, 256, 256), still(0, 0, 0, 0)),
        ],
        [((ROWS, D), BF), ((HD, D), F32), ((ROWS, H * 128), F32), ((ROWS, D), F32)],
        2 * ROWS * 4 * D * D,
    )
    (rest,) = call(
        rows_kernel,
        (9,),
        [
            att,
            ebx,
            (du, (ROWS, D), lambda i: (0, jnp.clip(i - 1, 0, 3))),
            h2,
            (g, (ROWS, D), lambda i: (0, jnp.clip(i - 5, 0, 3))),
            e,
        ],
        [((9 * D, D), BF, (D, D), lambda i: (i, 0))],
        2 * ROWS * 9 * D * D,
    )
    dqkv, key_map, e_next, norm_one = call(
        key_kernel,
        (1,),
        [
            (proj, (ROWS, D), still(0, 1)),
            (proj, (ROWS, D), still(0, 2)),
            fk,
            state_grad,
            dfk,
            dv,
            dq,
            cols,
            (maps, (1, PAIRS, 256, 256), still(1, 0, 0, 0)),
            (flat, (3 * D, D), still(0, 0)),
            x,
            norms[0],
            dx1,
        ],
        [((ROWS, 3 * D), BF), ((HD, D), F32), ((ROWS, D), F32), ((2, D), F32)],
        2 * ROWS * 3 * D * D,
    )
    (head,) = call(
        proj_rows_kernel,
        (3,),
        [(dqkv, (ROWS, D), lambda i: (0, i)), h1],
        [((3 * D, D), BF, (D, D), lambda i: (i, 0))],
        2 * ROWS * 3 * D * D,
    )
    small = jnp.concatenate([query_map, key_map, norm_one, norm_two], axis=0)
    return e_next, rest, head, small


def pair_maps(fmap):
    grid = fmap.reshape(LAYERS, 2, HD, PAIRS, 2, HD).transpose(0, 1, 3, 4, 2, 5)
    both = jnp.concatenate([grid, -grid], axis=-1)
    empty = jnp.zeros_like(both[:, :, :, 0])
    top = jnp.concatenate([both[:, :, :, 0], empty], axis=-1)
    bottom = jnp.concatenate([empty, both[:, :, :, 1]], axis=-1)
    return jnp.concatenate(two(jnp.concatenate([top, bottom], axis=3)), axis=3)


def doc_layout(doc_lengths, start, span):
    ends = jnp.cumsum(doc_lengths, axis=1)
    places = start + jnp.arange(span, dtype=jnp.int32)
    documents = jnp.sum((places[None, :, None] >= ends[:, None, :]).astype(jnp.int32), axis=2)
    before = jnp.sum((start - 1 >= ends).astype(jnp.int32), axis=1)
    previous = jnp.where(start > 0, before, -1)
    mark = (documents == previous[:, None]).reshape(-1, 1)
    last = (documents == documents[:, span - 1 :]).reshape(-1, 1)
    lane = jnp.arange(128)[None, :]
    cols = jnp.where(lane == 0, mark, (lane == 1) & last).astype(F32)
    names = (documents + (DOCS + 1) * jnp.arange(documents.shape[0])[:, None]).reshape(-1)
    lower = jnp.arange(names.shape[0])[:, None] >= jnp.arange(names.shape[0])[None, :]
    visible = (lower & (names[:, None] == names[None, :])).astype(F32)
    return cols, visible


def body(tokens, doc_lengths, weights, norm_gain, norm_bias, fmap, cotangent):
    net = Net()
    sequences, span = tokens.shape[:2]
    start = lax.axis_index("seq") * span
    gathered = [lax.all_gather(weights[layer], AXES, axis=0, tiled=True) for layer in range(LAYERS)]
    rows = sequences * span
    cols, visible = doc_layout(doc_lengths, start, span)
    last_doc = last_docs(doc_lengths, span)
    maps = pair_maps(fmap)
    norms = jnp.stack([norm_gain, norm_bias], axis=2)
    x = tokens.reshape(rows, D).astype(F32)
    saved = []
    for layer in range(LAYERS):
        x, kept = forward_layer(net, x, gathered[layer], norms[layer], maps[layer], cols, visible, last_doc)
        saved.append(kept)
    result = x.astype(BF).reshape(tokens.shape)
    e = cotangent.reshape(rows, D).astype(F32)
    shards = [None] * LAYERS
    small = [None] * LAYERS
    cut = net.nz * 3 * D // (4 * D + 2 * FF)
    for layer in range(LAYERS - 1, -1, -1):
        e, rest, head, terms = backward_layer(
            net, e, gathered[layer], norms[layer], maps[layer], cols, visible, last_doc, saved[layer]
        )
        rest = scatter_planes(net, rest, cut, net.nz)
        head = scatter_planes(net, head, 0, cut)
        shards[layer] = jnp.where(net.z < cut, head, rest)
        small[layer] = sum_everywhere(net, terms)
    small = jnp.stack(small)
    cut = 2 * HD
    return (
        result,
        e.reshape(tokens.shape),
        jnp.stack(shards),
        small[:, cut::2],
        small[:, cut + 1 :: 2],
        small[:, :cut].reshape(fmap.shape),
    )


def solution(mesh):
    in_specs = (
        P("batch", "seq", None),
        P("batch", None),
        P(None, ("seq", "batch"), None),
        P(),
        P(),
        P(),
        P("batch", "seq", None),
    )
    out_specs = (
        P("batch", "seq", None),
        P("batch", "seq", None),
        P(None, ("seq", "batch"), None),
        P(),
        P(),
        P(),
    )
    return jax.shard_map(body, mesh=mesh, in_specs=in_specs, out_specs=out_specs, check_vma=False)
```

```python
import functools

import jax
import jax.numpy as jnp
from jax import lax
from jax.experimental import pallas as pl
from jax.experimental.pallas import tpu as pltpu
from jax.sharding import PartitionSpec as P

D = 768
H = 12
HD = 64
FF = 3072
LAYERS = 2
DOCS = 4
EPSILON = 1e-05
F32 = jnp.float32
BF = jnp.bfloat16
PAIRS = H // 2
WIDE_LIMIT = 40 * 1024 * 1024


AXES = ("seq", "batch")


class Net:
    def __init__(self):
        self.nz = lax.axis_size("seq") // 4
        self.nb = lax.axis_size("batch")
        place = lax.axis_index("seq")
        self.z = place // 4
        self.y = (place // 2) % 2
        self.c = place % 2
        self.b = lax.axis_index("batch")

    def move(self, array, target):
        pairs = []
        for index in range(self.nz * 4 * self.nb):
            place = index // self.nb
            goal = target(place // 4, (place // 2) % 2, place % 2, index % self.nb)
            if goal is not None:
                z, y, c, b = goal
                pairs.append((index, ((z * 2 + y) * 2 + c) * self.nb + b))
        return lax.ppermute(array, AXES, pairs)

    def core(self, array):
        return self.move(array, lambda z, y, c, b: (z, y, 1 - c, b))

    def flip_y(self, array):
        return self.move(array, lambda z, y, c, b: (z, 1 - y, c, b))

    def turn_b(self, array, step):
        return self.move(array, lambda z, y, c, b: (z, y, c, (b + step) % self.nb))

    def shift_z(self, array, step):
        def target(z, y, c, b):
            return (z + step, y, c, b) if 0 <= z + step < self.nz else None

        return self.move(array, target)


def pick(array, index, axis=0):
    return lax.dynamic_index_in_dim(array, index, axis, False)


def last_docs(doc_lengths, span):
    ends = jnp.cumsum(doc_lengths, axis=1)

    def last_doc(block):
        found = jnp.sum(((block + 1) * span - 1 >= ends).astype(jnp.int32), axis=1)
        return jnp.where(block < 0, -1, found)

    return last_doc


def doublings(count):
    step = 1
    while step < count:
        yield step
        step *= 2


def scan_gates(net, last_doc, reverse):
    base = 4 * net.z
    first = base + 2 * net.y
    if reverse:
        pairs = [(first, first - 1), (base + 1, base - 1), (base + 3, base + 1), (first + 1, first)]
        for step in doublings(net.nz):
            pairs += [(4 * (net.z + step) - 1, base + 3), (4 * (net.z + step) - 1, base - 1)]
    else:
        pairs = [(first, first + 1), (base + 1, base + 3), (base - 1, base + 1), (first - 1, first)]
        for step in doublings(net.nz):
            pairs += [(4 * (net.z - step) + 3, base - 1), (4 * (net.z - step) + 3, base + 3)]
    same = jnp.stack([last_doc(a) == last_doc(b) for a, b in pairs])
    return pick(same, net.c, 1).astype(F32)


def scan_steps(net, packed, gates, reverse):
    wide = F32
    low = F32
    mine = pick(packed, net.c)
    theirs = yield net.core(pick(packed, 1 - net.c))
    zero = jnp.equal(net.c, 0)
    part0 = jnp.where(zero, mine, theirs).astype(wide)
    part1 = jnp.where(zero, theirs, mine).astype(wide)
    if reverse:
        chip = part0 + gates[0] * part1
    else:
        chip = gates[0] * part0 + part1
    chip = chip.astype(low)
    own = pick(chip, net.y)
    other = yield net.flip_y(pick(chip, 1 - net.y))
    down = jnp.equal(net.y, 0)
    row0 = jnp.where(down, own, other).astype(wide)
    row1 = jnp.where(down, other, own).astype(wide)
    if reverse:
        plane = row0 + gates[1] * row1
    else:
        plane = gates[1] * row0 + row1
    entering = jnp.zeros(plane.shape, wide)
    for index, step in enumerate(doublings(net.nz)):
        part = yield net.shift_z(plane, -step if reverse else step)
        entering = entering + gates[4 + 2 * index] * part
        plane = plane + gates[5 + 2 * index] * part
    if reverse:
        row1_in = entering
        row0_in = gates[2] * entering + row1
    else:
        row0_in = entering
        row1_in = gates[2] * entering + row0
    own_in = jnp.where(down, row0_in, row1_in)
    other_in = yield net.flip_y(jnp.where(down, row1_in, row0_in).astype(low))
    other_in = other_in.astype(wide)
    chip_in = jnp.where(down, jnp.stack([own_in, other_in]), jnp.stack([other_in, own_in]))
    if reverse:
        core1_in = chip_in
        core0_in = gates[3] * chip_in + part1
    else:
        core0_in = chip_in
        core1_in = gates[3] * chip_in + part0
    core0_in = core0_in.astype(low)
    core1_in = core1_in.astype(low)
    kept = jnp.where(zero, core0_in, core1_in)
    sent = yield net.core(jnp.where(zero, core1_in, core0_in))
    return jnp.where(zero, jnp.stack([kept, sent]), jnp.stack([sent, kept]))


def finish(steps, value):
    while True:
        try:
            value = steps.send(value)
        except StopIteration as stop:
            return stop.value


def tie(*groups):
    return lax.optimization_barrier(groups)


class Scatter:
    def __init__(self, net, first, last):
        self.net = net
        self.first = first
        self.last = last

    def core(self, *pairs):
        net = self.net
        pairs = [(keep, net.core(send)) for keep, send in pairs]
        if (pairs[0][0].shape[1] // net.nb) % 32 == 0:
            return split_call(net, pairs)
        total = jnp.concatenate([(a.astype(F32) + b.astype(F32)).astype(BF) for a, b in pairs], axis=0)
        total = total.reshape(self.last - self.first, 2, net.nb, -1, D)
        half = total.shape[3] // 2
        top = total[:, :, :, :half]
        bottom = total[:, :, :, half:]
        return (
            [pick(top, (net.b + step) % net.nb, 2) for step in range(net.nb)],
            [pick(bottom, net.y, 1), pick(bottom, 1 - net.y, 1)],
        )

    def over_b(self, parts):
        total = parts[0].astype(F32)
        for step in range(1, self.net.nb):
            total = total + self.net.turn_b(parts[step], step).astype(F32)
        return total.astype(BF)

    def over_y(self, parts):
        return (parts[0].astype(F32) + self.net.flip_y(parts[1]).astype(F32)).astype(BF)

    def first_side(self, buffers):
        net = self.net
        top = self.over_b(buffers[0])
        bottom = self.over_y(buffers[1])
        return (
            [pick(top, net.y, 1), pick(top, 1 - net.y, 1)],
            [pick(bottom, (net.b + step) % net.nb, 1) for step in range(net.nb)],
        )

    def second_side(self, buffers):
        net = self.net
        rows = jnp.concatenate([self.over_y(buffers[0]), self.over_b(buffers[1])], axis=1)
        limit = self.last - self.first - 1
        return [
            pick(rows, jnp.clip((net.z + step) % net.nz - self.first, 0, limit)) for step in range(net.nz)
        ]

    def tree(self, total):
        for step in doublings(self.net.nz):

            def target(z, y, c, b, step=step):
                far = (z - self.first) % self.net.nz
                return ((z - step) % self.net.nz, y, c, b) if far % (2 * step) == step else None

            total = (total.astype(F32) + self.net.move(total, target).astype(F32)).astype(BF)
        return total

    def over_z(self, buffers):
        if self.last - self.first == 1:
            return [self.tree(buffers[0])]
        came = [buffers[0]]
        for step in range(1, self.net.nz):

            def target(z, y, c, b, step=step):
                goal = (z + step) % self.net.nz
                return (goal, y, c, b) if self.first <= goal < self.last else None

            came.append(self.net.move(buffers[step], target))
        return came


def sum_steps(net, array):
    targets = [lambda z, y, c, b: (z, y, 1 - c, b)]
    for step in doublings(net.nz):
        targets.append(lambda z, y, c, b, step=step: (z ^ step, y, c, b))
    for step in doublings(net.nb):
        targets.append(lambda z, y, c, b, step=step: (z, y, c, b ^ step))
    targets.append(lambda z, y, c, b: (z, 1 - y, c, b))
    for target in targets:
        array = array.astype(BF)
        came = yield net.move(array, target)
        array = array.astype(F32) + came.astype(F32)
    return array


def nn(a, b):
    return lax.dot_general(a, b, (((1,), (0,)), ((), ())), preferred_element_type=F32)


def nt(a, b):
    return lax.dot_general(a, b, (((1,), (1,)), ((), ())), preferred_element_type=F32)


def tn(a, b):
    return lax.dot_general(a, b, (((0,), (0,)), ((), ())), preferred_element_type=F32)


def two(a):
    high = a.astype(BF)
    return high, (a - high.astype(F32)).astype(BF)


def left_half(shape):
    return lax.broadcasted_iota(jnp.int32, shape, 1) < 64


def normed(values, gain, bias):
    mean = jnp.mean(values, axis=1, keepdims=True)
    centred = values - mean
    variance = jnp.mean(centred * centred, axis=1, keepdims=True)
    return centred * lax.rsqrt(variance + EPSILON) * gain + bias


def normed_back(values, gain, upstream):
    mean = jnp.mean(values, axis=1, keepdims=True)
    centred = values - mean
    variance = jnp.mean(centred * centred, axis=1, keepdims=True)
    scale = lax.rsqrt(variance + EPSILON)
    unit = centred * scale
    inner = upstream * gain
    grad = scale * (
        inner
        - jnp.mean(inner, axis=1, keepdims=True)
        - unit * jnp.mean(inner * unit, axis=1, keepdims=True)
    )
    return grad, jnp.sum(upstream * unit, axis=0, keepdims=True), jnp.sum(upstream, axis=0, keepdims=True)


def softmax_halves(values):
    left = left_half(values.shape)
    low = jnp.float32(-jnp.inf)
    top0 = jnp.max(jnp.where(left, values, low), axis=1, keepdims=True)
    top1 = jnp.max(jnp.where(left, low, values), axis=1, keepdims=True)
    raised = jnp.exp(values - jnp.where(left, top0, top1))
    sum0 = jnp.sum(jnp.where(left, raised, 0.0), axis=1, keepdims=True)
    sum1 = jnp.sum(jnp.where(left, 0.0, raised), axis=1, keepdims=True)
    return raised / jnp.where(left, sum0, sum1)


def softmax_halves_back(weights, upstream):
    left = left_half(weights.shape)
    product = weights * upstream
    sum0 = jnp.sum(jnp.where(left, product, 0.0), axis=1, keepdims=True)
    sum1 = jnp.sum(jnp.where(left, 0.0, product), axis=1, keepdims=True)
    return product - weights * jnp.where(left, sum0, sum1)


def lanes(ref, head):
    return ref[:, head * 128 : (head + 1) * 128]


def state_at(ref, seq, pair):
    start = pair % 3 * 128
    return ref[seq, pair // 3, start : start + 128, :]


def normaliser_at(ref, head):
    row = H // 2 * HD + head % 6
    parts = [ref[seq, head // 6, row : row + 1, :] for seq in range(2)]
    return jnp.concatenate([jnp.broadcast_to(part, (64, 128)) for part in parts], axis=0)


def store_state(ref, seq, pair, block, row):
    half = pair // 3
    start = pair % 3 * 128
    ref[seq, half, start : start + 64, :] = block[:64, :128]
    ref[seq, half, start + 64 : start + 128, :] = block[64:, 128:]
    tail = H // 2 * HD + pair % 3 * 2
    ref[seq, half, tail : tail + 1, :] = row[:, :128]
    ref[seq, half, tail + 1 : tail + 2, :] = row[:, 128:]


def clear_tail(ref):
    for seq in range(2):
        for half in range(2):
            ref[seq, half, 390:400, :] = jnp.zeros((10, 128), F32)


def head_kernel(x_ref, norm_ref, w_ref, map_ref, cols_ref, h_ref, proj_ref, fq_ref, fk_ref, state_ref):
    step = pl.program_id(0)

    @pl.when(step == 0)
    def _():
        h_ref[...] = normed(x_ref[...], norm_ref[0:1, :], norm_ref[1:2, :]).astype(BF)

    proj_ref[...] = nt(h_ref[...], w_ref[...]).astype(BF)

    def features(out_ref):
        for pair in range(PAIRS):
            part = lanes(proj_ref, pair)
            before = nn(jnp.concatenate([part, part], axis=1), map_ref[0, pair])
            for side in range(2):
                head = pair * 2 + side
                out_ref[:, head * 128 : (head + 1) * 128] = softmax_halves(
                    before[:, side * 128 : (side + 1) * 128]
                )

    @pl.when(step == 0)
    def _():
        features(fq_ref)

    @pl.when(step == 1)
    def _():
        features(fk_ref)

    @pl.when(step == 2)
    def _():
        clear_tail(state_ref)
        for seq in range(2):
            rows = slice(seq * 64, seq * 64 + 64)
            last = cols_ref[rows, 1:2]
            for pair in range(PAIRS):
                feats = fk_ref[rows, pair * 256 : (pair + 1) * 256].astype(BF).astype(F32) * last
                block = tn(proj_ref[rows, pair * 128 : (pair + 1) * 128], feats.astype(BF))
                store_state(state_ref, seq, pair, block, jnp.sum(feats, axis=0, keepdims=True))


def tail_kernel(
    x_ref, v_ref, fq_ref, fk_ref, state_ref, cols_ref, vis_ref, norm_ref, wo_ref, wu_ref, wd_ref,
    o_ref, rden_ref, att_ref, x1_ref, h2_ref, u_ref, g_ref, out_ref,
):
    @pl.when(pl.program_id(0) == 0)
    def _():
        visible = vis_ref[...]
        mark = cols_ref[:, 0:1]
        left = left_half((128, 128))
        for pair in range(PAIRS):
            value = lanes(v_ref, pair)
            nothing = jnp.zeros_like(value)
            state = [jnp.concatenate(two(state_at(state_ref, seq, pair)), axis=1) for seq in range(2)]
            weights = []
            totals = []
            carried = []
            for side in range(2):
                head = pair * 2 + side
                query = lanes(fq_ref, head).astype(BF)
                score = nt(query, lanes(fk_ref, head).astype(BF)) * visible
                weights.append(score.astype(BF))
                wide = query.astype(F32) * normaliser_at(state_ref, head) * mark
                totals.append(jnp.sum(score + wide, axis=1, keepdims=True))
                twice = jnp.concatenate([query, query], axis=1)
                carried.append(
                    jnp.concatenate([nt(twice[:64], state[0]), nt(twice[64:], state[1])], axis=0)
                )
            number = nn(
                jnp.concatenate(weights, axis=1),
                jnp.concatenate([jnp.where(left, value, nothing), jnp.where(left, nothing, value)], axis=0),
            )
            number = number + mark * jnp.where(left, carried[0], carried[1])
            inverse = 1.0 / jnp.where(left, totals[0], totals[1])
            output = number * inverse
            cut = slice(pair * 128, (pair + 1) * 128)
            o_ref[:, cut] = output
            rden_ref[:, cut] = inverse
            att_ref[:, cut] = output.astype(BF)
        x1 = x_ref[...] + nn(att_ref[...], wo_ref[...])
        x1_ref[...] = x1
        h2_ref[...] = normed(x1, norm_ref[0:1, :], norm_ref[1:2, :]).astype(BF)
        out_ref[...] = x1

    u = nt(h2_ref[...], wu_ref[...])
    u_ref[...] = u
    inner = jnp.tanh(0.7978845608028654 * (u + 0.044715 * (u * u * u)))
    g = (0.5 * u * (1.0 + inner)).astype(BF)
    g_ref[...] = g
    out_ref[...] += nn(g, wd_ref[...])


def back_kernel(
    e_ref, u_ref, x1_ref, norm_ref, wd_ref, wu_ref, wo_ref, o_ref, rden_ref, fq_ref, cols_ref,
    du_ref, dx1_ref, ebx_ref, dn_ref, dd_ref, state_ref, gn_ref, total,
):
    step = pl.program_id(0)
    dg = nt(e_ref[...].astype(BF), wd_ref[...])
    u = u_ref[...]
    inner = jnp.tanh(0.7978845608028654 * (u + 0.044715 * (u * u * u)))
    slope = 0.5 * (1.0 + inner) + (0.5 * u) * (1.0 - inner * inner) * (
        0.7978845608028654 * (1.0 + 0.134145 * (u * u))
    )
    du = (dg * slope).astype(BF)
    du_ref[...] = du
    part = nn(du, wu_ref[...])

    @pl.when(step == 0)
    def _():
        total[...] = part

    @pl.when(step > 0)
    def _():
        total[...] += part

    @pl.when(step == pl.num_programs(0) - 1)
    def _():
        grad, gain, bias = normed_back(x1_ref[...], norm_ref[0:1, :], total[...])
        gn_ref[0:1, :] = gain
        gn_ref[1:2, :] = bias
        dx1 = e_ref[...] + grad
        dx1_ref[...] = dx1
        low = dx1.astype(BF)
        ebx_ref[...] = low
        dn_ref[...] = nt(low, wo_ref[...]).astype(BF).astype(F32) * rden_ref[...]
        left = left_half((128, 128))
        lane = lax.broadcasted_iota(jnp.int32, (128, 128), 1)
        clear_tail(state_ref)
        columns = jnp.zeros((128, 128), F32)
        for pair in range(PAIRS):
            dn = lanes(dn_ref, pair)
            product = dn * lanes(o_ref, pair)
            d0 = -jnp.sum(jnp.where(left, product, 0.0), axis=1, keepdims=True)
            d1 = -jnp.sum(jnp.where(left, 0.0, product), axis=1, keepdims=True)
            columns = jnp.where(lane == pair * 2, d0, jnp.where(lane == pair * 2 + 1, d1, columns))
            for seq in range(2):
                rows = slice(seq * 64, seq * 64 + 64)
                mark = cols_ref[rows, 0:1]
                high, rest = two(dn[rows] * mark)
                feats = fq_ref[rows, pair * 256 : (pair + 1) * 256].astype(BF)
                block = tn(jnp.concatenate([high, rest], axis=0), jnp.concatenate([feats, feats], axis=0))
                wide = feats.astype(F32)
                row = jnp.concatenate(
                    [
                        jnp.sum(wide[:, :128] * (d0[rows] * mark), axis=0, keepdims=True),
                        jnp.sum(wide[:, 128:] * (d1[rows] * mark), axis=0, keepdims=True),
                    ],
                    axis=1,
                )
                store_state(state_ref, seq, pair, block, row)
        dd_ref[...] = columns


def fold_map(pair_weights, low_q):
    left = left_half((128, 128))
    folded = [weight - pltpu.roll(weight, 64, 1) for weight in pair_weights]
    grad = jnp.where(left, folded[0], pltpu.roll(folded[1], 64, 1))
    high, rest = two(grad)
    twice = jnp.concatenate([low_q, low_q], axis=0)
    table = tn(twice, jnp.concatenate([high, rest], axis=0))
    return jnp.where(left[:64], table[:64], table[64:])


def query_kernel(
    q_ref, v_ref, fq_ref, fk_ref, state_ref, dn_ref, dd_ref, cols_ref, vis_ref, map_ref,
    dq_ref, dmap_ref, dfk_ref, dv_ref,
):
    visible = vis_ref[...]
    low_visible = visible.astype(BF)
    mark = cols_ref[:, 0:1]
    left = left_half((128, 128))
    for pair in range(PAIRS):
        value = lanes(v_ref, pair)
        dn = lanes(dn_ref, pair)
        twice = jnp.concatenate([value, value], axis=1)
        state = [two(state_at(state_ref, seq, pair)) for seq in range(2)]
        weights = []
        shifts = []
        turned = []
        for side in range(2):
            head = pair * 2 + side
            wide = lanes(fq_ref, head)
            query = wide.astype(BF)
            key = lanes(fk_ref, head).astype(BF)
            score = (nt(query, key) * visible).astype(BF)
            mine = jnp.where(left, dn, 0.0) if side == 0 else jnp.where(left, 0.0, dn)
            high, rest = two(mine)
            dd = dd_ref[:, head : head + 1]
            shift = (nt(jnp.concatenate([high, rest], axis=1), twice) + dd).astype(BF) * low_visible
            carried = jnp.concatenate(
                [
                    nn(
                        jnp.concatenate([high[rows], high[rows], rest[rows]], axis=1),
                        jnp.concatenate([state[seq][0], state[seq][1], state[seq][0]], axis=0),
                    )
                    for seq, rows in ((0, slice(0, 64)), (1, slice(64, 128)))
                ],
                axis=0,
            )
            dfq = nn(shift, key) + mark * (carried + dd * normaliser_at(state_ref, head))
            dfk_ref[:, head * 128 : (head + 1) * 128] = tn(shift, query)
            weights.append(softmax_halves_back(wide, dfq))
            shifts.append(score)
            turned.append(high)
        cut = slice(pair * 128, (pair + 1) * 128)
        dv_ref[:, cut] = tn(jnp.concatenate(shifts, axis=0), jnp.concatenate(turned, axis=0))
        low = jnp.concatenate(weights, axis=1).astype(BF)
        dq_ref[:, cut] = nt(low, map_ref[0, pair, :128, :]).astype(BF)
        dmap_ref[:, cut] = fold_map(weights, lanes(q_ref, pair))


def key_kernel(
    k_ref, v_ref, fk_ref, state_ref, dfk_ref, dv_ref, dq_ref, cols_ref, map_ref, w_ref, x_ref, norm_ref, dx1_ref,
    dqkv_ref, dmap_ref, e_ref, gn_ref,
):
    last = cols_ref[:, 1:2]
    left = left_half((128, 128))
    dqkv_ref[:, :D] = dq_ref[...]
    for pair in range(PAIRS):
        value = lanes(v_ref, pair)
        nothing = jnp.zeros_like(value)
        state = [two(state_at(state_ref, seq, pair)) for seq in range(2)]
        weights = []
        grads = []
        for side in range(2):
            head = pair * 2 + side
            wide = lanes(fk_ref, head)
            key = wide.astype(BF)
            mine = jnp.where(left, value, nothing) if side == 0 else jnp.where(left, nothing, value)
            carried = []
            turned = []
            for seq, rows in ((0, slice(0, 64)), (1, slice(64, 128))):
                high, rest = state[seq]
                carried.append(
                    nn(
                        jnp.concatenate([mine[rows], mine[rows]], axis=1),
                        jnp.concatenate([high, rest], axis=0),
                    )
                )
                turned.append(nt(key[rows], high))
            carried = jnp.concatenate(carried, axis=0)
            dfk = lanes(dfk_ref, head) + last * (carried + normaliser_at(state_ref, head))
            weights.append(softmax_halves_back(wide, dfk))
            grads.append(jnp.concatenate(turned, axis=0))
        cut = slice(pair * 128, (pair + 1) * 128)
        dv = lanes(dv_ref, pair) + last * jnp.where(left, grads[0], grads[1])
        dqkv_ref[:, 2 * D + pair * 128 : 2 * D + (pair + 1) * 128] = dv.astype(BF)
        low = jnp.concatenate(weights, axis=1).astype(BF)
        dqkv_ref[:, D + pair * 128 : D + (pair + 1) * 128] = nt(low, map_ref[0, pair, :128, :]).astype(BF)
        dmap_ref[:, cut] = fold_map(weights, lanes(k_ref, pair))
    upstream = nn(dqkv_ref[...], w_ref[...])
    grad, gain, bias = normed_back(x_ref[...], norm_ref[0:1, :], upstream)
    gn_ref[0:1, :] = gain
    gn_ref[1:2, :] = bias
    e_ref[...] = dx1_ref[...] + grad


def store_sides(block, keep_ref, send_ref):
    zero = lax.rem(lax.axis_index("seq"), 2) == 0
    groups, size = keep_ref.shape[:2]
    for group in range(groups):
        low = block[group * 2 * size : group * 2 * size + size]
        high = block[group * 2 * size + size : group * 2 * size + 2 * size]
        keep_ref[group] = jnp.where(zero, low, high).astype(BF)
        send_ref[group] = jnp.where(zero, high, low).astype(BF)


def rows_kernel(att_ref, ebx_ref, du_ref, h2_ref, g_ref, e_ref, keep_ref, send_ref, held):
    terms = ((0, D, att_ref, ebx_ref), (D, D + FF, du_ref, h2_ref), (D + FF, D + 2 * FF, g_ref, e_ref))
    for step in range((D + 2 * FF) // TILE):
        start = step * TILE

        @pl.when(pl.program_id(0) == step)
        def _(start=start):
            for first, last, left, right in terms:
                low = max(start, first)
                high = min(start + TILE, last)
                if low < high:
                    held[low - start : high - start, :] = tn(
                        left[:, low - first : high - first], right[...].astype(BF)
                    )
            store_sides(held, keep_ref, send_ref)


def proj_rows_kernel(dqkv_ref, h_ref, keep_ref, send_ref, held):
    held[...] = tn(dqkv_ref[...], h_ref[...])
    store_sides(held, keep_ref, send_ref)


def split_kernel(runs, nb, *refs):
    tops = refs[2 * len(runs) : 2 * len(runs) + nb]
    bottoms = refs[2 * len(runs) + nb :]
    half = tops[0].shape[2]
    y = lax.rem(lax.axis_index("seq") // 2, 2)
    b = lax.axis_index("batch")
    start = 0
    for index, count in enumerate(runs):
        keep, came = refs[2 * index : 2 * index + 2]

        @pl.when((pl.program_id(0) >= start) & (pl.program_id(0) < start + count))
        def _(keep=keep, came=came):
            def rows(row_y, row_b, offset):
                at = pl.ds(pl.multiple_of(row_b * 2 * half + offset, 16), half)
                return (keep[row_y, at, :].astype(F32) + came[row_y, at, :].astype(F32)).astype(BF)

            for step, top in enumerate(tops):
                for side in range(2):
                    top[0, side] = rows(side, lax.rem(b + step, nb), 0)
            for step, bottom in enumerate(bottoms):
                for side in range(nb):
                    bottom[0, side] = rows(lax.rem(y + step, 2), side, half)

        start += count


def split_call(net, pairs):
    size = pairs[0][0].shape[1]
    half = size // net.nb // 2
    runs = [keep.shape[0] // 2 for keep, _ in pairs]
    planes = sum(runs)
    operands = []
    start = 0
    for pair, count in zip(pairs, runs):

        def index(i, start=start, count=count):
            return (jnp.clip(i - start, 0, count - 1), 0, 0)

        operands += [(array, (2, size, D), index) for array in pair]
        start += count
    outputs = [((planes, 2, half, D), BF, (1, 2, half, D), lambda i: (i, 0, 0, 0))] * net.nb
    outputs += [((planes, net.nb, half, D), BF, (1, net.nb, half, D), lambda i: (i, 0, 0, 0))] * 2
    parts = call(functools.partial(split_kernel, runs, net.nb), (planes,), operands, outputs, 0)
    return parts[: net.nb], parts[net.nb :]


def whole(array):
    rank = array.ndim
    return pl.BlockSpec(array.shape, lambda *_: (0,) * rank)


def call(kernel, grid, operands, outputs, flops, scratch=()):
    arrays = []
    in_specs = []
    for operand in operands:
        if isinstance(operand, tuple):
            arrays.append(operand[0])
            in_specs.append(pl.BlockSpec(operand[1], operand[2]))
        else:
            arrays.append(operand)
            in_specs.append(whole(operand))
    shapes = [jax.ShapeDtypeStruct(out[0], out[1]) for out in outputs]
    out_specs = []
    for out, shape in zip(outputs, shapes):
        out_specs.append(pl.BlockSpec(out[2], out[3]) if len(out) > 2 else whole(shape))
    moved = sum(a.size * a.dtype.itemsize for a in shapes)
    for spec, a in zip(in_specs, arrays):
        moved += a.size * a.dtype.itemsize if a.shape[0] < 9000 else 4 * D * D
    return pl.pallas_call(
        kernel,
        grid=grid,
        in_specs=in_specs,
        out_specs=out_specs,
        out_shape=shapes,
        scratch_shapes=list(scratch),
        compiler_params=pltpu.CompilerParams(vmem_limit_bytes=WIDE_LIMIT),
        cost_estimate=pl.CostEstimate(flops=flops, bytes_accessed=moved, transcendentals=0),
    )(*arrays)


STATE = (2, 2, H // 2 * HD + 16, 128)
ROWS = 128
CHUNK = 512
TILE = 3 * D // 2
CHUNKS = FF // CHUNK


def still(*index):
    return lambda i: index


def forward_layer(net, x, flat, norms, maps, cols, visible, gates):
    h1, proj, fq, fk, local = call(
        head_kernel,
        (3,),
        [
            x,
            norms[0],
            (flat, (D, D), lambda i: (i, 0)),
            (maps, (1, PAIRS, 256, 256), lambda i: (jnp.minimum(i, 1), 0, 0, 0)),
            cols,
        ],
        [
            ((ROWS, D), BF),
            ((ROWS, 3 * D), BF, (ROWS, D), lambda i: (0, i)),
            ((ROWS, H * 128), F32),
            ((ROWS, H * 128), F32),
            (STATE, F32),
        ],
        2 * ROWS * 3 * D * D,
    )
    state = finish(scan_steps(net, local, gates, False), None)
    o, rden, att, x1, h2, u, g, result = call(
        tail_kernel,
        (CHUNKS,),
        [
            x,
            (proj, (ROWS, D), still(0, 2)),
            fq,
            fk,
            state,
            cols,
            visible,
            norms[1],
            (flat, (D, D), still(3, 0)),
            (flat, (CHUNK, D), lambda i: (CHUNKS + i, 0)),
            (flat, (CHUNK, D), lambda i: (2 * CHUNKS + i, 0)),
        ],
        [
            ((ROWS, D), F32),
            ((ROWS, D), F32),
            ((ROWS, D), BF),
            ((ROWS, D), F32),
            ((ROWS, D), BF),
            ((ROWS, FF), F32, (ROWS, CHUNK), lambda i: (0, i)),
            ((ROWS, FF), BF, (ROWS, CHUNK), lambda i: (0, i)),
            ((ROWS, D), F32),
        ],
        2 * ROWS * 9 * D * D,
    )
    return result, (x, h1, proj, fq, fk, state, o, rden, att, x1, h2, u, g)


def back_call(e, flat, norms, cols, kept):
    x, h1, proj, fq, fk, state, o, rden, att, x1, h2, u, g = kept
    return call(
        back_kernel,
        (CHUNKS,),
        [
            e,
            (u, (ROWS, CHUNK), lambda i: (0, i)),
            x1,
            norms[1],
            (flat, (CHUNK, D), lambda i: (2 * CHUNKS + i, 0)),
            (flat, (CHUNK, D), lambda i: (CHUNKS + i, 0)),
            (flat, (D, D), still(3, 0)),
            o,
            rden,
            fq,
            cols,
        ],
        [
            ((ROWS, FF), BF, (ROWS, CHUNK), lambda i: (0, i)),
            ((ROWS, D), F32),
            ((ROWS, D), BF),
            ((ROWS, D), F32),
            ((ROWS, 128), F32),
            (STATE, F32),
            ((2, D), F32),
        ],
        2 * ROWS * 9 * D * D,
        [pltpu.VMEM((ROWS, D), F32)],
    )


def query_call(maps, cols, visible, kept, back):
    proj, fq, fk, state = kept[2:6]
    dn, dd = back[3:5]
    return call(
        query_kernel,
        (1,),
        [
            (proj, (ROWS, D), still(0, 0)),
            (proj, (ROWS, D), still(0, 2)),
            fq,
            fk,
            state,
            dn,
            dd,
            cols,
            visible,
            (maps, (1, PAIRS, 256, 256), still(0, 0, 0, 0)),
        ],
        [((ROWS, D), BF), ((HD, D), F32), ((ROWS, H * 128), F32), ((ROWS, D), F32)],
        2 * ROWS * 4 * D * D,
    )


def sides(net, count):
    side = (4 * D + 2 * FF) // (4 * net.nz)
    shape = (count // (2 * side), side, D)
    return [(shape, BF, (TILE // (2 * side), side, D), lambda i: (i, 0, 0))] * 2


def rows_call(net, e, kept, back):
    att, h2, g = kept[8], kept[10], kept[12]
    du, ebx = back[0], back[2]
    return call(
        rows_kernel,
        ((D + 2 * FF) // TILE,),
        [att, ebx, du, h2, g, e],
        sides(net, D + 2 * FF),
        2 * ROWS * 9 * D * D,
        [pltpu.VMEM((TILE, D), F32)],
    )


def key_call(flat, norms, maps, cols, kept, back, query, state_grad):
    x, proj, fk = kept[0], kept[2], kept[4]
    dx1 = back[1]
    dq, query_map, dfk, dv = query
    return call(
        key_kernel,
        (1,),
        [
            (proj, (ROWS, D), still(0, 1)),
            (proj, (ROWS, D), still(0, 2)),
            fk,
            state_grad,
            dfk,
            dv,
            dq,
            cols,
            (maps, (1, PAIRS, 256, 256), still(1, 0, 0, 0)),
            (flat, (3 * D, D), still(0, 0)),
            x,
            norms[0],
            dx1,
        ],
        [((ROWS, 3 * D), BF), ((HD, D), F32), ((ROWS, D), F32), ((2, D), F32)],
        2 * ROWS * 3 * D * D,
    )


def proj_rows_call(net, kept, dqkv):
    return call(
        proj_rows_kernel,
        (3 * D // TILE,),
        [(dqkv, (ROWS, TILE), lambda i: (0, i)), kept[1]],
        sides(net, 3 * D),
        2 * ROWS * 3 * D * D,
        [pltpu.VMEM((TILE, D), F32)],
    )


def pair_maps(fmap):
    grid = fmap.reshape(LAYERS, 2, HD, PAIRS, 2, HD).transpose(0, 1, 3, 4, 2, 5)
    both = jnp.concatenate([grid, -grid], axis=-1)
    empty = jnp.zeros_like(both[:, :, :, 0])
    top = jnp.concatenate([both[:, :, :, 0], empty], axis=-1)
    bottom = jnp.concatenate([empty, both[:, :, :, 1]], axis=-1)
    return jnp.concatenate(two(jnp.concatenate([top, bottom], axis=3)), axis=3)


def doc_layout(doc_lengths, start, span):
    ends = jnp.cumsum(doc_lengths, axis=1)
    places = start + jnp.arange(span, dtype=jnp.int32)
    documents = jnp.sum((places[None, :, None] >= ends[:, None, :]).astype(jnp.int32), axis=2)
    before = jnp.sum((start - 1 >= ends).astype(jnp.int32), axis=1)
    previous = jnp.where(start > 0, before, -1)
    mark = (documents == previous[:, None]).reshape(-1, 1)
    last = (documents == documents[:, span - 1 :]).reshape(-1, 1)
    lane = jnp.arange(128)[None, :]
    cols = jnp.where(lane == 0, mark, (lane == 1) & last).astype(F32)
    names = (documents + (DOCS + 1) * jnp.arange(documents.shape[0])[:, None]).reshape(-1)
    lower = jnp.arange(names.shape[0])[:, None] >= jnp.arange(names.shape[0])[None, :]
    visible = (lower & (names[:, None] == names[None, :])).astype(F32)
    return cols, visible


def body(tokens, doc_lengths, weights, norm_gain, norm_bias, fmap, cotangent):
    net = Net()
    sequences, span = tokens.shape[:2]
    start = lax.axis_index("seq") * span
    gathered = [lax.all_gather(weights[layer], AXES, axis=0, tiled=True) for layer in range(LAYERS)]
    rows = sequences * span
    cols, visible = doc_layout(doc_lengths, start, span)
    last_doc = last_docs(doc_lengths, span)
    gates = [scan_gates(net, last_doc, reverse) for reverse in (False, True)]
    maps = pair_maps(fmap)
    norms = jnp.stack([norm_gain, norm_bias], axis=2)
    x = tokens.reshape(rows, D).astype(F32)
    e1 = cotangent.reshape(rows, D).astype(F32)
    gathered[0], gates, cols, visible, maps, norms, x, e1 = tie(
        gathered[0], gates, cols, visible, maps, norms, x, e1
    )
    saved = []
    for layer in range(LAYERS):
        x, kept = forward_layer(net, x, gathered[layer], norms[layer], maps[layer], cols, visible, gates[0])
        saved.append(kept)
    result = x.astype(BF).reshape(tokens.shape)
    cut = net.nz * 3 * D // (4 * D + 2 * FF)
    rest_sum = Scatter(net, cut, net.nz)
    both_sum = Scatter(net, 0, net.nz)
    head_sum = Scatter(net, 0, cut)
    kept0, kept1 = saved

    back1 = back_call(e1, gathered[1], norms[1], cols, kept1)
    scan = scan_steps(net, back1[5], gates[1], True)
    came = next(scan)
    rest1 = rows_call(net, e1, kept1, back1)
    came, rest1 = tie(came, rest1)
    came = scan.send(came)
    query1 = query_call(maps[1], cols, visible, kept1, back1)
    came, query1 = tie(came, query1)
    came = scan.send(came)
    rest1 = rest_sum.core(rest1)
    came, rest1 = tie(came, rest1)
    for _ in range(1, len(list(doublings(net.nz)))):
        came = scan.send(came)
    came = scan.send(came)
    came, rest1 = tie(came, rest1)
    state_grad = finish(scan, came)
    dqkv1, key_map1, e0, norm_one1 = key_call(
        gathered[1], norms[1], maps[1], cols, kept1, back1, query1, state_grad
    )
    small1 = jnp.concatenate([query1[1], key_map1, norm_one1, back1[6]], axis=0)

    back0 = back_call(e0, gathered[0], norms[0], cols, kept0)
    scan = scan_steps(net, back0[5], gates[1], True)
    came = next(scan)
    rest0 = rows_call(net, e0, kept0, back0)
    head1 = proj_rows_call(net, kept1, dqkv1)
    rest1 = rest_sum.first_side(rest1)
    came, rest0, head1, rest1 = tie(came, rest0, head1, rest1)
    came = scan.send(came)
    came, rest1 = tie(came, rest1)
    came = scan.send(came)
    both = both_sum.core(head1, rest0)
    came, tops, bottoms = tie(came, *both)
    for _ in range(1, len(list(doublings(net.nz)))):
        came = scan.send(came)
    rest1 = rest_sum.second_side(rest1)
    query0 = query_call(maps[0], cols, visible, kept0, back0)
    came, rest1, query0 = tie(came, rest1, query0)
    came = scan.send(came)
    came, rest1, bottoms = tie(came, rest1, bottoms)
    both = (tops, bottoms)
    state_grad = finish(scan, came)
    dqkv0, key_map0, e, norm_one0 = key_call(
        gathered[0], norms[0], maps[0], cols, kept0, back0, query0, state_grad
    )

    head0 = proj_rows_call(net, kept0, dqkv0)
    small0 = jnp.concatenate([query0[1], key_map0, norm_one0, back0[6]], axis=0)
    summing = sum_steps(net, jnp.stack([small0, small1]))
    came = next(summing)
    head0 = head_sum.core(head0)
    came, head0 = tie(came, head0)
    came = summing.send(came)
    rest1 = rest_sum.over_z(rest1)
    both = both_sum.first_side(both)
    both, rest1 = tie(both, rest1)
    head0 = head_sum.first_side(head0)
    came, head0, both = tie(came, head0, both)
    came = summing.send(came)
    both = both_sum.second_side(both)
    head0 = head_sum.second_side(head0)
    came, both, head0 = tie(came, both, head0)
    came = summing.send(came)
    both = both_sum.over_z(both)
    head0 = head_sum.over_z(head0)
    came, both = tie(came, both)
    small = finish(summing, came)

    def total(parts):
        return sum(part.astype(F32) for part in parts)

    both = total(both)
    shards = [jnp.where(net.z < cut, total(head0), both), jnp.where(net.z < cut, both, total(rest1))]
    cut = 2 * HD
    return (
        result,
        e.reshape(tokens.shape),
        jnp.stack(shards),
        small[:, cut::2],
        small[:, cut + 1 :: 2],
        small[:, :cut].reshape(fmap.shape),
    )


def solution(mesh):
    in_specs = (
        P("batch", "seq", None),
        P("batch", None),
        P(None, ("seq", "batch"), None),
        P(),
        P(),
        P(),
        P("batch", "seq", None),
    )
    out_specs = (
        P("batch", "seq", None),
        P("batch", "seq", None),
        P(None, ("seq", "batch"), None),
        P(),
        P(),
        P(),
    )
    return jax.shard_map(body, mesh=mesh, in_specs=in_specs, out_specs=out_specs, check_vma=False)
```

```python
import functools

import jax
import jax.numpy as jnp
from jax import lax
from jax.experimental import pallas as pl
from jax.experimental.pallas import tpu as pltpu
from jax.sharding import PartitionSpec as P

D = 768
H = 12
HD = 64
FF = 3072
LAYERS = 2
DOCS = 4
EPSILON = 1e-05
F32 = jnp.float32
BF = jnp.bfloat16
PAIRS = H // 2
WIDE_LIMIT = 40 * 1024 * 1024


AXES = ("seq", "batch")


class Net:
    def __init__(self):
        self.nz = lax.axis_size("seq") // 4
        self.nb = lax.axis_size("batch")
        place = lax.axis_index("seq")
        self.z = place // 4
        self.y = (place // 2) % 2
        self.c = place % 2
        self.b = lax.axis_index("batch")

    def move(self, array, target):
        pairs = []
        for index in range(self.nz * 4 * self.nb):
            place = index // self.nb
            goal = target(place // 4, (place // 2) % 2, place % 2, index % self.nb)
            if goal is not None:
                z, y, c, b = goal
                pairs.append((index, ((z * 2 + y) * 2 + c) * self.nb + b))
        return lax.ppermute(array, AXES, pairs)

    def core(self, array):
        return self.move(array, lambda z, y, c, b: (z, y, 1 - c, b))

    def flip_y(self, array):
        return self.move(array, lambda z, y, c, b: (z, 1 - y, c, b))

    def turn_b(self, array, step):
        return self.move(array, lambda z, y, c, b: (z, y, c, (b + step) % self.nb))

    def shift_z(self, array, step):
        def target(z, y, c, b):
            return (z + step, y, c, b) if 0 <= z + step < self.nz else None

        return self.move(array, target)


def pick(array, index, axis=0):
    return lax.dynamic_index_in_dim(array, index, axis, False)


def last_docs(doc_lengths, span):
    ends = jnp.cumsum(doc_lengths, axis=1)

    def last_doc(block):
        found = jnp.sum(((block + 1) * span - 1 >= ends).astype(jnp.int32), axis=1)
        return jnp.where(block < 0, -1, found)

    return last_doc


def doublings(count):
    step = 1
    while step < count:
        yield step
        step *= 2


def scan_gates(net, last_doc, reverse):
    base = 4 * net.z
    first = base + 2 * net.y
    if reverse:
        pairs = [(first, first - 1), (base + 1, base - 1), (base + 3, base + 1), (first + 1, first)]
        for step in doublings(net.nz):
            pairs += [(4 * (net.z + step) - 1, base + 3), (4 * (net.z + step) - 1, base - 1)]
    else:
        pairs = [(first, first + 1), (base + 1, base + 3), (base - 1, base + 1), (first - 1, first)]
        for step in doublings(net.nz):
            pairs += [(4 * (net.z - step) + 3, base - 1), (4 * (net.z - step) + 3, base + 3)]
    same = jnp.stack([last_doc(a) == last_doc(b) for a, b in pairs])
    return pick(same, net.c, 1).astype(F32)


def scan_steps(net, packed, gates, reverse):
    wide = F32
    low = F32
    mine = pick(packed, net.c)
    theirs = yield net.core(pick(packed, 1 - net.c))
    zero = jnp.equal(net.c, 0)
    part0 = jnp.where(zero, mine, theirs).astype(wide)
    part1 = jnp.where(zero, theirs, mine).astype(wide)
    if reverse:
        chip = part0 + gates[0] * part1
    else:
        chip = gates[0] * part0 + part1
    chip = chip.astype(low)
    own = pick(chip, net.y)
    other = yield net.flip_y(pick(chip, 1 - net.y))
    down = jnp.equal(net.y, 0)
    row0 = jnp.where(down, own, other).astype(wide)
    row1 = jnp.where(down, other, own).astype(wide)
    if reverse:
        plane = row0 + gates[1] * row1
    else:
        plane = gates[1] * row0 + row1
    entering = jnp.zeros(plane.shape, wide)
    for index, step in enumerate(doublings(net.nz)):
        part = yield net.shift_z(plane, -step if reverse else step)
        entering = entering + gates[4 + 2 * index] * part
        plane = plane + gates[5 + 2 * index] * part
    if reverse:
        row1_in = entering
        row0_in = gates[2] * entering + row1
    else:
        row0_in = entering
        row1_in = gates[2] * entering + row0
    own_in = jnp.where(down, row0_in, row1_in)
    other_in = yield net.flip_y(jnp.where(down, row1_in, row0_in).astype(low))
    other_in = other_in.astype(wide)
    chip_in = jnp.where(down, jnp.stack([own_in, other_in]), jnp.stack([other_in, own_in]))
    if reverse:
        core1_in = chip_in
        core0_in = gates[3] * chip_in + part1
    else:
        core0_in = chip_in
        core1_in = gates[3] * chip_in + part0
    core0_in = core0_in.astype(low)
    core1_in = core1_in.astype(low)
    kept = jnp.where(zero, core0_in, core1_in)
    sent = yield net.core(jnp.where(zero, core1_in, core0_in))
    return jnp.where(zero, jnp.stack([kept, sent]), jnp.stack([sent, kept]))


def finish(steps, value):
    while True:
        try:
            value = steps.send(value)
        except StopIteration as stop:
            return stop.value


def tie(*groups):
    return lax.optimization_barrier(groups)


class Gather:
    def __init__(self, net, shard):
        self.net = net
        self.shard = shard
        self.groups = []

    def along_z(self, shard, step):
        return self.net.move(shard, lambda z, y, c, b: ((z + step) % self.net.nz, y, c, b))

    def sides(self, blocks):
        return self.net.turn_b(blocks, 1), self.net.flip_y(blocks)

    def corners(self, over_b, over_y):
        half = over_b.shape[1] // 2
        return self.net.flip_y(over_b[:, :half]), self.net.turn_b(over_y[:, half:], 1)

    def add(self, steps, blocks, sides, corners):
        self.groups.append((steps, (blocks, *sides, *corners), (self.edges(blocks, sides), self.points(corners))))

    def edges(self, blocks, sides):
        return self.net.core(jnp.concatenate([blocks, *sides], axis=0))

    def points(self, corners):
        return self.net.core(jnp.concatenate(corners, axis=1))

    def rows(self, first, last):
        net = self.net
        size = self.shard.shape[0]
        arrays = []
        for _, mine, other in self.groups:
            arrays += [*mine, *other]
        steps = [group[0] for group in self.groups]
        blocks = (last - first) * 4 * net.nb
        return pl.pallas_call(
            functools.partial(place_kernel, steps, first, last, size),
            in_specs=[pl.BlockSpec(memory_space=pl.ANY)] * len(arrays),
            out_specs=pl.BlockSpec(memory_space=pl.ANY),
            out_shape=jax.ShapeDtypeStruct((blocks * size, D), BF),
            scratch_shapes=[
                pltpu.VMEM((blocks * size, D), BF),
                pltpu.SemaphoreType.DMA((last - first, 10)),
                pltpu.SemaphoreType.DMA((last - first,)),
            ],
            compiler_params=pltpu.CompilerParams(vmem_limit_bytes=60 * 1024 * 1024),
            cost_estimate=pl.CostEstimate(flops=0, bytes_accessed=blocks * size * D * 4, transcendentals=0),
        )(*arrays)


def place_kernel(steps, first, last, size, *refs):
    arrays, (out, held, in_sems, out_sems) = refs[:-4], refs[-4:]
    place = lax.axis_index("seq")
    z = place // 4
    y = lax.rem(place // 2, 2)
    c = lax.rem(place, 2)
    b = lax.axis_index("batch")
    half = size // 2
    plane_rows = 8 * size

    def copies(plane, group, index):
        mine = arrays[7 * group : 7 * group + 5]
        edges, points = arrays[7 * group + 5 : 7 * group + 7]
        count = len(steps[group])
        spots = ((0, 0, 0), (0, 1, 0), (1, 0, 0), (1, 1, 0), (1, 1, half))
        parts = [(array.at[index], spot, 0) for array, spot in zip(mine, spots)]
        parts += [(edges.at[count * slot + index], spots[slot], 1) for slot in range(3)]
        parts.append((points.at[index], spots[3], 1))
        made = []
        for number, (source, (dy, db, offset), dc) in enumerate(parts):
            row = (lax.rem(y + dy, 2) * 2 + lax.rem(c + dc, 2)) * 2 + lax.rem(b + db, 2)
            start = pl.multiple_of((plane - first) * plane_rows + row * size + offset, 16)
            target = held.at[pl.ds(start, source.shape[0])]
            made.append(pltpu.make_async_copy(source, target, in_sems.at[plane - first, number]))
        return made

    def each(plane, act):
        for group, kinds in enumerate(steps):
            for index, step in enumerate(kinds):

                @pl.when(lax.rem(z - plane + 4, 4) == step)
                def _(group=group, index=index):
                    for copy in copies(plane, group, index):
                        act(copy)

    def output(plane):
        rows = pl.ds((plane - first) * plane_rows, plane_rows)
        return pltpu.make_async_copy(held.at[rows], out.at[rows], out_sems.at[plane - first])

    for plane in range(first, last):
        each(plane, lambda copy: copy.start())
    for plane in range(first, last):
        each(plane, lambda copy: copy.wait())
        output(plane).start()
    for plane in range(first, last):
        output(plane).wait()


class Scatter:
    def __init__(self, net, first, last):
        self.net = net
        self.first = first
        self.last = last

    def split(self, pairs):
        net = self.net
        if (pairs[0][0].shape[1] // net.nb) % 32 == 0:
            return split_call(net, pairs)
        total = jnp.concatenate([(a.astype(F32) + b.astype(F32)).astype(BF) for a, b in pairs], axis=0)
        total = total.reshape(self.last - self.first, 2, net.nb, -1, D)
        half = total.shape[3] // 2
        top = total[:, :, :, :half]
        bottom = total[:, :, :, half:]
        return (
            [pick(top, (net.b + step) % net.nb, 2) for step in range(net.nb)],
            [pick(bottom, net.y, 1), pick(bottom, 1 - net.y, 1)],
        )

    def send_b(self, parts):
        return [parts[0]] + [self.net.turn_b(parts[step], step) for step in range(1, self.net.nb)]

    def send_y(self, parts):
        return [parts[0], self.net.flip_y(parts[1])]

    def first_send(self, buffers):
        return self.send_b(buffers[0]), self.send_y(buffers[1])

    def first_add(self, came):
        net = self.net
        top = add_up(came[0]).astype(BF)
        bottom = add_up(came[1]).astype(BF)
        return (
            [pick(top, net.y, 1), pick(top, 1 - net.y, 1)],
            [pick(bottom, (net.b + step) % net.nb, 1) for step in range(net.nb)],
        )

    def second_send(self, buffers):
        return self.send_y(buffers[0]), self.send_b(buffers[1])

    def second_add(self, came):
        return jnp.concatenate([add_up(part).astype(BF) for part in came], axis=1)

    def z_send(self, rows):
        net = self.net
        limit = self.last - self.first - 1
        came = []
        for step in range(net.nz):
            part = pick(rows, jnp.clip((net.z + step) % net.nz - self.first, 0, limit))

            def target(z, y, c, b, step=step):
                goal = (z + step) % net.nz
                return (goal, y, c, b) if self.first <= goal < self.last else None

            came.append(net.move(part, target) if step else part)
        return came

    def z_halves(self, rows):
        net = self.net
        empty = [jnp.zeros((count,) + rows.shape[1:], BF) for count in (self.first, net.nz - self.last)]
        rows = jnp.concatenate([empty[0], rows, empty[1]], axis=0)
        step = net.nz // 2
        while step:
            upper = (net.z // step) % 2
            halves = rows.reshape((2, step) + rows.shape[1:])
            kept = pick(halves, upper)
            came = yield net.move(pick(halves, 1 - upper), lambda z, y, c, b, step=step: (z ^ step, y, c, b))
            rows = (kept.astype(F32) + came.astype(F32)).astype(BF)
            step //= 2
        return [rows[0]]

    def z_tree(self, rows):
        total = rows[0]
        for step in doublings(self.net.nz):

            def target(z, y, c, b, step=step):
                far = (z - self.first) % self.net.nz
                return ((z - step) % self.net.nz, y, c, b) if far % (2 * step) == step else None

            total = (total.astype(F32) + self.net.move(total, target).astype(F32)).astype(BF)
        return [total]

    def z_sum(self, rows):
        return self.z_tree(rows) if self.last - self.first == 1 else self.z_send(rows)


def add_up(parts):
    return sum(part.astype(F32) for part in parts)


def sum_steps(net, array):
    targets = []
    for step in doublings(net.nz):
        targets.append(lambda z, y, c, b, step=step: (z ^ step, y, c, b))
    for step in doublings(net.nb):
        targets.append(lambda z, y, c, b, step=step: (z, y, c, b ^ step))
    targets.append(lambda z, y, c, b: (z, y, 1 - c, b))
    targets.append(lambda z, y, c, b: (z, 1 - y, c, b))
    for target in targets:
        array = array.astype(BF)
        came = yield net.move(array, target)
        array = array.astype(F32) + came.astype(F32)
    return array


def nn(a, b):
    return lax.dot_general(a, b, (((1,), (0,)), ((), ())), preferred_element_type=F32)


def nt(a, b):
    return lax.dot_general(a, b, (((1,), (1,)), ((), ())), preferred_element_type=F32)


def tn(a, b):
    return lax.dot_general(a, b, (((0,), (0,)), ((), ())), preferred_element_type=F32)


def two(a):
    high = a.astype(BF)
    return high, (a - high.astype(F32)).astype(BF)


def left_half(shape):
    return lax.broadcasted_iota(jnp.int32, shape, 1) < 64


def normed(values, gain, bias):
    mean = jnp.mean(values, axis=1, keepdims=True)
    centred = values - mean
    variance = jnp.mean(centred * centred, axis=1, keepdims=True)
    return centred * lax.rsqrt(variance + EPSILON) * gain + bias


def normed_back(values, gain, upstream):
    mean = jnp.mean(values, axis=1, keepdims=True)
    centred = values - mean
    variance = jnp.mean(centred * centred, axis=1, keepdims=True)
    scale = lax.rsqrt(variance + EPSILON)
    unit = centred * scale
    inner = upstream * gain
    grad = scale * (
        inner
        - jnp.mean(inner, axis=1, keepdims=True)
        - unit * jnp.mean(inner * unit, axis=1, keepdims=True)
    )
    return grad, jnp.sum(upstream * unit, axis=0, keepdims=True), jnp.sum(upstream, axis=0, keepdims=True)


def softmax_halves(values):
    left = left_half(values.shape)
    low = jnp.float32(-jnp.inf)
    top0 = jnp.max(jnp.where(left, values, low), axis=1, keepdims=True)
    top1 = jnp.max(jnp.where(left, low, values), axis=1, keepdims=True)
    raised = jnp.exp(values - jnp.where(left, top0, top1))
    sum0 = jnp.sum(jnp.where(left, raised, 0.0), axis=1, keepdims=True)
    sum1 = jnp.sum(jnp.where(left, 0.0, raised), axis=1, keepdims=True)
    return raised / jnp.where(left, sum0, sum1)


def softmax_halves_back(weights, upstream):
    left = left_half(weights.shape)
    product = weights * upstream
    sum0 = jnp.sum(jnp.where(left, product, 0.0), axis=1, keepdims=True)
    sum1 = jnp.sum(jnp.where(left, 0.0, product), axis=1, keepdims=True)
    return product - weights * jnp.where(left, sum0, sum1)


def lanes(ref, head):
    return ref[:, head * 128 : (head + 1) * 128]


def state_at(ref, seq, pair):
    start = pair % 3 * 128
    return ref[seq, pair // 3, start : start + 128, :]


def normaliser_at(ref, head):
    row = H // 2 * HD + head % 6
    parts = [ref[seq, head // 6, row : row + 1, :] for seq in range(2)]
    return jnp.concatenate([jnp.broadcast_to(part, (64, 128)) for part in parts], axis=0)


def store_state(ref, seq, pair, block, row):
    half = pair // 3
    start = pair % 3 * 128
    ref[seq, half, start : start + 64, :] = block[:64, :128]
    ref[seq, half, start + 64 : start + 128, :] = block[64:, 128:]
    tail = H // 2 * HD + pair % 3 * 2
    ref[seq, half, tail : tail + 1, :] = row[:, :128]
    ref[seq, half, tail + 1 : tail + 2, :] = row[:, 128:]


def clear_tail(ref):
    for seq in range(2):
        for half in range(2):
            ref[seq, half, 390:400, :] = jnp.zeros((10, 128), F32)


def head_kernel(x_ref, norm_ref, w_ref, map_ref, cols_ref, h_ref, proj_ref, fq_ref, fk_ref, state_ref):
    step = pl.program_id(0)

    @pl.when(step == 0)
    def _():
        h_ref[...] = normed(x_ref[...], norm_ref[0:1, :], norm_ref[1:2, :]).astype(BF)

    proj_ref[...] = nt(h_ref[...], w_ref[...]).astype(BF)

    def features(out_ref):
        for pair in range(PAIRS):
            part = lanes(proj_ref, pair)
            before = nn(jnp.concatenate([part, part], axis=1), map_ref[0, pair])
            for side in range(2):
                head = pair * 2 + side
                out_ref[:, head * 128 : (head + 1) * 128] = softmax_halves(
                    before[:, side * 128 : (side + 1) * 128]
                )

    @pl.when(step == 0)
    def _():
        features(fq_ref)

    @pl.when(step == 1)
    def _():
        features(fk_ref)

    @pl.when(step == 2)
    def _():
        clear_tail(state_ref)
        for seq in range(2):
            rows = slice(seq * 64, seq * 64 + 64)
            last = cols_ref[rows, 1:2]
            for pair in range(PAIRS):
                feats = fk_ref[rows, pair * 256 : (pair + 1) * 256].astype(BF).astype(F32) * last
                block = tn(proj_ref[rows, pair * 128 : (pair + 1) * 128], feats.astype(BF))
                store_state(state_ref, seq, pair, block, jnp.sum(feats, axis=0, keepdims=True))


def tail_kernel(
    x_ref, v_ref, fq_ref, fk_ref, state_ref, cols_ref, vis_ref, norm_ref, wo_ref, wu_ref, wd_ref,
    o_ref, rden_ref, att_ref, x1_ref, h2_ref, u_ref, g_ref, out_ref,
):
    @pl.when(pl.program_id(0) == 0)
    def _():
        visible = vis_ref[...]
        mark = cols_ref[:, 0:1]
        left = left_half((128, 128))
        for pair in range(PAIRS):
            value = lanes(v_ref, pair)
            nothing = jnp.zeros_like(value)
            state = [jnp.concatenate(two(state_at(state_ref, seq, pair)), axis=1) for seq in range(2)]
            weights = []
            totals = []
            carried = []
            for side in range(2):
                head = pair * 2 + side
                query = lanes(fq_ref, head).astype(BF)
                score = nt(query, lanes(fk_ref, head).astype(BF)) * visible
                weights.append(score.astype(BF))
                wide = query.astype(F32) * normaliser_at(state_ref, head) * mark
                totals.append(jnp.sum(score + wide, axis=1, keepdims=True))
                twice = jnp.concatenate([query, query], axis=1)
                carried.append(
                    jnp.concatenate([nt(twice[:64], state[0]), nt(twice[64:], state[1])], axis=0)
                )
            number = nn(
                jnp.concatenate(weights, axis=1),
                jnp.concatenate([jnp.where(left, value, nothing), jnp.where(left, nothing, value)], axis=0),
            )
            number = number + mark * jnp.where(left, carried[0], carried[1])
            inverse = 1.0 / jnp.where(left, totals[0], totals[1])
            output = number * inverse
            cut = slice(pair * 128, (pair + 1) * 128)
            o_ref[:, cut] = output
            rden_ref[:, cut] = inverse
            att_ref[:, cut] = output.astype(BF)
        x1 = x_ref[...] + nn(att_ref[...], wo_ref[...])
        x1_ref[...] = x1
        h2_ref[...] = normed(x1, norm_ref[0:1, :], norm_ref[1:2, :]).astype(BF)
        out_ref[...] = x1

    u = nt(h2_ref[...], wu_ref[...])
    u_ref[...] = u
    inner = jnp.tanh(0.7978845608028654 * (u + 0.044715 * (u * u * u)))
    g = (0.5 * u * (1.0 + inner)).astype(BF)
    g_ref[...] = g
    out_ref[...] += nn(g, wd_ref[...])


def back_kernel(
    e_ref, u_ref, x1_ref, norm_ref, wd_ref, wu_ref, wo_ref, o_ref, rden_ref, fq_ref, cols_ref,
    du_ref, dx1_ref, ebx_ref, dn_ref, dd_ref, state_ref, gn_ref, total,
):
    step = pl.program_id(0)
    dg = nt(e_ref[...].astype(BF), wd_ref[...])
    u = u_ref[...]
    inner = jnp.tanh(0.7978845608028654 * (u + 0.044715 * (u * u * u)))
    slope = 0.5 * (1.0 + inner) + (0.5 * u) * (1.0 - inner * inner) * (
        0.7978845608028654 * (1.0 + 0.134145 * (u * u))
    )
    du = (dg * slope).astype(BF)
    du_ref[...] = du
    part = nn(du, wu_ref[...])

    @pl.when(step == 0)
    def _():
        total[...] = part

    @pl.when(step > 0)
    def _():
        total[...] += part

    @pl.when(step == pl.num_programs(0) - 1)
    def _():
        grad, gain, bias = normed_back(x1_ref[...], norm_ref[0:1, :], total[...])
        gn_ref[0:1, :] = gain
        gn_ref[1:2, :] = bias
        dx1 = e_ref[...] + grad
        dx1_ref[...] = dx1
        low = dx1.astype(BF)
        ebx_ref[...] = low
        dn_ref[...] = nt(low, wo_ref[...]).astype(BF).astype(F32) * rden_ref[...]
        left = left_half((128, 128))
        lane = lax.broadcasted_iota(jnp.int32, (128, 128), 1)
        clear_tail(state_ref)
        columns = jnp.zeros((128, 128), F32)
        for pair in range(PAIRS):
            dn = lanes(dn_ref, pair)
            product = dn * lanes(o_ref, pair)
            d0 = -jnp.sum(jnp.where(left, product, 0.0), axis=1, keepdims=True)
            d1 = -jnp.sum(jnp.where(left, 0.0, product), axis=1, keepdims=True)
            columns = jnp.where(lane == pair * 2, d0, jnp.where(lane == pair * 2 + 1, d1, columns))
            for seq in range(2):
                rows = slice(seq * 64, seq * 64 + 64)
                mark = cols_ref[rows, 0:1]
                high, rest = two(dn[rows] * mark)
                feats = fq_ref[rows, pair * 256 : (pair + 1) * 256].astype(BF)
                block = tn(jnp.concatenate([high, rest], axis=0), jnp.concatenate([feats, feats], axis=0))
                wide = feats.astype(F32)
                row = jnp.concatenate(
                    [
                        jnp.sum(wide[:, :128] * (d0[rows] * mark), axis=0, keepdims=True),
                        jnp.sum(wide[:, 128:] * (d1[rows] * mark), axis=0, keepdims=True),
                    ],
                    axis=1,
                )
                store_state(state_ref, seq, pair, block, row)
        dd_ref[...] = columns


def fold_map(pair_weights, low_q):
    left = left_half((128, 128))
    folded = [weight - pltpu.roll(weight, 64, 1) for weight in pair_weights]
    grad = jnp.where(left, folded[0], pltpu.roll(folded[1], 64, 1))
    high, rest = two(grad)
    twice = jnp.concatenate([low_q, low_q], axis=0)
    table = tn(twice, jnp.concatenate([high, rest], axis=0))
    return jnp.where(left[:64], table[:64], table[64:])


def query_kernel(
    q_ref, v_ref, fq_ref, fk_ref, state_ref, dn_ref, dd_ref, cols_ref, vis_ref, map_ref,
    dq_ref, dmap_ref, dfk_ref, dv_ref,
):
    visible = vis_ref[...]
    low_visible = visible.astype(BF)
    mark = cols_ref[:, 0:1]
    left = left_half((128, 128))
    for pair in range(PAIRS):
        value = lanes(v_ref, pair)
        dn = lanes(dn_ref, pair)
        twice = jnp.concatenate([value, value], axis=1)
        state = [two(state_at(state_ref, seq, pair)) for seq in range(2)]
        weights = []
        shifts = []
        turned = []
        for side in range(2):
            head = pair * 2 + side
            wide = lanes(fq_ref, head)
            query = wide.astype(BF)
            key = lanes(fk_ref, head).astype(BF)
            score = (nt(query, key) * visible).astype(BF)
            mine = jnp.where(left, dn, 0.0) if side == 0 else jnp.where(left, 0.0, dn)
            high, rest = two(mine)
            dd = dd_ref[:, head : head + 1]
            shift = (nt(jnp.concatenate([high, rest], axis=1), twice) + dd).astype(BF) * low_visible
            carried = jnp.concatenate(
                [
                    nn(
                        jnp.concatenate([high[rows], high[rows], rest[rows]], axis=1),
                        jnp.concatenate([state[seq][0], state[seq][1], state[seq][0]], axis=0),
                    )
                    for seq, rows in ((0, slice(0, 64)), (1, slice(64, 128)))
                ],
                axis=0,
            )
            dfq = nn(shift, key) + mark * (carried + dd * normaliser_at(state_ref, head))
            dfk_ref[:, head * 128 : (head + 1) * 128] = tn(shift, query)
            weights.append(softmax_halves_back(wide, dfq))
            shifts.append(score)
            turned.append(high)
        cut = slice(pair * 128, (pair + 1) * 128)
        dv_ref[:, cut] = tn(jnp.concatenate(shifts, axis=0), jnp.concatenate(turned, axis=0))
        low = jnp.concatenate(weights, axis=1).astype(BF)
        dq_ref[:, cut] = nt(low, map_ref[0, pair, :128, :]).astype(BF)
        dmap_ref[:, cut] = fold_map(weights, lanes(q_ref, pair))


def key_kernel(
    k_ref, v_ref, fk_ref, state_ref, dfk_ref, dv_ref, dq_ref, cols_ref, map_ref, w_ref, x_ref, norm_ref, dx1_ref,
    dqkv_ref, dmap_ref, e_ref, gn_ref,
):
    last = cols_ref[:, 1:2]
    left = left_half((128, 128))
    dqkv_ref[:, :D] = dq_ref[...]
    for pair in range(PAIRS):
        value = lanes(v_ref, pair)
        nothing = jnp.zeros_like(value)
        state = [two(state_at(state_ref, seq, pair)) for seq in range(2)]
        weights = []
        grads = []
        for side in range(2):
            head = pair * 2 + side
            wide = lanes(fk_ref, head)
            key = wide.astype(BF)
            mine = jnp.where(left, value, nothing) if side == 0 else jnp.where(left, nothing, value)
            carried = []
            turned = []
            for seq, rows in ((0, slice(0, 64)), (1, slice(64, 128))):
                high, rest = state[seq]
                carried.append(
                    nn(
                        jnp.concatenate([mine[rows], mine[rows]], axis=1),
                        jnp.concatenate([high, rest], axis=0),
                    )
                )
                turned.append(nt(key[rows], high))
            carried = jnp.concatenate(carried, axis=0)
            dfk = lanes(dfk_ref, head) + last * (carried + normaliser_at(state_ref, head))
            weights.append(softmax_halves_back(wide, dfk))
            grads.append(jnp.concatenate(turned, axis=0))
        cut = slice(pair * 128, (pair + 1) * 128)
        dv = lanes(dv_ref, pair) + last * jnp.where(left, grads[0], grads[1])
        dqkv_ref[:, 2 * D + pair * 128 : 2 * D + (pair + 1) * 128] = dv.astype(BF)
        low = jnp.concatenate(weights, axis=1).astype(BF)
        dqkv_ref[:, D + pair * 128 : D + (pair + 1) * 128] = nt(low, map_ref[0, pair, :128, :]).astype(BF)
        dmap_ref[:, cut] = fold_map(weights, lanes(k_ref, pair))
    upstream = nn(dqkv_ref[...], w_ref[...])
    grad, gain, bias = normed_back(x_ref[...], norm_ref[0:1, :], upstream)
    gn_ref[0:1, :] = gain
    gn_ref[1:2, :] = bias
    e_ref[...] = dx1_ref[...] + grad


def store_sides(block, keep_ref, send_ref):
    zero = lax.rem(lax.axis_index("seq"), 2) == 0
    groups, size = keep_ref.shape[:2]
    for group in range(groups):
        low = block[group * 2 * size : group * 2 * size + size]
        high = block[group * 2 * size + size : group * 2 * size + 2 * size]
        keep_ref[group] = jnp.where(zero, low, high).astype(BF)
        send_ref[group] = jnp.where(zero, high, low).astype(BF)


def rows_kernel(att_ref, ebx_ref, du_ref, h2_ref, g_ref, e_ref, keep_ref, send_ref, held):
    terms = ((0, D, att_ref, ebx_ref), (D, D + FF, du_ref, h2_ref), (D + FF, D + 2 * FF, g_ref, e_ref))
    for step in range((D + 2 * FF) // TILE):
        start = step * TILE

        @pl.when(pl.program_id(0) == step)
        def _(start=start):
            for first, last, left, right in terms:
                low = max(start, first)
                high = min(start + TILE, last)
                if low < high:
                    held[low - start : high - start, :] = tn(
                        left[:, low - first : high - first], right[...].astype(BF)
                    )
            store_sides(held, keep_ref, send_ref)


def proj_rows_kernel(dqkv_ref, h_ref, keep_ref, send_ref, held):
    held[...] = tn(dqkv_ref[...], h_ref[...])
    store_sides(held, keep_ref, send_ref)


def split_kernel(runs, nb, *refs):
    tops = refs[2 * len(runs) : 2 * len(runs) + nb]
    bottoms = refs[2 * len(runs) + nb :]
    half = tops[0].shape[2]
    y = lax.rem(lax.axis_index("seq") // 2, 2)
    b = lax.axis_index("batch")
    start = 0
    for index, count in enumerate(runs):
        keep, came = refs[2 * index : 2 * index + 2]

        @pl.when((pl.program_id(0) >= start) & (pl.program_id(0) < start + count))
        def _(keep=keep, came=came):
            def rows(row_y, row_b, offset):
                at = pl.ds(pl.multiple_of(row_b * 2 * half + offset, 16), half)
                return (keep[row_y, at, :].astype(F32) + came[row_y, at, :].astype(F32)).astype(BF)

            for step, top in enumerate(tops):
                for side in range(2):
                    top[0, side] = rows(side, lax.rem(b + step, nb), 0)
            for step, bottom in enumerate(bottoms):
                for side in range(nb):
                    bottom[0, side] = rows(lax.rem(y + step, 2), side, half)

        start += count


def split_call(net, pairs):
    size = pairs[0][0].shape[1]
    half = size // net.nb // 2
    runs = [keep.shape[0] // 2 for keep, _ in pairs]
    planes = sum(runs)
    operands = []
    start = 0
    for pair, count in zip(pairs, runs):

        def index(i, start=start, count=count):
            return (jnp.clip(i - start, 0, count - 1), 0, 0)

        operands += [(array, (2, size, D), index) for array in pair]
        start += count
    outputs = [((planes, 2, half, D), BF, (1, 2, half, D), lambda i: (i, 0, 0, 0))] * net.nb
    outputs += [((planes, net.nb, half, D), BF, (1, net.nb, half, D), lambda i: (i, 0, 0, 0))] * 2
    parts = call(functools.partial(split_kernel, runs, net.nb), (planes,), operands, outputs, 0)
    return parts[: net.nb], parts[net.nb :]


def whole(array):
    rank = array.ndim
    return pl.BlockSpec(array.shape, lambda *_: (0,) * rank)


def call(kernel, grid, operands, outputs, flops, scratch=()):
    arrays = []
    in_specs = []
    for operand in operands:
        if isinstance(operand, tuple):
            arrays.append(operand[0])
            in_specs.append(pl.BlockSpec(operand[1], operand[2]))
        else:
            arrays.append(operand)
            in_specs.append(whole(operand))
    shapes = [jax.ShapeDtypeStruct(out[0], out[1]) for out in outputs]
    out_specs = []
    for out, shape in zip(outputs, shapes):
        out_specs.append(pl.BlockSpec(out[2], out[3]) if len(out) > 2 else whole(shape))
    moved = sum(a.size * a.dtype.itemsize for a in shapes)
    for spec, a in zip(in_specs, arrays):
        moved += a.size * a.dtype.itemsize if a.shape[0] < 6000 else 6 * D * D
    return pl.pallas_call(
        kernel,
        grid=grid,
        in_specs=in_specs,
        out_specs=out_specs,
        out_shape=shapes,
        scratch_shapes=list(scratch),
        compiler_params=pltpu.CompilerParams(vmem_limit_bytes=WIDE_LIMIT),
        cost_estimate=pl.CostEstimate(flops=flops, bytes_accessed=moved, transcendentals=0),
    )(*arrays)


STATE = (2, 2, H // 2 * HD + 16, 128)
ROWS = 128
CHUNK = D
TILE = 3 * D // 2
CHUNKS = FF // CHUNK


def still(*index):
    return lambda i: index


def head_call(x, flat, norms, maps, cols):
    return call(
        head_kernel,
        (3,),
        [
            x,
            norms[0],
            (flat[0], (D, D), lambda i: (i, 0)),
            (maps, (1, PAIRS, 256, 256), lambda i: (jnp.minimum(i, 1), 0, 0, 0)),
            cols,
        ],
        [
            ((ROWS, D), BF),
            ((ROWS, 3 * D), BF, (ROWS, D), lambda i: (0, i)),
            ((ROWS, H * 128), F32),
            ((ROWS, H * 128), F32),
            (STATE, F32),
        ],
        2 * ROWS * 3 * D * D,
    )


def tail_call(x, flat, norms, cols, visible, head, state):
    h1, proj, fq, fk, local = head
    o, rden, att, x1, h2, u, g, result = call(
        tail_kernel,
        (CHUNKS,),
        [
            x,
            (proj, (ROWS, D), still(0, 2)),
            fq,
            fk,
            state,
            cols,
            visible,
            norms[1],
            (flat[1], (D, D), still(0, 0)),
            (flat[1], (CHUNK, D), lambda i: (1 + i, 0)),
            (flat[1], (CHUNK, D), lambda i: (1 + CHUNKS + i, 0)),
        ],
        [
            ((ROWS, D), F32),
            ((ROWS, D), F32),
            ((ROWS, D), BF),
            ((ROWS, D), F32),
            ((ROWS, D), BF),
            ((ROWS, FF), F32, (ROWS, CHUNK), lambda i: (0, i)),
            ((ROWS, FF), BF, (ROWS, CHUNK), lambda i: (0, i)),
            ((ROWS, D), F32),
        ],
        2 * ROWS * 9 * D * D,
    )
    return result, (x, h1, proj, fq, fk, state, o, rden, att, x1, h2, u, g)


def back_call(e, flat, norms, cols, kept):
    x, h1, proj, fq, fk, state, o, rden, att, x1, h2, u, g = kept
    return call(
        back_kernel,
        (CHUNKS,),
        [
            e,
            (u, (ROWS, CHUNK), lambda i: (0, i)),
            x1,
            norms[1],
            (flat[1], (CHUNK, D), lambda i: (1 + CHUNKS + i, 0)),
            (flat[1], (CHUNK, D), lambda i: (1 + i, 0)),
            (flat[1], (D, D), still(0, 0)),
            o,
            rden,
            fq,
            cols,
        ],
        [
            ((ROWS, FF), BF, (ROWS, CHUNK), lambda i: (0, i)),
            ((ROWS, D), F32),
            ((ROWS, D), BF),
            ((ROWS, D), F32),
            ((ROWS, 128), F32),
            (STATE, F32),
            ((2, D), F32),
        ],
        2 * ROWS * 9 * D * D,
        [pltpu.VMEM((ROWS, D), F32)],
    )


def query_call(maps, cols, visible, kept, back):
    proj, fq, fk, state = kept[2:6]
    dn, dd = back[3:5]
    return call(
        query_kernel,
        (1,),
        [
            (proj, (ROWS, D), still(0, 0)),
            (proj, (ROWS, D), still(0, 2)),
            fq,
            fk,
            state,
            dn,
            dd,
            cols,
            visible,
            (maps, (1, PAIRS, 256, 256), still(0, 0, 0, 0)),
        ],
        [((ROWS, D), BF), ((HD, D), F32), ((ROWS, H * 128), F32), ((ROWS, D), F32)],
        2 * ROWS * 4 * D * D,
    )


def sides(net, count):
    side = (4 * D + 2 * FF) // (4 * net.nz)
    shape = (count // (2 * side), side, D)
    return [(shape, BF, (TILE // (2 * side), side, D), lambda i: (i, 0, 0))] * 2


def rows_call(net, e, kept, back):
    att, h2, g = kept[8], kept[10], kept[12]
    du, ebx = back[0], back[2]
    return call(
        rows_kernel,
        ((D + 2 * FF) // TILE,),
        [att, ebx, du, h2, g, e],
        sides(net, D + 2 * FF),
        2 * ROWS * 9 * D * D,
        [pltpu.VMEM((TILE, D), F32)],
    )


def key_call(flat, norms, maps, cols, kept, back, query, state_grad):
    x, proj, fk = kept[0], kept[2], kept[4]
    dx1 = back[1]
    dq, query_map, dfk, dv = query
    return call(
        key_kernel,
        (1,),
        [
            (proj, (ROWS, D), still(0, 1)),
            (proj, (ROWS, D), still(0, 2)),
            fk,
            state_grad,
            dfk,
            dv,
            dq,
            cols,
            (maps, (1, PAIRS, 256, 256), still(1, 0, 0, 0)),
            (flat[0], (3 * D, D), still(0, 0)),
            x,
            norms[0],
            dx1,
        ],
        [((ROWS, 3 * D), BF), ((HD, D), F32), ((ROWS, D), F32), ((2, D), F32)],
        2 * ROWS * 3 * D * D,
    )


def proj_rows_call(net, kept, dqkv):
    return call(
        proj_rows_kernel,
        (3 * D // TILE,),
        [(dqkv, (ROWS, TILE), lambda i: (0, i)), kept[1]],
        sides(net, 3 * D),
        2 * ROWS * 3 * D * D,
        [pltpu.VMEM((TILE, D), F32)],
    )


def pair_maps(fmap):
    grid = fmap.reshape(LAYERS, 2, HD, PAIRS, 2, HD).transpose(0, 1, 3, 4, 2, 5)
    both = jnp.concatenate([grid, -grid], axis=-1)
    empty = jnp.zeros_like(both[:, :, :, 0])
    top = jnp.concatenate([both[:, :, :, 0], empty], axis=-1)
    bottom = jnp.concatenate([empty, both[:, :, :, 1]], axis=-1)
    return jnp.concatenate(two(jnp.concatenate([top, bottom], axis=3)), axis=3)


def doc_layout(doc_lengths, start, span):
    ends = jnp.cumsum(doc_lengths, axis=1)
    places = start + jnp.arange(span, dtype=jnp.int32)
    documents = jnp.sum((places[None, :, None] >= ends[:, None, :]).astype(jnp.int32), axis=2)
    before = jnp.sum((start - 1 >= ends).astype(jnp.int32), axis=1)
    previous = jnp.where(start > 0, before, -1)
    mark = (documents == previous[:, None]).reshape(-1, 1)
    last = (documents == documents[:, span - 1 :]).reshape(-1, 1)
    lane = jnp.arange(128)[None, :]
    cols = jnp.where(lane == 0, mark, (lane == 1) & last).astype(F32)
    names = (documents + (DOCS + 1) * jnp.arange(documents.shape[0])[:, None]).reshape(-1)
    lower = jnp.arange(names.shape[0])[:, None] >= jnp.arange(names.shape[0])[None, :]
    visible = (lower & (names[:, None] == names[None, :])).astype(F32)
    return cols, visible


def body(tokens, doc_lengths, weights, norm_gain, norm_bias, fmap, cotangent):
    net = Net()
    sequences, span = tokens.shape[:2]
    start = lax.axis_index("seq") * span
    rows = sequences * span
    def prepare(doc_lengths, fmap, norm_gain, norm_bias, tokens, cotangent):
        cols, visible = doc_layout(doc_lengths, start, span)
        last_doc = last_docs(doc_lengths, span)
        gates = [scan_gates(net, last_doc, reverse) for reverse in (False, True)]
        maps = pair_maps(fmap)
        norms = jnp.stack([norm_gain, norm_bias], axis=2)
        x, e = [array.reshape(rows, D).astype(F32) for array in (tokens, cotangent)]
        return cols, visible, gates, maps, norms, x, e

    given = (doc_lengths, fmap, norm_gain, norm_bias, tokens, cotangent)
    steps = len(list(doublings(net.nz)))
    if net.nz == 4 and net.nb == 2 and weights.shape[1] % 32 == 0:
        first, second = [Gather(net, weights[layer]) for layer in range(LAYERS)]
        own = first.shard[None]
        next_z = [first.along_z(first.shard, step) for step in (1, 3)]
        sides = first.sides(own)
        own, sides, shard = tie(own, sides, first.shard)
        corners = first.corners(*sides)
        own, sides, corners, next_z, shard, given = tie(own, sides, corners, next_z, shard, given)
        far = first.along_z(shard, 2)[None]
        next_z = jnp.stack(next_z)
        next_sides = first.sides(next_z)
        prepared = prepare(*given)
        next_z, next_sides, far, shard = tie(next_z, next_sides, far, second.shard)
        next_corners = first.corners(*next_sides)
        far_sides = first.sides(far)
        second_z = [second.along_z(shard, step) for step in (1, 3)]
        first.add((0,), own, sides, corners)
        next_corners, far, far_sides, prepared, second_z = tie(
            next_corners, far, far_sides, prepared, second_z
        )
        cols, visible, gates, maps, norms, x, e1 = prepared
        far_corners = first.corners(*far_sides)
        first.add((1, 3), next_z, next_sides, next_corners)
        own = shard[None]
        sides = second.sides(own)
        second_z.append(second.along_z(shard, 2))
        far, far_sides, far_corners = tie(far, far_sides, far_corners)
        first.add((2,), far, far_sides, far_corners)
        head = first.rows(0, 1)
        kept0 = head_call(x, (head, None), norms[0], maps[0], cols)
        scan = scan_steps(net, kept0[4], gates[0], False)
        came = next(scan)
        came, own, sides, second_z = tie(came, own, sides, second_z)
        corners = second.corners(*sides)
        second_z = jnp.stack(second_z)
        came = scan.send(came)
        came, own, sides, corners, second_z = tie(came, own, sides, corners, second_z)
        second_sides = second.sides(second_z)
        second.add((0,), own, sides, corners)
        came = scan.send(came)
        for _ in range(1, steps):
            came = scan.send(came)
        rest = first.rows(1, net.nz)
        came, rest = tie(came, rest)
        came = scan.send(came)
        came, second_z, second_sides = tie(came, second_z, second_sides)
        second_corners = second.corners(*second_sides)
        edges = second.edges(second_z, second_sides)
        state = finish(scan, came)
        x1, kept0 = tail_call(x, (head, rest), norms[0], cols, visible, kept0, state)
        x1, second_corners, edges = tie(x1, second_corners, edges)
        points = second.points(second_corners)
        second.groups.append(((1, 3, 2), (second_z, *second_sides, *second_corners), (edges, points)))
        gathered = [(head, rest)]
        head = second.rows(0, 1)
        kept1 = head_call(x1, (head, None), norms[1], maps[1], cols)
        scan = scan_steps(net, kept1[4], gates[0], False)
        came = next(scan)
        rest = second.rows(1, net.nz)
        for _ in range(steps + 1):
            came = scan.send(came)
        came, rest = tie(came, rest)
        state = finish(scan, came)
        gathered.append((head, rest))
    else:
        gathered = [lax.all_gather(weights[layer], AXES, axis=0, tiled=True) for layer in range(LAYERS)]
        gathered = [(flat[: 3 * D], flat[3 * D :]) for flat in gathered]
        cols, visible, gates, maps, norms, x, e1 = prepare(*given)
        kept0 = head_call(x, gathered[0], norms[0], maps[0], cols)
        state = finish(scan_steps(net, kept0[4], gates[0], False), None)
        x1, kept0 = tail_call(x, gathered[0], norms[0], cols, visible, kept0, state)
        kept1 = head_call(x1, gathered[1], norms[1], maps[1], cols)
        state = finish(scan_steps(net, kept1[4], gates[0], False), None)
    x, kept1 = tail_call(x1, gathered[1], norms[1], cols, visible, kept1, state)
    result = x.astype(BF).reshape(tokens.shape)
    cut = net.nz * 3 * D // (4 * D + 2 * FF)
    rest_sum = Scatter(net, cut, net.nz)
    both_sum = Scatter(net, 0, net.nz)
    head_sum = Scatter(net, 0, cut)

    back1 = back_call(e1, gathered[1], norms[1], cols, kept1)
    scan = scan_steps(net, back1[5], gates[1], True)
    came = next(scan)
    came, held = tie(came, e1)
    came = scan.send(came)
    keep, send = rows_call(net, held, kept1, back1)
    came, keep, send, back1 = tie(came, keep, send, back1)
    came = scan.send(came)
    swapped = net.core(send)
    query1 = query_call(maps[1], cols, visible, kept1, back1)
    came, query1, keep, swapped = tie(came, query1, keep, swapped)
    for _ in range(1, len(list(doublings(net.nz)))):
        came = scan.send(came)
    tops, bottoms = rest_sum.split([(keep, swapped)])
    came, tops, bottoms = tie(came, tops, bottoms)
    came = scan.send(came)
    came, bottoms = tie(came, bottoms)
    rest1 = rest_sum.first_send((tops, bottoms))
    state_grad = finish(scan, came)
    dqkv1, key_map1, e0, norm_one1 = key_call(
        gathered[1], norms[1], maps[1], cols, kept1, back1, query1, state_grad
    )
    small1 = jnp.concatenate([query1[1], key_map1, norm_one1, back1[6]], axis=0)

    back0 = back_call(e0, gathered[0], norms[0], cols, kept0)
    back0, dqkv1 = tie(back0, dqkv1)
    scan = scan_steps(net, back0[5], gates[1], True)
    came = next(scan)
    keep1, send1 = proj_rows_call(net, kept1, dqkv1)
    came, keep1, send1, held = tie(came, keep1, send1, e0)
    came = scan.send(came)
    swapped1 = net.core(send1)
    keep0, send0 = rows_call(net, held, kept0, back0)
    came, keep0, send0, rest1 = tie(came, keep0, send0, rest1)
    came = scan.send(came)
    swapped0 = net.core(send0)
    rest1 = rest_sum.first_add(rest1)
    came, rest1, keep0, swapped0, keep1, swapped1 = tie(came, rest1, keep0, swapped0, keep1, swapped1)
    for _ in range(1, len(list(doublings(net.nz)))):
        came = scan.send(came)
    rest1 = rest_sum.second_send(rest1)
    tops, bottoms = both_sum.split([(keep1, swapped1), (keep0, swapped0)])
    came, tops, bottoms, back0, rest1 = tie(came, tops, bottoms, back0, rest1)
    came = scan.send(came)
    query0 = query_call(maps[0], cols, visible, kept0, back0)
    rest1 = rest_sum.second_add(rest1)
    came, bottoms, query0, rest1 = tie(came, bottoms, query0, rest1)
    both = both_sum.first_send((tops, bottoms))
    rest1 = rest_sum.z_halves(rest1)
    apart = next(rest1)
    state_grad = finish(scan, came)
    dqkv0, key_map0, e, norm_one0 = key_call(
        gathered[0], norms[0], maps[0], cols, kept0, back0, query0, state_grad
    )

    small0 = jnp.concatenate([query0[1], key_map0, norm_one0, back0[6]], axis=0)
    summing = sum_steps(net, jnp.stack([small0, small1]))
    small = next(summing)
    both, dqkv0 = tie(both, dqkv0)
    both = both_sum.first_add(both)
    keep, send = proj_rows_call(net, kept0, dqkv0)
    both, keep, send, apart, small = tie(both, keep, send, apart, small)
    both = both_sum.second_send(both)
    swapped = net.core(send)
    apart = rest1.send(apart)
    small = summing.send(small)
    head0 = head_sum.split([(keep, swapped)])
    head0, apart = tie(head0, apart)
    head0 = head_sum.first_send(head0)
    rest1 = finish(rest1, apart)
    both = both_sum.second_add(both)
    both, small = tie(both, small)
    both = both_sum.z_sum(both)
    head0 = head_sum.first_add(head0)
    small = summing.send(small)
    head0, small = tie(head0, small)
    head0 = head_sum.second_send(head0)
    small = summing.send(small)
    head0 = head_sum.second_add(head0)
    head0, small = tie(head0, small)
    head0 = head_sum.z_sum(head0)
    small, both = tie(summing.send(small), both)
    small = finish(summing, small)

    both = add_up(both)
    shards = [
        jnp.where(net.z < cut, add_up(head0), both),
        jnp.where(net.z < cut, both, add_up(rest1)),
    ]
    cut = 2 * HD
    return (
        result,
        e.reshape(tokens.shape),
        jnp.stack(shards),
        small[:, cut::2],
        small[:, cut + 1 :: 2],
        small[:, :cut].reshape(fmap.shape),
    )


def solution(mesh):
    in_specs = (
        P("batch", "seq", None),
        P("batch", None),
        P(None, ("seq", "batch"), None),
        P(),
        P(),
        P(),
        P("batch", "seq", None),
    )
    out_specs = (
        P("batch", "seq", None),
        P("batch", "seq", None),
        P(None, ("seq", "batch"), None),
        P(),
        P(),
        P(),
    )
    return jax.shard_map(body, mesh=mesh, in_specs=in_specs, out_specs=out_specs, check_vma=False)
```

```python
import functools

import jax
import jax.numpy as jnp
from jax import lax
from jax.experimental import pallas as pl
from jax.experimental.pallas import tpu as pltpu
from jax.sharding import PartitionSpec as P

D = 768
H = 12
HD = 64
FF = 3072
LAYERS = 2
DOCS = 4
EPSILON = 1e-05
F32 = jnp.float32
BF = jnp.bfloat16
PAIRS = H // 2
WIDE_LIMIT = 40 * 1024 * 1024


AXES = ("seq", "batch")


class Net:
    def __init__(self):
        self.nz = lax.axis_size("seq") // 4
        self.nb = lax.axis_size("batch")
        place = lax.axis_index("seq")
        self.z = place // 4
        self.y = (place // 2) % 2
        self.c = place % 2
        self.b = lax.axis_index("batch")

    def move(self, array, target):
        pairs = []
        for index in range(self.nz * 4 * self.nb):
            place = index // self.nb
            goal = target(place // 4, (place // 2) % 2, place % 2, index % self.nb)
            if goal is not None:
                z, y, c, b = goal
                pairs.append((index, ((z * 2 + y) * 2 + c) * self.nb + b))
        return lax.ppermute(array, AXES, pairs)

    def core(self, array):
        return self.move(array, lambda z, y, c, b: (z, y, 1 - c, b))

    def flip_y(self, array):
        return self.move(array, lambda z, y, c, b: (z, 1 - y, c, b))

    def turn_b(self, array, step):
        return self.move(array, lambda z, y, c, b: (z, y, c, (b + step) % self.nb))

    def shift_z(self, array, step):
        def target(z, y, c, b):
            return (z + step, y, c, b) if 0 <= z + step < self.nz else None

        return self.move(array, target)


def pick(array, index, axis=0):
    return lax.dynamic_index_in_dim(array, index, axis, False)


def last_docs(doc_lengths, span):
    ends = jnp.cumsum(doc_lengths, axis=1)

    def last_doc(block):
        found = jnp.sum(((block + 1) * span - 1 >= ends).astype(jnp.int32), axis=1)
        return jnp.where(block < 0, -1, found)

    return last_doc


def doublings(count):
    step = 1
    while step < count:
        yield step
        step *= 2


def scan_gates(net, last_doc, reverse):
    base = 4 * net.z
    first = base + 2 * net.y
    if reverse:
        pairs = [(first, first - 1), (base + 1, base - 1), (base + 3, base + 1), (first + 1, first)]
        for step in doublings(net.nz):
            pairs += [(4 * (net.z + step) - 1, base + 3), (4 * (net.z + step) - 1, base - 1)]
    else:
        pairs = [(first, first + 1), (base + 1, base + 3), (base - 1, base + 1), (first - 1, first)]
        for step in doublings(net.nz):
            pairs += [(4 * (net.z - step) + 3, base - 1), (4 * (net.z - step) + 3, base + 3)]
    same = jnp.stack([last_doc(a) == last_doc(b) for a, b in pairs])
    return pick(same, net.c, 1).astype(F32)


def scan_steps(net, packed, gates, reverse):
    wide = F32
    low = F32
    mine = pick(packed, net.c)
    theirs = yield net.core(pick(packed, 1 - net.c))
    zero = jnp.equal(net.c, 0)
    part0 = jnp.where(zero, mine, theirs).astype(wide)
    part1 = jnp.where(zero, theirs, mine).astype(wide)
    if reverse:
        chip = part0 + gates[0] * part1
    else:
        chip = gates[0] * part0 + part1
    chip = chip.astype(low)
    own = pick(chip, net.y)
    other = yield net.flip_y(pick(chip, 1 - net.y))
    down = jnp.equal(net.y, 0)
    row0 = jnp.where(down, own, other).astype(wide)
    row1 = jnp.where(down, other, own).astype(wide)
    if reverse:
        plane = row0 + gates[1] * row1
    else:
        plane = gates[1] * row0 + row1
    entering = jnp.zeros(plane.shape, wide)
    for index, step in enumerate(doublings(net.nz)):
        part = yield net.shift_z(plane, -step if reverse else step)
        entering = entering + gates[4 + 2 * index] * part
        plane = plane + gates[5 + 2 * index] * part
    if reverse:
        row1_in = entering
        row0_in = gates[2] * entering + row1
    else:
        row0_in = entering
        row1_in = gates[2] * entering + row0
    own_in = jnp.where(down, row0_in, row1_in)
    other_in = yield net.flip_y(jnp.where(down, row1_in, row0_in).astype(low))
    other_in = other_in.astype(wide)
    chip_in = jnp.where(down, jnp.stack([own_in, other_in]), jnp.stack([other_in, own_in]))
    if reverse:
        core1_in = chip_in
        core0_in = gates[3] * chip_in + part1
    else:
        core0_in = chip_in
        core1_in = gates[3] * chip_in + part0
    core0_in = core0_in.astype(low)
    core1_in = core1_in.astype(low)
    kept = jnp.where(zero, core0_in, core1_in)
    sent = yield net.core(jnp.where(zero, core1_in, core0_in))
    return jnp.where(zero, jnp.stack([kept, sent]), jnp.stack([sent, kept]))


def finish(steps, value):
    while True:
        try:
            value = steps.send(value)
        except StopIteration as stop:
            return stop.value


def after(value, *conditions):
    return lax.optimization_barrier((value, conditions))[0]


def tie(*groups):
    return lax.optimization_barrier(groups)


class Gather:
    def __init__(self, net, shard):
        self.net = net
        self.shard = shard
        self.groups = []

    def along_z(self, shard, step):
        return self.net.move(shard, lambda z, y, c, b: ((z + step) % self.net.nz, y, c, b))

    def sides(self, blocks):
        return self.net.turn_b(blocks, 1), self.net.flip_y(blocks)

    def corners(self, over_b, over_y):
        half = over_b.shape[1] // 2
        return self.net.flip_y(over_b[:, :half]), self.net.turn_b(over_y[:, half:], 1)

    def add(self, steps, blocks, sides, corners):
        self.groups.append((steps, (blocks, *sides, *corners), (self.edges(blocks, sides), self.points(corners))))

    def edges(self, blocks, sides):
        return self.net.core(jnp.concatenate([blocks, *sides], axis=0))

    def points(self, corners):
        return self.net.core(jnp.concatenate(corners, axis=1))

    def rows(self, first, last):
        net = self.net
        size = self.shard.shape[0]
        arrays = []
        for _, mine, other in self.groups:
            arrays += [*mine, *other]
        steps = [group[0] for group in self.groups]
        blocks = (last - first) * 4 * net.nb
        return pl.pallas_call(
            functools.partial(place_kernel, steps, first, last, size),
            in_specs=[pl.BlockSpec(memory_space=pl.ANY)] * len(arrays),
            out_specs=pl.BlockSpec(memory_space=pl.ANY),
            out_shape=jax.ShapeDtypeStruct((blocks * size, D), BF),
            scratch_shapes=[
                pltpu.VMEM((blocks * size, D), BF),
                pltpu.SemaphoreType.DMA((last - first, 10)),
                pltpu.SemaphoreType.DMA((last - first,)),
            ],
            compiler_params=pltpu.CompilerParams(vmem_limit_bytes=60 * 1024 * 1024),
            cost_estimate=pl.CostEstimate(flops=0, bytes_accessed=blocks * size * D * 4, transcendentals=0),
        )(*arrays)


def place_kernel(steps, first, last, size, *refs):
    arrays, (out, held, in_sems, out_sems) = refs[:-4], refs[-4:]
    place = lax.axis_index("seq")
    z = place // 4
    y = lax.rem(place // 2, 2)
    c = lax.rem(place, 2)
    b = lax.axis_index("batch")
    half = size // 2
    plane_rows = 8 * size

    def copies(plane, group, index):
        mine = arrays[7 * group : 7 * group + 5]
        edges, points = arrays[7 * group + 5 : 7 * group + 7]
        count = len(steps[group])
        spots = ((0, 0, 0), (0, 1, 0), (1, 0, 0), (1, 1, 0), (1, 1, half))
        parts = [(array.at[index], spot, 0) for array, spot in zip(mine, spots)]
        parts += [(edges.at[count * slot + index], spots[slot], 1) for slot in range(3)]
        parts.append((points.at[index], spots[3], 1))
        made = []
        for number, (source, (dy, db, offset), dc) in enumerate(parts):
            row = (lax.rem(y + dy, 2) * 2 + lax.rem(c + dc, 2)) * 2 + lax.rem(b + db, 2)
            start = pl.multiple_of((plane - first) * plane_rows + row * size + offset, 16)
            target = held.at[pl.ds(start, source.shape[0])]
            made.append(pltpu.make_async_copy(source, target, in_sems.at[plane - first, number]))
        return made

    def each(plane, act):
        for group, kinds in enumerate(steps):
            for index, step in enumerate(kinds):

                @pl.when(lax.rem(z - plane + 4, 4) == step)
                def _(group=group, index=index):
                    for copy in copies(plane, group, index):
                        act(copy)

    def output(plane):
        rows = pl.ds((plane - first) * plane_rows, plane_rows)
        return pltpu.make_async_copy(held.at[rows], out.at[rows], out_sems.at[plane - first])

    for plane in range(first, last):
        each(plane, lambda copy: copy.start())
    for plane in range(first, last):
        each(plane, lambda copy: copy.wait())
        output(plane).start()
    for plane in range(first, last):
        output(plane).wait()


class Scatter:
    def __init__(self, net, first, last):
        self.net = net
        self.first = first
        self.last = last

    def split(self, pairs):
        net = self.net
        if (pairs[0][0].shape[1] // net.nb) % 32 == 0:
            return split_call(net, pairs)
        total = jnp.concatenate([(a.astype(F32) + b.astype(F32)).astype(BF) for a, b in pairs], axis=0)
        total = total.reshape(self.last - self.first, 2, net.nb, -1, D)
        half = total.shape[3] // 2
        top = total[:, :, :, :half]
        bottom = total[:, :, :, half:]
        return (
            [pick(top, (net.b + step) % net.nb, 2) for step in range(net.nb)],
            [pick(bottom, net.y, 1), pick(bottom, 1 - net.y, 1)],
        )

    def send_b(self, parts):
        return [parts[0]] + [self.net.turn_b(parts[step], step) for step in range(1, self.net.nb)]

    def send_y(self, parts):
        return [parts[0], self.net.flip_y(parts[1])]

    def first_send(self, buffers):
        return self.send_b(buffers[0]), self.send_y(buffers[1])

    def first_add(self, came):
        net = self.net
        top = add_up(came[0]).astype(BF)
        bottom = add_up(came[1]).astype(BF)
        return (
            [pick(top, net.y, 1), pick(top, 1 - net.y, 1)],
            [pick(bottom, (net.b + step) % net.nb, 1) for step in range(net.nb)],
        )

    def second_send(self, buffers):
        return self.send_y(buffers[0]), self.send_b(buffers[1])

    def second_add(self, came):
        return jnp.concatenate([add_up(part).astype(BF) for part in came], axis=1)

    def z_send(self, rows, steps):
        net = self.net
        limit = self.last - self.first - 1
        came = []
        for step in steps:
            part = pick(rows, jnp.clip((net.z + step) % net.nz - self.first, 0, limit))

            def target(z, y, c, b, step=step):
                goal = (z + step) % net.nz
                return (goal, y, c, b) if self.first <= goal < self.last else None

            came.append(net.move(part, target) if step else part)
        return came

    def z_halves(self, rows):
        net = self.net
        empty = [jnp.zeros((count,) + rows.shape[1:], BF) for count in (self.first, net.nz - self.last)]
        rows = jnp.concatenate([empty[0], rows, empty[1]], axis=0)
        step = net.nz // 2
        while step:
            upper = (net.z // step) % 2
            halves = rows.reshape((2, step) + rows.shape[1:])
            kept = pick(halves, upper)
            came = yield net.move(pick(halves, 1 - upper), lambda z, y, c, b, step=step: (z ^ step, y, c, b))
            rows = (kept.astype(F32) + came.astype(F32)).astype(BF)
            step //= 2
        return [rows[0]]

    def z_tree(self, rows):
        total = rows[0]
        for step in doublings(self.net.nz):

            def target(z, y, c, b, step=step):
                far = (z - self.first) % self.net.nz
                return ((z - step) % self.net.nz, y, c, b) if far % (2 * step) == step else None

            came = yield self.net.move(total, target)
            total = (total.astype(F32) + came.astype(F32)).astype(BF)
        return [total]

    def z_sum(self, rows):
        half = self.net.nz // 2
        came = yield self.z_send(rows, [half])
        rest = yield self.z_send(rows, [step for step in range(1, self.net.nz) if step != half])
        return came + rest + self.z_send(rows, [0])


def add_up(parts):
    return sum(part.astype(F32) for part in parts)


def sum_steps(net, array):
    targets = []
    for step in doublings(net.nz):
        targets.append(lambda z, y, c, b, step=step: (z ^ step, y, c, b))
    for step in doublings(net.nb):
        targets.append(lambda z, y, c, b, step=step: (z, y, c, b ^ step))
    targets.append(lambda z, y, c, b: (z, y, 1 - c, b))
    targets.append(lambda z, y, c, b: (z, 1 - y, c, b))
    for target in targets:
        array = array.astype(BF)
        came = yield net.move(array, target)
        array = array.astype(F32) + came.astype(F32)
    return array


def nn(a, b):
    return lax.dot_general(a, b, (((1,), (0,)), ((), ())), preferred_element_type=F32)


def nt(a, b):
    return lax.dot_general(a, b, (((1,), (1,)), ((), ())), preferred_element_type=F32)


def tn(a, b):
    return lax.dot_general(a, b, (((0,), (0,)), ((), ())), preferred_element_type=F32)


def two(a):
    high = a.astype(BF)
    return high, (a - high.astype(F32)).astype(BF)


def left_half(shape):
    return lax.broadcasted_iota(jnp.int32, shape, 1) < 64


def normed(values, gain, bias):
    mean = jnp.mean(values, axis=1, keepdims=True)
    centred = values - mean
    variance = jnp.mean(centred * centred, axis=1, keepdims=True)
    return centred * lax.rsqrt(variance + EPSILON) * gain + bias


def normed_back(values, gain, upstream):
    mean = jnp.mean(values, axis=1, keepdims=True)
    centred = values - mean
    variance = jnp.mean(centred * centred, axis=1, keepdims=True)
    scale = lax.rsqrt(variance + EPSILON)
    unit = centred * scale
    inner = upstream * gain
    grad = scale * (
        inner
        - jnp.mean(inner, axis=1, keepdims=True)
        - unit * jnp.mean(inner * unit, axis=1, keepdims=True)
    )
    return grad, jnp.sum(upstream * unit, axis=0, keepdims=True), jnp.sum(upstream, axis=0, keepdims=True)


def softmax_halves(values):
    left = left_half(values.shape)
    low = jnp.float32(-jnp.inf)
    top0 = jnp.max(jnp.where(left, values, low), axis=1, keepdims=True)
    top1 = jnp.max(jnp.where(left, low, values), axis=1, keepdims=True)
    raised = jnp.exp(values - jnp.where(left, top0, top1))
    sum0 = jnp.sum(jnp.where(left, raised, 0.0), axis=1, keepdims=True)
    sum1 = jnp.sum(jnp.where(left, 0.0, raised), axis=1, keepdims=True)
    return raised / jnp.where(left, sum0, sum1)


def softmax_halves_back(weights, upstream):
    left = left_half(weights.shape)
    product = weights * upstream
    sum0 = jnp.sum(jnp.where(left, product, 0.0), axis=1, keepdims=True)
    sum1 = jnp.sum(jnp.where(left, 0.0, product), axis=1, keepdims=True)
    return product - weights * jnp.where(left, sum0, sum1)


def lanes(ref, head):
    return ref[:, head * 128 : (head + 1) * 128]


def state_at(ref, seq, pair):
    start = pair % 3 * 128
    return ref[seq, pair // 3, start : start + 128, :]


def normaliser_at(ref, head):
    row = H // 2 * HD + head % 6
    parts = [ref[seq, head // 6, row : row + 1, :] for seq in range(2)]
    return jnp.concatenate([jnp.broadcast_to(part, (64, 128)) for part in parts], axis=0)


def store_state(ref, seq, pair, block, row):
    half = pair // 3
    start = pair % 3 * 128
    ref[seq, half, start : start + 64, :] = block[:64, :128]
    ref[seq, half, start + 64 : start + 128, :] = block[64:, 128:]
    tail = H // 2 * HD + pair % 3 * 2
    ref[seq, half, tail : tail + 1, :] = row[:, :128]
    ref[seq, half, tail + 1 : tail + 2, :] = row[:, 128:]


def clear_tail(ref):
    for seq in range(2):
        for half in range(2):
            ref[seq, half, 390:400, :] = jnp.zeros((10, 128), F32)


def head_kernel(x_ref, norm_ref, w_ref, map_ref, cols_ref, h_ref, proj_ref, fq_ref, fk_ref, state_ref):
    step = pl.program_id(0)

    @pl.when(step == 0)
    def _():
        h_ref[...] = normed(x_ref[...], norm_ref[0:1, :], norm_ref[1:2, :]).astype(BF)

    proj_ref[...] = nt(h_ref[...], w_ref[...]).astype(BF)

    def features(out_ref):
        for pair in range(PAIRS):
            part = lanes(proj_ref, pair)
            before = nn(jnp.concatenate([part, part], axis=1), map_ref[0, pair])
            for side in range(2):
                head = pair * 2 + side
                out_ref[:, head * 128 : (head + 1) * 128] = softmax_halves(
                    before[:, side * 128 : (side + 1) * 128]
                )

    @pl.when(step == 0)
    def _():
        features(fq_ref)

    @pl.when(step == 1)
    def _():
        features(fk_ref)

    @pl.when(step == 2)
    def _():
        clear_tail(state_ref)
        for seq in range(2):
            rows = slice(seq * 64, seq * 64 + 64)
            last = cols_ref[rows, 1:2]
            for pair in range(PAIRS):
                feats = fk_ref[rows, pair * 256 : (pair + 1) * 256].astype(BF).astype(F32) * last
                block = tn(proj_ref[rows, pair * 128 : (pair + 1) * 128], feats.astype(BF))
                store_state(state_ref, seq, pair, block, jnp.sum(feats, axis=0, keepdims=True))


def tail_kernel(
    x_ref, v_ref, fq_ref, fk_ref, state_ref, cols_ref, vis_ref, norm_ref, wo_ref, wu_ref, wd_ref,
    o_ref, rden_ref, att_ref, x1_ref, h2_ref, u_ref, g_ref, out_ref,
):
    @pl.when(pl.program_id(0) == 0)
    def _():
        visible = vis_ref[...]
        mark = cols_ref[:, 0:1]
        left = left_half((128, 128))
        for pair in range(PAIRS):
            value = lanes(v_ref, pair)
            nothing = jnp.zeros_like(value)
            state = [jnp.concatenate(two(state_at(state_ref, seq, pair)), axis=1) for seq in range(2)]
            weights = []
            totals = []
            carried = []
            for side in range(2):
                head = pair * 2 + side
                query = lanes(fq_ref, head).astype(BF)
                score = nt(query, lanes(fk_ref, head).astype(BF)) * visible
                weights.append(score.astype(BF))
                wide = query.astype(F32) * normaliser_at(state_ref, head) * mark
                totals.append(jnp.sum(score + wide, axis=1, keepdims=True))
                twice = jnp.concatenate([query, query], axis=1)
                carried.append(
                    jnp.concatenate([nt(twice[:64], state[0]), nt(twice[64:], state[1])], axis=0)
                )
            number = nn(
                jnp.concatenate(weights, axis=1),
                jnp.concatenate([jnp.where(left, value, nothing), jnp.where(left, nothing, value)], axis=0),
            )
            number = number + mark * jnp.where(left, carried[0], carried[1])
            inverse = 1.0 / jnp.where(left, totals[0], totals[1])
            output = number * inverse
            cut = slice(pair * 128, (pair + 1) * 128)
            o_ref[:, cut] = output
            rden_ref[:, cut] = inverse
            att_ref[:, cut] = output.astype(BF)
        x1 = x_ref[...] + nn(att_ref[...], wo_ref[...])
        x1_ref[...] = x1
        h2_ref[...] = normed(x1, norm_ref[0:1, :], norm_ref[1:2, :]).astype(BF)
        out_ref[...] = x1

    u = nt(h2_ref[...], wu_ref[...])
    u_ref[...] = u
    inner = jnp.tanh(0.7978845608028654 * (u + 0.044715 * (u * u * u)))
    g = (0.5 * u * (1.0 + inner)).astype(BF)
    g_ref[...] = g
    out_ref[...] += nn(g, wd_ref[...])


def back_kernel(
    e_ref, u_ref, x1_ref, norm_ref, wd_ref, wu_ref, wo_ref, o_ref, rden_ref, fq_ref, cols_ref,
    du_ref, dx1_ref, ebx_ref, dn_ref, dd_ref, state_ref, gn_ref, total,
):
    step = pl.program_id(0)
    dg = nt(e_ref[...].astype(BF), wd_ref[...])
    u = u_ref[...]
    inner = jnp.tanh(0.7978845608028654 * (u + 0.044715 * (u * u * u)))
    slope = 0.5 * (1.0 + inner) + (0.5 * u) * (1.0 - inner * inner) * (
        0.7978845608028654 * (1.0 + 0.134145 * (u * u))
    )
    du = (dg * slope).astype(BF)
    du_ref[...] = du
    part = nn(du, wu_ref[...])

    @pl.when(step == 0)
    def _():
        total[...] = part

    @pl.when(step > 0)
    def _():
        total[...] += part

    @pl.when(step == pl.num_programs(0) - 1)
    def _():
        grad, gain, bias = normed_back(x1_ref[...], norm_ref[0:1, :], total[...])
        gn_ref[0:1, :] = gain
        gn_ref[1:2, :] = bias
        dx1 = e_ref[...] + grad
        dx1_ref[...] = dx1
        low = dx1.astype(BF)
        ebx_ref[...] = low
        dn_ref[...] = nt(low, wo_ref[...]).astype(BF).astype(F32) * rden_ref[...]
        left = left_half((128, 128))
        lane = lax.broadcasted_iota(jnp.int32, (128, 128), 1)
        clear_tail(state_ref)
        columns = jnp.zeros((128, 128), F32)
        for pair in range(PAIRS):
            dn = lanes(dn_ref, pair)
            product = dn * lanes(o_ref, pair)
            d0 = -jnp.sum(jnp.where(left, product, 0.0), axis=1, keepdims=True)
            d1 = -jnp.sum(jnp.where(left, 0.0, product), axis=1, keepdims=True)
            columns = jnp.where(lane == pair * 2, d0, jnp.where(lane == pair * 2 + 1, d1, columns))
            for seq in range(2):
                rows = slice(seq * 64, seq * 64 + 64)
                mark = cols_ref[rows, 0:1]
                high, rest = two(dn[rows] * mark)
                feats = fq_ref[rows, pair * 256 : (pair + 1) * 256].astype(BF)
                block = tn(jnp.concatenate([high, rest], axis=0), jnp.concatenate([feats, feats], axis=0))
                wide = feats.astype(F32)
                row = jnp.concatenate(
                    [
                        jnp.sum(wide[:, :128] * (d0[rows] * mark), axis=0, keepdims=True),
                        jnp.sum(wide[:, 128:] * (d1[rows] * mark), axis=0, keepdims=True),
                    ],
                    axis=1,
                )
                store_state(state_ref, seq, pair, block, row)
        dd_ref[...] = columns


def fold_map(pair_weights, low_q):
    left = left_half((128, 128))
    folded = [weight - pltpu.roll(weight, 64, 1) for weight in pair_weights]
    grad = jnp.where(left, folded[0], pltpu.roll(folded[1], 64, 1))
    high, rest = two(grad)
    twice = jnp.concatenate([low_q, low_q], axis=0)
    table = tn(twice, jnp.concatenate([high, rest], axis=0))
    return jnp.where(left[:64], table[:64], table[64:])


def query_kernel(
    q_ref, v_ref, fq_ref, fk_ref, state_ref, dn_ref, dd_ref, cols_ref, vis_ref, map_ref,
    dq_ref, dmap_ref, dfk_ref, dv_ref,
):
    visible = vis_ref[...]
    low_visible = visible.astype(BF)
    mark = cols_ref[:, 0:1]
    left = left_half((128, 128))
    for pair in range(PAIRS):
        value = lanes(v_ref, pair)
        dn = lanes(dn_ref, pair)
        twice = jnp.concatenate([value, value], axis=1)
        state = [two(state_at(state_ref, seq, pair)) for seq in range(2)]
        weights = []
        shifts = []
        turned = []
        for side in range(2):
            head = pair * 2 + side
            wide = lanes(fq_ref, head)
            query = wide.astype(BF)
            key = lanes(fk_ref, head).astype(BF)
            score = (nt(query, key) * visible).astype(BF)
            mine = jnp.where(left, dn, 0.0) if side == 0 else jnp.where(left, 0.0, dn)
            high, rest = two(mine)
            dd = dd_ref[:, head : head + 1]
            shift = (nt(jnp.concatenate([high, rest], axis=1), twice) + dd).astype(BF) * low_visible
            carried = jnp.concatenate(
                [
                    nn(
                        jnp.concatenate([high[rows], high[rows], rest[rows]], axis=1),
                        jnp.concatenate([state[seq][0], state[seq][1], state[seq][0]], axis=0),
                    )
                    for seq, rows in ((0, slice(0, 64)), (1, slice(64, 128)))
                ],
                axis=0,
            )
            dfq = nn(shift, key) + mark * (carried + dd * normaliser_at(state_ref, head))
            dfk_ref[:, head * 128 : (head + 1) * 128] = tn(shift, query)
            weights.append(softmax_halves_back(wide, dfq))
            shifts.append(score)
            turned.append(high)
        cut = slice(pair * 128, (pair + 1) * 128)
        dv_ref[:, cut] = tn(jnp.concatenate(shifts, axis=0), jnp.concatenate(turned, axis=0))
        low = jnp.concatenate(weights, axis=1).astype(BF)
        dq_ref[:, cut] = nt(low, map_ref[0, pair, :128, :]).astype(BF)
        dmap_ref[:, cut] = fold_map(weights, lanes(q_ref, pair))


def key_kernel(
    k_ref, v_ref, fk_ref, state_ref, dfk_ref, dv_ref, dq_ref, cols_ref, map_ref, w_ref, x_ref, norm_ref, dx1_ref,
    dqkv_ref, dmap_ref, e_ref, gn_ref,
):
    last = cols_ref[:, 1:2]
    left = left_half((128, 128))
    dqkv_ref[:, :D] = dq_ref[...]
    for pair in range(PAIRS):
        value = lanes(v_ref, pair)
        nothing = jnp.zeros_like(value)
        state = [two(state_at(state_ref, seq, pair)) for seq in range(2)]
        weights = []
        grads = []
        for side in range(2):
            head = pair * 2 + side
            wide = lanes(fk_ref, head)
            key = wide.astype(BF)
            mine = jnp.where(left, value, nothing) if side == 0 else jnp.where(left, nothing, value)
            carried = []
            turned = []
            for seq, rows in ((0, slice(0, 64)), (1, slice(64, 128))):
                high, rest = state[seq]
                carried.append(
                    nn(
                        jnp.concatenate([mine[rows], mine[rows]], axis=1),
                        jnp.concatenate([high, rest], axis=0),
                    )
                )
                turned.append(nt(key[rows], high))
            carried = jnp.concatenate(carried, axis=0)
            dfk = lanes(dfk_ref, head) + last * (carried + normaliser_at(state_ref, head))
            weights.append(softmax_halves_back(wide, dfk))
            grads.append(jnp.concatenate(turned, axis=0))
        cut = slice(pair * 128, (pair + 1) * 128)
        dv = lanes(dv_ref, pair) + last * jnp.where(left, grads[0], grads[1])
        dqkv_ref[:, 2 * D + pair * 128 : 2 * D + (pair + 1) * 128] = dv.astype(BF)
        low = jnp.concatenate(weights, axis=1).astype(BF)
        dqkv_ref[:, D + pair * 128 : D + (pair + 1) * 128] = nt(low, map_ref[0, pair, :128, :]).astype(BF)
        dmap_ref[:, cut] = fold_map(weights, lanes(k_ref, pair))
    upstream = nn(dqkv_ref[...], w_ref[...])
    grad, gain, bias = normed_back(x_ref[...], norm_ref[0:1, :], upstream)
    gn_ref[0:1, :] = gain
    gn_ref[1:2, :] = bias
    e_ref[...] = dx1_ref[...] + grad


def store_sides(block, keep_ref, send_ref):
    zero = lax.rem(lax.axis_index("seq"), 2) == 0
    groups, size = keep_ref.shape[:2]
    for group in range(groups):
        low = block[group * 2 * size : group * 2 * size + size]
        high = block[group * 2 * size + size : group * 2 * size + 2 * size]
        keep_ref[group] = jnp.where(zero, low, high).astype(BF)
        send_ref[group] = jnp.where(zero, high, low).astype(BF)


def rows_kernel(att_ref, ebx_ref, du_ref, h2_ref, g_ref, e_ref, keep_ref, send_ref, held):
    terms = ((0, D, att_ref, ebx_ref), (D, D + FF, du_ref, h2_ref), (D + FF, D + 2 * FF, g_ref, e_ref))
    for step in range((D + 2 * FF) // TILE):
        start = step * TILE

        @pl.when(pl.program_id(0) == step)
        def _(start=start):
            for first, last, left, right in terms:
                low = max(start, first)
                high = min(start + TILE, last)
                if low < high:
                    held[low - start : high - start, :] = tn(
                        left[:, low - first : high - first], right[...].astype(BF)
                    )
            store_sides(held, keep_ref, send_ref)


def proj_rows_kernel(dqkv_ref, h_ref, keep_ref, send_ref, held):
    held[...] = tn(dqkv_ref[...], h_ref[...])
    store_sides(held, keep_ref, send_ref)


def split_kernel(runs, nb, *refs):
    tops = refs[2 * len(runs) : 2 * len(runs) + nb]
    bottoms = refs[2 * len(runs) + nb :]
    half = tops[0].shape[2]
    y = lax.rem(lax.axis_index("seq") // 2, 2)
    b = lax.axis_index("batch")
    start = 0
    for index, count in enumerate(runs):
        keep, came = refs[2 * index : 2 * index + 2]

        @pl.when((pl.program_id(0) >= start) & (pl.program_id(0) < start + count))
        def _(keep=keep, came=came):
            def rows(row_y, row_b, offset):
                at = pl.ds(pl.multiple_of(row_b * 2 * half + offset, 16), half)
                return (keep[row_y, at, :].astype(F32) + came[row_y, at, :].astype(F32)).astype(BF)

            for step, top in enumerate(tops):
                for side in range(2):
                    top[0, side] = rows(side, lax.rem(b + step, nb), 0)
            for step, bottom in enumerate(bottoms):
                for side in range(nb):
                    bottom[0, side] = rows(lax.rem(y + step, 2), side, half)

        start += count


def split_call(net, pairs):
    size = pairs[0][0].shape[1]
    half = size // net.nb // 2
    runs = [keep.shape[0] // 2 for keep, _ in pairs]
    planes = sum(runs)
    operands = []
    start = 0
    for pair, count in zip(pairs, runs):

        def index(i, start=start, count=count):
            return (jnp.clip(i - start, 0, count - 1), 0, 0)

        operands += [(array, (2, size, D), index) for array in pair]
        start += count
    outputs = [((planes, 2, half, D), BF, (1, 2, half, D), lambda i: (i, 0, 0, 0))] * net.nb
    outputs += [((planes, net.nb, half, D), BF, (1, net.nb, half, D), lambda i: (i, 0, 0, 0))] * 2
    parts = call(functools.partial(split_kernel, runs, net.nb), (planes,), operands, outputs, 0)
    return parts[: net.nb], parts[net.nb :]


def whole(array):
    rank = array.ndim
    return pl.BlockSpec(array.shape, lambda *_: (0,) * rank)


def call(kernel, grid, operands, outputs, flops, scratch=()):
    arrays = []
    in_specs = []
    for operand in operands:
        if isinstance(operand, tuple):
            arrays.append(operand[0])
            in_specs.append(pl.BlockSpec(operand[1], operand[2]))
        else:
            arrays.append(operand)
            in_specs.append(whole(operand))
    shapes = [jax.ShapeDtypeStruct(out[0], out[1]) for out in outputs]
    out_specs = []
    for out, shape in zip(outputs, shapes):
        out_specs.append(pl.BlockSpec(out[2], out[3]) if len(out) > 2 else whole(shape))
    moved = sum(a.size * a.dtype.itemsize for a in shapes)
    for spec, a in zip(in_specs, arrays):
        moved += a.size * a.dtype.itemsize if a.shape[0] < 6000 else 6 * D * D
    return pl.pallas_call(
        kernel,
        grid=grid,
        in_specs=in_specs,
        out_specs=out_specs,
        out_shape=shapes,
        scratch_shapes=list(scratch),
        compiler_params=pltpu.CompilerParams(vmem_limit_bytes=WIDE_LIMIT),
        cost_estimate=pl.CostEstimate(flops=flops, bytes_accessed=moved, transcendentals=0),
    )(*arrays)


STATE = (2, 2, H // 2 * HD + 16, 128)
ROWS = 128
CHUNK = D
TILE = 3 * D // 2
CHUNKS = FF // CHUNK


def still(*index):
    return lambda i: index


def head_call(x, flat, norms, maps, cols):
    return call(
        head_kernel,
        (3,),
        [
            x,
            norms[0],
            (flat[0], (D, D), lambda i: (i, 0)),
            (maps, (1, PAIRS, 256, 256), lambda i: (jnp.minimum(i, 1), 0, 0, 0)),
            cols,
        ],
        [
            ((ROWS, D), BF),
            ((ROWS, 3 * D), BF, (ROWS, D), lambda i: (0, i)),
            ((ROWS, H * 128), F32),
            ((ROWS, H * 128), F32),
            (STATE, F32),
        ],
        2 * ROWS * 3 * D * D,
    )


def tail_call(x, flat, norms, cols, visible, head, state):
    h1, proj, fq, fk, local = head
    o, rden, att, x1, h2, u, g, result = call(
        tail_kernel,
        (CHUNKS,),
        [
            x,
            (proj, (ROWS, D), still(0, 2)),
            fq,
            fk,
            state,
            cols,
            visible,
            norms[1],
            (flat[1], (D, D), still(0, 0)),
            (flat[1], (CHUNK, D), lambda i: (1 + i, 0)),
            (flat[1], (CHUNK, D), lambda i: (1 + CHUNKS + i, 0)),
        ],
        [
            ((ROWS, D), F32),
            ((ROWS, D), F32),
            ((ROWS, D), BF),
            ((ROWS, D), F32),
            ((ROWS, D), BF),
            ((ROWS, FF), F32, (ROWS, CHUNK), lambda i: (0, i)),
            ((ROWS, FF), BF, (ROWS, CHUNK), lambda i: (0, i)),
            ((ROWS, D), F32),
        ],
        2 * ROWS * 9 * D * D,
    )
    return result, (x, h1, proj, fq, fk, state, o, rden, att, x1, h2, u, g)


def back_call(e, flat, norms, cols, kept):
    x, h1, proj, fq, fk, state, o, rden, att, x1, h2, u, g = kept
    return call(
        back_kernel,
        (CHUNKS,),
        [
            e,
            (u, (ROWS, CHUNK), lambda i: (0, i)),
            x1,
            norms[1],
            (flat[1], (CHUNK, D), lambda i: (1 + CHUNKS + i, 0)),
            (flat[1], (CHUNK, D), lambda i: (1 + i, 0)),
            (flat[1], (D, D), still(0, 0)),
            o,
            rden,
            fq,
            cols,
        ],
        [
            ((ROWS, FF), BF, (ROWS, CHUNK), lambda i: (0, i)),
            ((ROWS, D), F32),
            ((ROWS, D), BF),
            ((ROWS, D), F32),
            ((ROWS, 128), F32),
            (STATE, F32),
            ((2, D), F32),
        ],
        2 * ROWS * 9 * D * D,
        [pltpu.VMEM((ROWS, D), F32)],
    )


def query_call(maps, cols, visible, kept, back):
    proj, fq, fk, state = kept[2:6]
    dn, dd = back[3:5]
    return call(
        query_kernel,
        (1,),
        [
            (proj, (ROWS, D), still(0, 0)),
            (proj, (ROWS, D), still(0, 2)),
            fq,
            fk,
            state,
            dn,
            dd,
            cols,
            visible,
            (maps, (1, PAIRS, 256, 256), still(0, 0, 0, 0)),
        ],
        [((ROWS, D), BF), ((HD, D), F32), ((ROWS, H * 128), F32), ((ROWS, D), F32)],
        2 * ROWS * 4 * D * D,
    )


def sides(net, count):
    side = (4 * D + 2 * FF) // (4 * net.nz)
    shape = (count // (2 * side), side, D)
    return [(shape, BF, (TILE // (2 * side), side, D), lambda i: (i, 0, 0))] * 2


def rows_call(net, e, kept, back):
    att, h2, g = kept[8], kept[10], kept[12]
    du, ebx = back[0], back[2]
    return call(
        rows_kernel,
        ((D + 2 * FF) // TILE,),
        [att, ebx, du, h2, g, e],
        sides(net, D + 2 * FF),
        2 * ROWS * 9 * D * D,
        [pltpu.VMEM((TILE, D), F32)],
    )


def key_call(flat, norms, maps, cols, kept, back, query, state_grad):
    x, proj, fk = kept[0], kept[2], kept[4]
    dx1 = back[1]
    dq, query_map, dfk, dv = query
    return call(
        key_kernel,
        (1,),
        [
            (proj, (ROWS, D), still(0, 1)),
            (proj, (ROWS, D), still(0, 2)),
            fk,
            state_grad,
            dfk,
            dv,
            dq,
            cols,
            (maps, (1, PAIRS, 256, 256), still(1, 0, 0, 0)),
            (flat[0], (3 * D, D), still(0, 0)),
            x,
            norms[0],
            dx1,
        ],
        [((ROWS, 3 * D), BF), ((HD, D), F32), ((ROWS, D), F32), ((2, D), F32)],
        2 * ROWS * 3 * D * D,
    )


def proj_rows_call(net, kept, dqkv):
    return call(
        proj_rows_kernel,
        (3 * D // TILE,),
        [(dqkv, (ROWS, TILE), lambda i: (0, i)), kept[1]],
        sides(net, 3 * D),
        2 * ROWS * 3 * D * D,
        [pltpu.VMEM((TILE, D), F32)],
    )


def pair_maps(fmap):
    grid = fmap.reshape(LAYERS, 2, HD, PAIRS, 2, HD).transpose(0, 1, 3, 4, 2, 5)
    both = jnp.concatenate([grid, -grid], axis=-1)
    empty = jnp.zeros_like(both[:, :, :, 0])
    top = jnp.concatenate([both[:, :, :, 0], empty], axis=-1)
    bottom = jnp.concatenate([empty, both[:, :, :, 1]], axis=-1)
    return jnp.concatenate(two(jnp.concatenate([top, bottom], axis=3)), axis=3)


def doc_layout(doc_lengths, start, span):
    ends = jnp.cumsum(doc_lengths, axis=1)
    places = start + jnp.arange(span, dtype=jnp.int32)
    documents = jnp.sum((places[None, :, None] >= ends[:, None, :]).astype(jnp.int32), axis=2)
    before = jnp.sum((start - 1 >= ends).astype(jnp.int32), axis=1)
    previous = jnp.where(start > 0, before, -1)
    mark = (documents == previous[:, None]).reshape(-1, 1)
    last = (documents == documents[:, span - 1 :]).reshape(-1, 1)
    lane = jnp.arange(128)[None, :]
    cols = jnp.where(lane == 0, mark, (lane == 1) & last).astype(F32)
    names = (documents + (DOCS + 1) * jnp.arange(documents.shape[0])[:, None]).reshape(-1)
    lower = jnp.arange(names.shape[0])[:, None] >= jnp.arange(names.shape[0])[None, :]
    visible = (lower & (names[:, None] == names[None, :])).astype(F32)
    return cols, visible


def body(tokens, doc_lengths, weights, norm_gain, norm_bias, fmap, cotangent):
    net = Net()
    sequences, span = tokens.shape[:2]
    start = lax.axis_index("seq") * span
    rows = sequences * span
    def prepare(doc_lengths, fmap, norm_gain, norm_bias, tokens, cotangent):
        cols, visible = doc_layout(doc_lengths, start, span)
        last_doc = last_docs(doc_lengths, span)
        gates = [scan_gates(net, last_doc, reverse) for reverse in (False, True)]
        maps = pair_maps(fmap)
        norms = jnp.stack([norm_gain, norm_bias], axis=2)
        x, e = [array.reshape(rows, D).astype(F32) for array in (tokens, cotangent)]
        return cols, visible, gates, maps, norms, x, e

    given = (doc_lengths, fmap, norm_gain, norm_bias, tokens, cotangent)
    steps = len(list(doublings(net.nz)))
    if net.nz == 4 and net.nb == 2 and weights.shape[1] % 32 == 0:
        first, second = [Gather(net, weights[layer]) for layer in range(LAYERS)]
        own = first.shard[None]
        next_z = [first.along_z(first.shard, step) for step in (1, 3)]
        sides = first.sides(own)
        own, sides, shard = tie(own, sides, first.shard)
        corners = first.corners(*sides)
        own, sides, corners, next_z, shard, given = tie(own, sides, corners, next_z, shard, given)
        far = first.along_z(shard, 2)[None]
        next_z = jnp.stack(next_z)
        next_sides = first.sides(next_z)
        prepared = prepare(*given)
        next_z, next_sides, far, shard = tie(next_z, next_sides, far, second.shard)
        next_corners = first.corners(*next_sides)
        far_sides = first.sides(far)
        second_z = [second.along_z(shard, step) for step in (1, 3)]
        first.add((0,), own, sides, corners)
        next_corners, far, far_sides, prepared, second_z = tie(
            next_corners, far, far_sides, prepared, second_z
        )
        cols, visible, gates, maps, norms, x, e1 = prepared
        far_corners = first.corners(*far_sides)
        first.add((1, 3), next_z, next_sides, next_corners)
        own = shard[None]
        sides = second.sides(own)
        second_z.append(second.along_z(shard, 2))
        far, far_sides, far_corners = tie(far, far_sides, far_corners)
        first.add((2,), far, far_sides, far_corners)
        head = first.rows(0, 1)
        kept0 = head_call(x, (head, None), norms[0], maps[0], cols)
        scan = scan_steps(net, kept0[4], gates[0], False)
        came = next(scan)
        came, own, sides, second_z = tie(came, own, sides, second_z)
        corners = second.corners(*sides)
        second_z = jnp.stack(second_z)
        came = scan.send(came)
        came, own, sides, corners, second_z = tie(came, own, sides, corners, second_z)
        second_sides = second.sides(second_z)
        second.add((0,), own, sides, corners)
        came = scan.send(came)
        for _ in range(1, steps):
            came = scan.send(came)
        rest = first.rows(1, net.nz)
        came, rest = tie(came, rest)
        came = scan.send(came)
        came, second_z, second_sides = tie(came, second_z, second_sides)
        second_corners = second.corners(*second_sides)
        edges = second.edges(second_z, second_sides)
        state = finish(scan, came)
        x1, kept0 = tail_call(x, (head, rest), norms[0], cols, visible, kept0, state)
        x1, second_corners, edges = tie(x1, second_corners, edges)
        points = second.points(second_corners)
        second.groups.append(((1, 3, 2), (second_z, *second_sides, *second_corners), (edges, points)))
        gathered = [(head, rest)]
        head = second.rows(0, 1)
        kept1 = head_call(x1, (head, None), norms[1], maps[1], cols)
        scan = scan_steps(net, kept1[4], gates[0], False)
        came = next(scan)
        rest = second.rows(1, net.nz)
        for _ in range(steps + 1):
            came = scan.send(came)
        came, rest = tie(came, rest)
        state = finish(scan, came)
        gathered.append((head, rest))
    else:
        gathered = [lax.all_gather(weights[layer], AXES, axis=0, tiled=True) for layer in range(LAYERS)]
        gathered = [(flat[: 3 * D], flat[3 * D :]) for flat in gathered]
        cols, visible, gates, maps, norms, x, e1 = prepare(*given)
        kept0 = head_call(x, gathered[0], norms[0], maps[0], cols)
        state = finish(scan_steps(net, kept0[4], gates[0], False), None)
        x1, kept0 = tail_call(x, gathered[0], norms[0], cols, visible, kept0, state)
        kept1 = head_call(x1, gathered[1], norms[1], maps[1], cols)
        state = finish(scan_steps(net, kept1[4], gates[0], False), None)
    x, kept1 = tail_call(x1, gathered[1], norms[1], cols, visible, kept1, state)
    result = x.astype(BF).reshape(tokens.shape)
    cut = net.nz * 3 * D // (4 * D + 2 * FF)
    rest_sum = Scatter(net, cut, net.nz)
    both_sum = Scatter(net, 0, net.nz)
    head_sum = Scatter(net, 0, cut)

    back1 = back_call(e1, gathered[1], norms[1], cols, kept1)
    scan = scan_steps(net, back1[5], gates[1], True)
    came = next(scan)
    came, held = tie(came, e1)
    came = scan.send(came)
    keep, send = rows_call(net, held, kept1, back1)
    came, keep, send, back1 = tie(came, keep, send, back1)
    came = scan.send(came)
    swapped = net.core(send)
    query1 = query_call(maps[1], cols, visible, kept1, back1)
    came, query1, keep, swapped = tie(came, query1, keep, swapped)
    for _ in range(1, len(list(doublings(net.nz)))):
        came = scan.send(came)
    tops, bottoms = rest_sum.split([(keep, swapped)])
    came, tops, bottoms = tie(came, tops, bottoms)
    came = scan.send(came)
    came, bottoms = tie(came, bottoms)
    rest1 = rest_sum.first_send((tops, bottoms))
    state_grad = finish(scan, came)
    dqkv1, key_map1, e0, norm_one1 = key_call(
        gathered[1], norms[1], maps[1], cols, kept1, back1, query1, state_grad
    )
    small1 = jnp.concatenate([query1[1], key_map1, norm_one1, back1[6]], axis=0)

    back0 = back_call(e0, gathered[0], norms[0], cols, kept0)
    back0, dqkv1 = tie(back0, dqkv1)
    scan = scan_steps(net, back0[5], gates[1], True)
    came = next(scan)
    keep1, send1 = proj_rows_call(net, kept1, dqkv1)
    came, keep1, send1, held = tie(came, keep1, send1, e0)
    came = scan.send(came)
    swapped1 = net.core(send1)
    keep0, send0 = rows_call(net, held, kept0, back0)
    came, keep0, send0, rest1 = tie(came, keep0, send0, rest1)
    came = scan.send(came)
    swapped0 = net.core(send0)
    rest1 = rest_sum.first_add(rest1)
    came, rest1, keep0, swapped0, keep1, swapped1 = tie(came, rest1, keep0, swapped0, keep1, swapped1)
    for _ in range(1, len(list(doublings(net.nz)))):
        came = scan.send(came)
    rest1 = rest_sum.second_send(rest1)
    tops, bottoms = both_sum.split([(keep1, swapped1), (keep0, swapped0)])
    came, tops, bottoms, back0, rest1 = tie(came, tops, bottoms, back0, rest1)
    came = scan.send(came)
    query0 = query_call(maps[0], cols, visible, kept0, back0)
    rest1 = rest_sum.second_add(rest1)
    came, bottoms, query0, rest1 = tie(came, bottoms, query0, rest1)
    both = both_sum.first_send((tops, bottoms))
    rest1 = rest_sum.z_halves(rest1)
    apart = next(rest1)
    state_grad = finish(scan, came)
    dqkv0, key_map0, e, norm_one0 = key_call(
        gathered[0], norms[0], maps[0], cols, kept0, back0, query0, state_grad
    )

    small0 = jnp.concatenate([query0[1], key_map0, norm_one0, back0[6]], axis=0)
    summing = sum_steps(net, jnp.stack([small0, small1]))
    small = next(summing)
    both, dqkv0 = tie(both, dqkv0)
    both = both_sum.first_add(both)
    both, dqkv0, apart, small = tie(both, dqkv0, apart, small)
    both = both_sum.second_send(both)
    keep, send = proj_rows_call(net, kept0, dqkv0)
    swapped = net.core(send)
    apart = rest1.send(apart)
    small = summing.send(small)
    head0 = head_sum.split([(keep, swapped)])
    head0, apart = tie(head0, apart)
    both = after(both, head0)
    head0 = head_sum.first_send(head0)
    rest1 = finish(rest1, apart)
    both = both_sum.second_add(both)
    both, small = tie(both, small)
    both = both_sum.z_sum(both)
    far = next(both)
    head0 = head_sum.first_add(head0)
    small = summing.send(after(small, head0))
    small, far = tie(small, far)
    near = both.send(far)
    head0 = head_sum.second_add(head_sum.second_send(head0))
    if cut == 1:
        head0 = head_sum.z_tree(head0)
    else:
        head0 = head_sum.z_sum(head0)
    came = next(head0)
    came, near = tie(came, near)
    both = finish(both, near)
    head0 = finish(head0, came)
    small = finish(summing, small)

    both = add_up(both)
    shards = [
        jnp.where(net.z < cut, add_up(head0), both),
        jnp.where(net.z < cut, both, add_up(rest1)),
    ]
    cut = 2 * HD
    return (
        result,
        e.reshape(tokens.shape),
        jnp.stack(shards),
        small[:, cut::2],
        small[:, cut + 1 :: 2],
        small[:, :cut].reshape(fmap.shape),
    )


def solution(mesh):
    in_specs = (
        P("batch", "seq", None),
        P("batch", None),
        P(None, ("seq", "batch"), None),
        P(),
        P(),
        P(),
        P("batch", "seq", None),
    )
    out_specs = (
        P("batch", "seq", None),
        P("batch", "seq", None),
        P(None, ("seq", "batch"), None),
        P(),
        P(),
        P(),
    )
    return jax.shard_map(body, mesh=mesh, in_specs=in_specs, out_specs=out_specs, check_vma=False)
```

```python
import functools

import jax
import jax.numpy as jnp
from jax import lax
from jax.experimental import pallas as pl
from jax.experimental.pallas import tpu as pltpu
from jax.sharding import PartitionSpec as P

D = 768
H = 12
HD = 64
FF = 3072
LAYERS = 2
DOCS = 4
EPSILON = 1e-05
F32 = jnp.float32
BF = jnp.bfloat16
PAIRS = H // 2
WIDE_LIMIT = 40 * 1024 * 1024


AXES = ("seq", "batch")


class Net:
    def __init__(self):
        self.nz = lax.axis_size("seq") // 4
        self.nb = lax.axis_size("batch")
        place = lax.axis_index("seq")
        self.z = place // 4
        self.y = (place // 2) % 2
        self.c = place % 2
        self.b = lax.axis_index("batch")

    def move(self, array, target):
        pairs = []
        for index in range(self.nz * 4 * self.nb):
            place = index // self.nb
            goal = target(place // 4, (place // 2) % 2, place % 2, index % self.nb)
            if goal is not None:
                z, y, c, b = goal
                pairs.append((index, ((z * 2 + y) * 2 + c) * self.nb + b))
        return lax.ppermute(array, AXES, pairs)

    def core(self, array):
        return self.move(array, lambda z, y, c, b: (z, y, 1 - c, b))

    def flip_y(self, array):
        return self.move(array, lambda z, y, c, b: (z, 1 - y, c, b))

    def turn_b(self, array, step):
        return self.move(array, lambda z, y, c, b: (z, y, c, (b + step) % self.nb))

    def shift_z(self, array, step):
        def target(z, y, c, b):
            return (z + step, y, c, b) if 0 <= z + step < self.nz else None

        return self.move(array, target)


def pick(array, index, axis=0):
    return lax.dynamic_index_in_dim(array, index, axis, False)


def last_docs(doc_lengths, span):
    ends = jnp.cumsum(doc_lengths, axis=1)

    def last_doc(block):
        found = jnp.sum(((block + 1) * span - 1 >= ends).astype(jnp.int32), axis=1)
        return jnp.where(block < 0, -1, found)

    return last_doc


def doublings(count):
    step = 1
    while step < count:
        yield step
        step *= 2


def scan_gates(net, last_doc, reverse):
    base = 4 * net.z
    first = base + 2 * net.y
    if reverse:
        pairs = [(first, first - 1), (base + 1, base - 1), (base + 3, base + 1), (first + 1, first)]
        for step in doublings(net.nz):
            pairs += [(4 * (net.z + step) - 1, base + 3), (4 * (net.z + step) - 1, base - 1)]
    else:
        pairs = [(first, first + 1), (base + 1, base + 3), (base - 1, base + 1), (first - 1, first)]
        for step in doublings(net.nz):
            pairs += [(4 * (net.z - step) + 3, base - 1), (4 * (net.z - step) + 3, base + 3)]
    same = jnp.stack([last_doc(a) == last_doc(b) for a, b in pairs])
    return pick(same, net.c, 1).astype(F32)


def scan_steps(net, packed, gates, reverse):
    wide = F32
    low = F32
    mine = pick(packed, net.c)
    theirs = yield net.core(pick(packed, 1 - net.c))
    zero = jnp.equal(net.c, 0)
    part0 = jnp.where(zero, mine, theirs).astype(wide)
    part1 = jnp.where(zero, theirs, mine).astype(wide)
    if reverse:
        chip = part0 + gates[0] * part1
    else:
        chip = gates[0] * part0 + part1
    chip = chip.astype(low)
    own = pick(chip, net.y)
    other = yield net.flip_y(pick(chip, 1 - net.y))
    down = jnp.equal(net.y, 0)
    row0 = jnp.where(down, own, other).astype(wide)
    row1 = jnp.where(down, other, own).astype(wide)
    if reverse:
        plane = row0 + gates[1] * row1
    else:
        plane = gates[1] * row0 + row1
    entering = jnp.zeros(plane.shape, wide)
    for index, step in enumerate(doublings(net.nz)):
        part = yield net.shift_z(plane, -step if reverse else step)
        entering = entering + gates[4 + 2 * index] * part
        plane = plane + gates[5 + 2 * index] * part
    if reverse:
        row1_in = entering
        row0_in = gates[2] * entering + row1
    else:
        row0_in = entering
        row1_in = gates[2] * entering + row0
    own_in = jnp.where(down, row0_in, row1_in)
    other_in = yield net.flip_y(jnp.where(down, row1_in, row0_in).astype(low))
    other_in = other_in.astype(wide)
    chip_in = jnp.where(down, jnp.stack([own_in, other_in]), jnp.stack([other_in, own_in]))
    if reverse:
        core1_in = chip_in
        core0_in = gates[3] * chip_in + part1
    else:
        core0_in = chip_in
        core1_in = gates[3] * chip_in + part0
    core0_in = core0_in.astype(low)
    core1_in = core1_in.astype(low)
    kept = jnp.where(zero, core0_in, core1_in)
    sent = yield net.core(jnp.where(zero, core1_in, core0_in))
    return jnp.where(zero, jnp.stack([kept, sent]), jnp.stack([sent, kept]))


def finish(steps, value):
    while True:
        try:
            value = steps.send(value)
        except StopIteration as stop:
            return stop.value


def after(value, *conditions):
    return lax.optimization_barrier((value, conditions))[0]


def tie(*groups):
    return lax.optimization_barrier(groups)


class Gather:
    def __init__(self, net, shard):
        self.net = net
        self.shard = shard
        self.half = shard.shape[0] // 2
        self.arrays = []
        self.parts = []

    def along_z(self, shard, step):
        return self.net.move(shard, lambda z, y, c, b: ((z + step) % self.net.nz, y, c, b))

    def sides(self, blocks):
        return self.net.turn_b(blocks, 1), self.net.flip_y(blocks)

    def cuts(self, sides):
        return sides[0][:, : self.half], sides[1][:, self.half :]

    def corners(self, cuts):
        return self.net.flip_y(cuts[0]), self.net.turn_b(cuts[1], 1)

    def note(self, array, spots, apart=0):
        size = array.shape[0] * array.shape[1] // len(spots)
        for number, (below, y, b, row) in enumerate(spots):
            index, start = divmod(number * size, array.shape[1])
            self.parts.append((len(self.arrays), index, start, size, below, y, b, apart, row))
        self.arrays.append(array)

    def note_pair(self, array, halves, block, apart):
        number = len(self.arrays)
        size = 2 * self.half
        for index, (below, y, b, row) in enumerate(halves):
            self.parts.append((number, 0, index * self.half, self.half, below, y, b, apart, row))
        for below, y, b, row in block:
            self.parts.append((number, 1, 0, size, below, y, b, apart, row))
        self.arrays.append(array)

    def both(self, array, swapped, spots):
        self.note(array, spots)
        self.note(swapped, spots, 1)

    def rows(self, first, last):
        size = self.shard.shape[0]
        blocks = (last - first) * 4 * self.net.nb
        return pl.pallas_call(
            functools.partial(place_kernel, self.parts, first, last, size),
            in_specs=[pl.BlockSpec(memory_space=pl.ANY)] * len(self.arrays),
            out_specs=pl.BlockSpec(memory_space=pl.ANY),
            out_shape=jax.ShapeDtypeStruct((blocks * size, D), BF),
            scratch_shapes=[
                pltpu.VMEM((blocks * size, D), BF),
                pltpu.SemaphoreType.DMA((last - first, 10)),
                pltpu.SemaphoreType.DMA((last - first,)),
            ],
            compiler_params=pltpu.CompilerParams(vmem_limit_bytes=60 * 1024 * 1024),
            cost_estimate=pl.CostEstimate(flops=0, bytes_accessed=blocks * size * D * 4, transcendentals=0),
        )(*self.arrays)


def block_copies(parts, first, size, arrays, held, sems):
    place = lax.axis_index("seq")
    z = place // 4
    y = lax.rem(place // 2, 2)
    c = lax.rem(place, 2)
    b = lax.axis_index("batch")

    def each(plane, act):
        for below in range(4):
            chosen = [part for part in parts if part[4] == below]

            @pl.when(lax.rem(z - plane + 4, 4) == below)
            def _(chosen=chosen):
                for number, (array, index, start, rows, _, dy, db, dc, offset) in enumerate(chosen):
                    row = (lax.rem(y + dy, 2) * 2 + lax.rem(c + dc, 2)) * 2 + lax.rem(b + db, 2)
                    goal = pl.multiple_of((plane - first) * 8 * size + row * size + offset, 16)
                    source = arrays[array].at[index, pl.ds(start, rows)]
                    target = held.at[pl.ds(goal, rows)]
                    act(pltpu.make_async_copy(source, target, sems.at[plane - first, number]))

    return each


def place_kernel(parts, first, last, size, *refs):
    arrays, (out, held, in_sems, out_sems) = refs[:-4], refs[-4:]
    each = block_copies(parts, first, size, arrays, held, in_sems)
    plane_rows = 8 * size

    def output(plane):
        rows = pl.ds((plane - first) * plane_rows, plane_rows)
        return pltpu.make_async_copy(held.at[rows], out.at[rows], out_sems.at[plane - first])

    for plane in range(first, last):
        each(plane, lambda copy: copy.start())
    for plane in range(first, last):
        each(plane, lambda copy: copy.wait())
        output(plane).start()
    for plane in range(first, last):
        output(plane).wait()


class Scatter:
    def __init__(self, net, first, last, share=9):
        self.net = net
        self.first = first
        self.last = last
        self.share = share

    def split(self, pairs):
        net = self.net
        if (pairs[0][0].shape[1] // net.nb) % 32 == 0:
            return split_call(net, pairs, self.share)
        total = jnp.concatenate([(a.astype(F32) + b.astype(F32)).astype(BF) for a, b in pairs], axis=0)
        total = total.reshape(self.last - self.first, 2, net.nb, -1, D)
        cut = total.shape[3] * self.share // 18
        top = total[:, :, :, :cut]
        bottom = total[:, :, :, cut:]
        return (
            [pick(top, (net.b + step) % net.nb, 2) for step in range(net.nb)],
            [pick(bottom, net.y, 1), pick(bottom, 1 - net.y, 1)],
        )

    def send_b(self, parts):
        return [parts[0]] + [self.net.turn_b(parts[step], step) for step in range(1, self.net.nb)]

    def send_y(self, parts):
        return [parts[0], self.net.flip_y(parts[1])]

    def first_send(self, buffers):
        return self.send_b(buffers[0]), self.send_y(buffers[1])

    def first_add(self, came):
        net = self.net
        if net.nb == 2 and came[0][0].shape[2] % 16 == 0 and came[1][0].shape[2] % 16 == 0:
            return fold_call(came)
        top = add_up(came[0]).astype(BF)
        bottom = add_up(came[1]).astype(BF)
        return (
            [pick(top, net.y, 1), pick(top, 1 - net.y, 1)],
            [pick(bottom, (net.b + step) % net.nb, 1) for step in range(net.nb)],
        )

    def second_send(self, buffers):
        return self.send_y(buffers[0]), self.send_b(buffers[1])

    def second_add(self, came):
        return jnp.concatenate([add_up(part).astype(BF) for part in came], axis=1)

    def z_send(self, rows, steps):
        net = self.net
        limit = self.last - self.first - 1
        came = []
        for step in steps:
            part = pick(rows, jnp.clip((net.z + step) % net.nz - self.first, 0, limit))

            def target(z, y, c, b, step=step):
                goal = (z + step) % net.nz
                return (goal, y, c, b) if self.first <= goal < self.last else None

            came.append(net.move(part, target) if step else part)
        return came

    def z_halves(self, rows):
        net = self.net
        empty = [jnp.zeros((count,) + rows.shape[1:], BF) for count in (self.first, net.nz - self.last)]
        rows = jnp.concatenate([empty[0], rows, empty[1]], axis=0)
        step = net.nz // 2
        while step:
            upper = (net.z // step) % 2
            halves = rows.reshape((2, step) + rows.shape[1:])
            kept = pick(halves, upper)
            came = yield net.move(pick(halves, 1 - upper), lambda z, y, c, b, step=step: (z ^ step, y, c, b))
            rows = (kept.astype(F32) + came.astype(F32)).astype(BF)
            step //= 2
        return [rows[0]]

    def z_tree(self, rows):
        total = rows[0]
        for step in doublings(self.net.nz):

            def target(z, y, c, b, step=step):
                far = (z - self.first) % self.net.nz
                return ((z - step) % self.net.nz, y, c, b) if far % (2 * step) == step else None

            came = yield self.net.move(total, target)
            total = (total.astype(F32) + came.astype(F32)).astype(BF)
        return [total]

    def z_sum(self, rows):
        half = self.net.nz // 2
        came = yield self.z_send(rows, [half])
        rest = yield self.z_send(rows, [step for step in range(1, self.net.nz) if step != half])
        return came + rest + self.z_send(rows, [0])


def add_up(parts):
    return sum(part.astype(F32) for part in parts)


def sum_steps(net, array):
    targets = []
    for step in doublings(net.nz):
        targets.append(lambda z, y, c, b, step=step: (z ^ step, y, c, b))
    for step in doublings(net.nb):
        targets.append(lambda z, y, c, b, step=step: (z, y, c, b ^ step))
    targets.append(lambda z, y, c, b: (z, y, 1 - c, b))
    targets.append(lambda z, y, c, b: (z, 1 - y, c, b))
    for target in targets:
        array = array.astype(BF)
        came = yield net.move(array, target)
        array = array.astype(F32) + came.astype(F32)
    return array


def nn(a, b):
    return lax.dot_general(a, b, (((1,), (0,)), ((), ())), preferred_element_type=F32)


def nt(a, b):
    return lax.dot_general(a, b, (((1,), (1,)), ((), ())), preferred_element_type=F32)


def tn(a, b):
    return lax.dot_general(a, b, (((0,), (0,)), ((), ())), preferred_element_type=F32)


def two(a):
    high = a.astype(BF)
    return high, (a - high.astype(F32)).astype(BF)


def left_half(shape):
    return lax.broadcasted_iota(jnp.int32, shape, 1) < 64


def normed(values, gain, bias):
    mean = jnp.mean(values, axis=1, keepdims=True)
    centred = values - mean
    variance = jnp.mean(centred * centred, axis=1, keepdims=True)
    return centred * lax.rsqrt(variance + EPSILON) * gain + bias


def normed_back(values, gain, upstream):
    mean = jnp.mean(values, axis=1, keepdims=True)
    centred = values - mean
    variance = jnp.mean(centred * centred, axis=1, keepdims=True)
    scale = lax.rsqrt(variance + EPSILON)
    unit = centred * scale
    inner = upstream * gain
    grad = scale * (
        inner
        - jnp.mean(inner, axis=1, keepdims=True)
        - unit * jnp.mean(inner * unit, axis=1, keepdims=True)
    )
    return grad, jnp.sum(upstream * unit, axis=0, keepdims=True), jnp.sum(upstream, axis=0, keepdims=True)


def softmax_halves(values):
    left = left_half(values.shape)
    low = jnp.float32(-jnp.inf)
    top0 = jnp.max(jnp.where(left, values, low), axis=1, keepdims=True)
    top1 = jnp.max(jnp.where(left, low, values), axis=1, keepdims=True)
    raised = jnp.exp(values - jnp.where(left, top0, top1))
    sum0 = jnp.sum(jnp.where(left, raised, 0.0), axis=1, keepdims=True)
    sum1 = jnp.sum(jnp.where(left, 0.0, raised), axis=1, keepdims=True)
    return raised / jnp.where(left, sum0, sum1)


def softmax_halves_back(weights, upstream):
    left = left_half(weights.shape)
    product = weights * upstream
    sum0 = jnp.sum(jnp.where(left, product, 0.0), axis=1, keepdims=True)
    sum1 = jnp.sum(jnp.where(left, 0.0, product), axis=1, keepdims=True)
    return product - weights * jnp.where(left, sum0, sum1)


def lanes(ref, head):
    return ref[:, head * 128 : (head + 1) * 128]


def state_at(ref, seq, pair):
    start = pair % 3 * 128
    return ref[seq, pair // 3, start : start + 128, :]


def normaliser_at(ref, head):
    row = H // 2 * HD + head % 6
    parts = [ref[seq, head // 6, row : row + 1, :] for seq in range(2)]
    return jnp.concatenate([jnp.broadcast_to(part, (64, 128)) for part in parts], axis=0)


def store_state(ref, seq, pair, block, row):
    half = pair // 3
    start = pair % 3 * 128
    ref[seq, half, start : start + 64, :] = block[:64, :128]
    ref[seq, half, start + 64 : start + 128, :] = block[64:, 128:]
    tail = H // 2 * HD + pair % 3 * 2
    ref[seq, half, tail : tail + 1, :] = row[:, :128]
    ref[seq, half, tail + 1 : tail + 2, :] = row[:, 128:]


def clear_tail(ref):
    for seq in range(2):
        for half in range(2):
            ref[seq, half, 390:400, :] = jnp.zeros((10, 128), F32)


def head_kernel(gather, x_ref, norm_ref, map_ref, cols_ref, *refs):
    step = pl.program_id(0)
    if gather is None:
        w_ref, h_ref, proj_ref, fq_ref, fk_ref, state_ref = refs
    else:
        arrays, (h_ref, proj_ref, fq_ref, fk_ref, state_ref, held, sems) = refs[:-7], refs[-7:]
        each = block_copies(gather[0], 0, gather[1], arrays, held, sems)

    @pl.when(step == 0)
    def _():
        if gather is not None:
            each(0, lambda copy: copy.start())
        h_ref[...] = normed(x_ref[...], norm_ref[0:1, :], norm_ref[1:2, :]).astype(BF)
        if gather is not None:
            each(0, lambda copy: copy.wait())

    weights = w_ref[...] if gather is None else held[pl.ds(pl.multiple_of(step * D, D), D), :]
    proj_ref[...] = nt(h_ref[...], weights).astype(BF)

    def features(out_ref):
        for pair in range(PAIRS):
            part = lanes(proj_ref, pair)
            before = nn(jnp.concatenate([part, part], axis=1), map_ref[0, pair])
            for side in range(2):
                head = pair * 2 + side
                out_ref[:, head * 128 : (head + 1) * 128] = softmax_halves(
                    before[:, side * 128 : (side + 1) * 128]
                )

    @pl.when(step == 0)
    def _():
        features(fq_ref)

    @pl.when(step == 1)
    def _():
        features(fk_ref)

    @pl.when(step == 2)
    def _():
        clear_tail(state_ref)
        for seq in range(2):
            rows = slice(seq * 64, seq * 64 + 64)
            last = cols_ref[rows, 1:2]
            for pair in range(PAIRS):
                feats = fk_ref[rows, pair * 256 : (pair + 1) * 256].astype(BF).astype(F32) * last
                block = tn(proj_ref[rows, pair * 128 : (pair + 1) * 128], feats.astype(BF))
                store_state(state_ref, seq, pair, block, jnp.sum(feats, axis=0, keepdims=True))


def tail_kernel(
    x_ref, v_ref, fq_ref, fk_ref, state_ref, cols_ref, vis_ref, norm_ref, wo_ref, wu_ref, wd_ref,
    o_ref, rden_ref, att_ref, x1_ref, h2_ref, u_ref, g_ref, out_ref,
):
    @pl.when(pl.program_id(0) == 0)
    def _():
        visible = vis_ref[...]
        mark = cols_ref[:, 0:1]
        left = left_half((128, 128))
        for pair in range(PAIRS):
            value = lanes(v_ref, pair)
            nothing = jnp.zeros_like(value)
            state = [jnp.concatenate(two(state_at(state_ref, seq, pair)), axis=1) for seq in range(2)]
            weights = []
            totals = []
            carried = []
            for side in range(2):
                head = pair * 2 + side
                query = lanes(fq_ref, head).astype(BF)
                score = nt(query, lanes(fk_ref, head).astype(BF)) * visible
                weights.append(score.astype(BF))
                wide = query.astype(F32) * normaliser_at(state_ref, head) * mark
                totals.append(jnp.sum(score + wide, axis=1, keepdims=True))
                twice = jnp.concatenate([query, query], axis=1)
                carried.append(
                    jnp.concatenate([nt(twice[:64], state[0]), nt(twice[64:], state[1])], axis=0)
                )
            number = nn(
                jnp.concatenate(weights, axis=1),
                jnp.concatenate([jnp.where(left, value, nothing), jnp.where(left, nothing, value)], axis=0),
            )
            number = number + mark * jnp.where(left, carried[0], carried[1])
            inverse = 1.0 / jnp.where(left, totals[0], totals[1])
            output = number * inverse
            cut = slice(pair * 128, (pair + 1) * 128)
            o_ref[:, cut] = output
            rden_ref[:, cut] = inverse
            att_ref[:, cut] = output.astype(BF)
        x1 = x_ref[...] + nn(att_ref[...], wo_ref[...])
        x1_ref[...] = x1
        h2_ref[...] = normed(x1, norm_ref[0:1, :], norm_ref[1:2, :]).astype(BF)
        out_ref[...] = x1

    u = nt(h2_ref[...], wu_ref[...])
    u_ref[...] = u
    inner = jnp.tanh(0.7978845608028654 * (u + 0.044715 * (u * u * u)))
    g = (0.5 * u * (1.0 + inner)).astype(BF)
    g_ref[...] = g
    out_ref[...] += nn(g, wd_ref[...])


def back_kernel(
    e_ref, u_ref, x1_ref, norm_ref, wd_ref, wu_ref, wo_ref, o_ref, rden_ref, fq_ref, cols_ref,
    du_ref, dx1_ref, ebx_ref, dn_ref, dd_ref, state_ref, gn_ref, total,
):
    step = pl.program_id(0)
    dg = nt(e_ref[...].astype(BF), wd_ref[...])
    u = u_ref[...]
    inner = jnp.tanh(0.7978845608028654 * (u + 0.044715 * (u * u * u)))
    slope = 0.5 * (1.0 + inner) + (0.5 * u) * (1.0 - inner * inner) * (
        0.7978845608028654 * (1.0 + 0.134145 * (u * u))
    )
    du = (dg * slope).astype(BF)
    du_ref[...] = du
    part = nn(du, wu_ref[...])

    @pl.when(step == 0)
    def _():
        total[...] = part

    @pl.when(step > 0)
    def _():
        total[...] += part

    @pl.when(step == pl.num_programs(0) - 1)
    def _():
        grad, gain, bias = normed_back(x1_ref[...], norm_ref[0:1, :], total[...])
        gn_ref[0:1, :] = gain
        gn_ref[1:2, :] = bias
        dx1 = e_ref[...] + grad
        dx1_ref[...] = dx1
        low = dx1.astype(BF)
        ebx_ref[...] = low
        dn_ref[...] = nt(low, wo_ref[...]).astype(BF).astype(F32) * rden_ref[...]
        left = left_half((128, 128))
        lane = lax.broadcasted_iota(jnp.int32, (128, 128), 1)
        clear_tail(state_ref)
        columns = jnp.zeros((128, 128), F32)
        for pair in range(PAIRS):
            dn = lanes(dn_ref, pair)
            product = dn * lanes(o_ref, pair)
            d0 = -jnp.sum(jnp.where(left, product, 0.0), axis=1, keepdims=True)
            d1 = -jnp.sum(jnp.where(left, 0.0, product), axis=1, keepdims=True)
            columns = jnp.where(lane == pair * 2, d0, jnp.where(lane == pair * 2 + 1, d1, columns))
            for seq in range(2):
                rows = slice(seq * 64, seq * 64 + 64)
                mark = cols_ref[rows, 0:1]
                high, rest = two(dn[rows] * mark)
                feats = fq_ref[rows, pair * 256 : (pair + 1) * 256].astype(BF)
                block = tn(jnp.concatenate([high, rest], axis=0), jnp.concatenate([feats, feats], axis=0))
                wide = feats.astype(F32)
                row = jnp.concatenate(
                    [
                        jnp.sum(wide[:, :128] * (d0[rows] * mark), axis=0, keepdims=True),
                        jnp.sum(wide[:, 128:] * (d1[rows] * mark), axis=0, keepdims=True),
                    ],
                    axis=1,
                )
                store_state(state_ref, seq, pair, block, row)
        dd_ref[...] = columns


def fold_map(pair_weights, low_q):
    left = left_half((128, 128))
    folded = [weight - pltpu.roll(weight, 64, 1) for weight in pair_weights]
    grad = jnp.where(left, folded[0], pltpu.roll(folded[1], 64, 1))
    high, rest = two(grad)
    twice = jnp.concatenate([low_q, low_q], axis=0)
    table = tn(twice, jnp.concatenate([high, rest], axis=0))
    return jnp.where(left[:64], table[:64], table[64:])


def query_kernel(
    q_ref, v_ref, fq_ref, fk_ref, state_ref, dn_ref, dd_ref, cols_ref, vis_ref, map_ref,
    dq_ref, dmap_ref, dfk_ref, dv_ref,
):
    visible = vis_ref[...]
    low_visible = visible.astype(BF)
    mark = cols_ref[:, 0:1]
    left = left_half((128, 128))
    for pair in range(PAIRS):
        value = lanes(v_ref, pair)
        dn = lanes(dn_ref, pair)
        twice = jnp.concatenate([value, value], axis=1)
        state = [two(state_at(state_ref, seq, pair)) for seq in range(2)]
        weights = []
        shifts = []
        turned = []
        for side in range(2):
            head = pair * 2 + side
            wide = lanes(fq_ref, head)
            query = wide.astype(BF)
            key = lanes(fk_ref, head).astype(BF)
            score = (nt(query, key) * visible).astype(BF)
            mine = jnp.where(left, dn, 0.0) if side == 0 else jnp.where(left, 0.0, dn)
            high, rest = two(mine)
            dd = dd_ref[:, head : head + 1]
            shift = (nt(jnp.concatenate([high, rest], axis=1), twice) + dd).astype(BF) * low_visible
            carried = jnp.concatenate(
                [
                    nn(
                        jnp.concatenate([high[rows], high[rows], rest[rows]], axis=1),
                        jnp.concatenate([state[seq][0], state[seq][1], state[seq][0]], axis=0),
                    )
                    for seq, rows in ((0, slice(0, 64)), (1, slice(64, 128)))
                ],
                axis=0,
            )
            dfq = nn(shift, key) + mark * (carried + dd * normaliser_at(state_ref, head))
            dfk_ref[:, head * 128 : (head + 1) * 128] = tn(shift, query)
            weights.append(softmax_halves_back(wide, dfq))
            shifts.append(score)
            turned.append(high)
        cut = slice(pair * 128, (pair + 1) * 128)
        dv_ref[:, cut] = tn(jnp.concatenate(shifts, axis=0), jnp.concatenate(turned, axis=0))
        low = jnp.concatenate(weights, axis=1).astype(BF)
        dq_ref[:, cut] = nt(low, map_ref[0, pair, :128, :]).astype(BF)
        dmap_ref[:, cut] = fold_map(weights, lanes(q_ref, pair))


def key_kernel(
    k_ref, v_ref, fk_ref, state_ref, dfk_ref, dv_ref, dq_ref, cols_ref, map_ref, w_ref, x_ref, norm_ref, dx1_ref,
    dqkv_ref, dmap_ref, e_ref, gn_ref,
):
    last = cols_ref[:, 1:2]
    left = left_half((128, 128))
    dqkv_ref[:, :D] = dq_ref[...]
    for pair in range(PAIRS):
        value = lanes(v_ref, pair)
        nothing = jnp.zeros_like(value)
        state = [two(state_at(state_ref, seq, pair)) for seq in range(2)]
        weights = []
        grads = []
        for side in range(2):
            head = pair * 2 + side
            wide = lanes(fk_ref, head)
            key = wide.astype(BF)
            mine = jnp.where(left, value, nothing) if side == 0 else jnp.where(left, nothing, value)
            carried = []
            turned = []
            for seq, rows in ((0, slice(0, 64)), (1, slice(64, 128))):
                high, rest = state[seq]
                carried.append(
                    nn(
                        jnp.concatenate([mine[rows], mine[rows]], axis=1),
                        jnp.concatenate([high, rest], axis=0),
                    )
                )
                turned.append(nt(key[rows], high))
            carried = jnp.concatenate(carried, axis=0)
            dfk = lanes(dfk_ref, head) + last * (carried + normaliser_at(state_ref, head))
            weights.append(softmax_halves_back(wide, dfk))
            grads.append(jnp.concatenate(turned, axis=0))
        cut = slice(pair * 128, (pair + 1) * 128)
        dv = lanes(dv_ref, pair) + last * jnp.where(left, grads[0], grads[1])
        dqkv_ref[:, 2 * D + pair * 128 : 2 * D + (pair + 1) * 128] = dv.astype(BF)
        low = jnp.concatenate(weights, axis=1).astype(BF)
        dqkv_ref[:, D + pair * 128 : D + (pair + 1) * 128] = nt(low, map_ref[0, pair, :128, :]).astype(BF)
        dmap_ref[:, cut] = fold_map(weights, lanes(k_ref, pair))
    upstream = nn(dqkv_ref[...], w_ref[...])
    grad, gain, bias = normed_back(x_ref[...], norm_ref[0:1, :], upstream)
    gn_ref[0:1, :] = gain
    gn_ref[1:2, :] = bias
    e_ref[...] = dx1_ref[...] + grad


def store_sides(block, keep_ref, send_ref):
    zero = lax.rem(lax.axis_index("seq"), 2) == 0
    groups, size = keep_ref.shape[:2]
    for group in range(groups):
        low = block[group * 2 * size : group * 2 * size + size]
        high = block[group * 2 * size + size : group * 2 * size + 2 * size]
        keep_ref[group] = jnp.where(zero, low, high).astype(BF)
        send_ref[group] = jnp.where(zero, high, low).astype(BF)


def rows_kernel(att_ref, ebx_ref, du_ref, h2_ref, g_ref, e_ref, keep_ref, send_ref, held):
    terms = ((0, D, att_ref, ebx_ref), (D, D + FF, du_ref, h2_ref), (D + FF, D + 2 * FF, g_ref, e_ref))
    for step in range((D + 2 * FF) // TILE):
        start = step * TILE

        @pl.when(pl.program_id(0) == step)
        def _(start=start):
            for first, last, left, right in terms:
                low = max(start, first)
                high = min(start + TILE, last)
                if low < high:
                    held[low - start : high - start, :] = tn(
                        left[:, low - first : high - first], right[...].astype(BF)
                    )
            store_sides(held, keep_ref, send_ref)


def proj_rows_kernel(dqkv_ref, h_ref, keep_ref, send_ref, held):
    held[...] = tn(dqkv_ref[...], h_ref[...])
    store_sides(held, keep_ref, send_ref)


def split_kernel(runs, nb, *refs):
    tops = refs[2 * len(runs) : 2 * len(runs) + nb]
    bottoms = refs[2 * len(runs) + nb :]
    upper, lower = tops[0].shape[2], bottoms[0].shape[2]
    y = lax.rem(lax.axis_index("seq") // 2, 2)
    b = lax.axis_index("batch")
    start = 0
    for index, count in enumerate(runs):
        keep, came = refs[2 * index : 2 * index + 2]

        @pl.when((pl.program_id(0) >= start) & (pl.program_id(0) < start + count))
        def _(keep=keep, came=came):
            def rows(row_y, row_b, offset, count):
                at = pl.ds(pl.multiple_of(row_b * (upper + lower) + offset, 16), count)
                return (keep[row_y, at, :].astype(F32) + came[row_y, at, :].astype(F32)).astype(BF)

            for step, top in enumerate(tops):
                for side in range(2):
                    top[0, side] = rows(side, lax.rem(b + step, nb), 0, upper)
            for step, bottom in enumerate(bottoms):
                for side in range(nb):
                    bottom[0, side] = rows(lax.rem(y + step, 2), side, upper, lower)

        start += count


def split_call(net, pairs, share):
    size = pairs[0][0].shape[1]
    upper = size // net.nb * share // 18
    lower = size // net.nb - upper
    runs = [keep.shape[0] // 2 for keep, _ in pairs]
    planes = sum(runs)
    operands = []
    start = 0
    for pair, count in zip(pairs, runs):

        def index(i, start=start, count=count):
            return (jnp.clip(i - start, 0, count - 1), 0, 0)

        operands += [(array, (2, size, D), index) for array in pair]
        start += count
    outputs = [((planes, 2, upper, D), BF, (1, 2, upper, D), lambda i: (i, 0, 0, 0))] * net.nb
    outputs += [((planes, net.nb, lower, D), BF, (1, net.nb, lower, D), lambda i: (i, 0, 0, 0))] * 2
    parts = call(functools.partial(split_kernel, runs, net.nb), (planes,), operands, outputs, 0)
    return parts[: net.nb], parts[net.nb :]


def fold_kernel(top_keep, top_came, bottom_keep, bottom_came, *outs):
    y = lax.rem(lax.axis_index("seq") // 2, 2)
    b = lax.axis_index("batch")
    for step in range(2):
        at = lax.rem(y + step, 2)
        outs[step][0] = (top_keep[0, at].astype(F32) + top_came[0, at].astype(F32)).astype(BF)
        at = lax.rem(b + step, 2)
        outs[2 + step][0] = (bottom_keep[0, at].astype(F32) + bottom_came[0, at].astype(F32)).astype(BF)


def fold_call(came):
    operands = []
    outputs = []
    for pair in came:
        shape = pair[0].shape
        operands += [(array, (1,) + shape[1:], lambda i: (i, 0, 0, 0)) for array in pair]
        outputs += [((shape[0],) + shape[2:], BF, (1,) + shape[2:], lambda i: (i, 0, 0))] * 2
    parts = call(fold_kernel, (shape[0],), operands, outputs, 0)
    return parts[:2], parts[2:]


def whole(array):
    rank = array.ndim
    return pl.BlockSpec(array.shape, lambda *_: (0,) * rank)


def call(kernel, grid, operands, outputs, flops, scratch=(), free=(), limit=WIDE_LIMIT):
    arrays = []
    in_specs = []
    for operand in operands:
        if isinstance(operand, tuple):
            arrays.append(operand[0])
            in_specs.append(pl.BlockSpec(operand[1], operand[2]))
        else:
            arrays.append(operand)
            in_specs.append(whole(operand))
    arrays += free
    in_specs += [pl.BlockSpec(memory_space=pl.ANY)] * len(free)
    shapes = [jax.ShapeDtypeStruct(out[0], out[1]) for out in outputs]
    out_specs = []
    for out, shape in zip(outputs, shapes):
        out_specs.append(pl.BlockSpec(out[2], out[3]) if len(out) > 2 else whole(shape))
    moved = sum(a.size * a.dtype.itemsize for a in shapes)
    for spec, a in zip(in_specs, arrays):
        moved += a.size * a.dtype.itemsize if a.shape[0] < 6000 else 6 * D * D
    return pl.pallas_call(
        kernel,
        grid=grid,
        in_specs=in_specs,
        out_specs=out_specs,
        out_shape=shapes,
        scratch_shapes=list(scratch),
        compiler_params=pltpu.CompilerParams(vmem_limit_bytes=limit),
        cost_estimate=pl.CostEstimate(flops=flops, bytes_accessed=moved, transcendentals=0),
    )(*arrays)


STATE = (2, 2, H // 2 * HD + 16, 128)
ROWS = 128
CHUNK = D
TILE = 3 * D // 2
CHUNKS = FF // CHUNK


def still(*index):
    return lambda i: index


def head_call(x, flat, norms, maps, cols, gather=None):
    operands = [
        x,
        norms[0],
        (maps, (1, PAIRS, 256, 256), lambda i: (jnp.minimum(i, 1), 0, 0, 0)),
        cols,
    ]
    outputs = [
        ((ROWS, D), BF),
        ((ROWS, 3 * D), BF, (ROWS, D), lambda i: (0, i)),
        ((ROWS, H * 128), F32),
        ((ROWS, H * 128), F32),
        (STATE, F32),
    ]
    flops = 2 * ROWS * 3 * D * D
    if gather is None:
        operands.append((flat[0], (D, D), lambda i: (i, 0)))
        return call(functools.partial(head_kernel, None), (3,), operands, outputs, flops)
    plan = (gather.parts, gather.shard.shape[0])
    scratch = [pltpu.VMEM((3 * D, D), BF), pltpu.SemaphoreType.DMA((1, 10))]
    return call(
        functools.partial(head_kernel, plan), (3,), operands, outputs, flops, scratch, gather.arrays, 60 * 1024 * 1024
    )


def tail_call(x, flat, norms, cols, visible, head, state):
    h1, proj, fq, fk, local = head
    o, rden, att, x1, h2, u, g, result = call(
        tail_kernel,
        (CHUNKS,),
        [
            x,
            (proj, (ROWS, D), still(0, 2)),
            fq,
            fk,
            state,
            cols,
            visible,
            norms[1],
            (flat[1], (D, D), still(0, 0)),
            (flat[1], (CHUNK, D), lambda i: (1 + i, 0)),
            (flat[1], (CHUNK, D), lambda i: (1 + CHUNKS + i, 0)),
        ],
        [
            ((ROWS, D), F32),
            ((ROWS, D), F32),
            ((ROWS, D), BF),
            ((ROWS, D), F32),
            ((ROWS, D), BF),
            ((ROWS, FF), F32, (ROWS, CHUNK), lambda i: (0, i)),
            ((ROWS, FF), BF, (ROWS, CHUNK), lambda i: (0, i)),
            ((ROWS, D), F32),
        ],
        2 * ROWS * 9 * D * D,
    )
    return result, (x, h1, proj, fq, fk, state, o, rden, att, x1, h2, u, g)


def back_call(e, flat, norms, cols, kept):
    x, h1, proj, fq, fk, state, o, rden, att, x1, h2, u, g = kept
    return call(
        back_kernel,
        (CHUNKS,),
        [
            e,
            (u, (ROWS, CHUNK), lambda i: (0, i)),
            x1,
            norms[1],
            (flat[1], (CHUNK, D), lambda i: (1 + CHUNKS + i, 0)),
            (flat[1], (CHUNK, D), lambda i: (1 + i, 0)),
            (flat[1], (D, D), still(0, 0)),
            o,
            rden,
            fq,
            cols,
        ],
        [
            ((ROWS, FF), BF, (ROWS, CHUNK), lambda i: (0, i)),
            ((ROWS, D), F32),
            ((ROWS, D), BF),
            ((ROWS, D), F32),
            ((ROWS, 128), F32),
            (STATE, F32),
            ((2, D), F32),
        ],
        2 * ROWS * 9 * D * D,
        [pltpu.VMEM((ROWS, D), F32)],
    )


def query_call(maps, cols, visible, kept, back):
    proj, fq, fk, state = kept[2:6]
    dn, dd = back[3:5]
    return call(
        query_kernel,
        (1,),
        [
            (proj, (ROWS, D), still(0, 0)),
            (proj, (ROWS, D), still(0, 2)),
            fq,
            fk,
            state,
            dn,
            dd,
            cols,
            visible,
            (maps, (1, PAIRS, 256, 256), still(0, 0, 0, 0)),
        ],
        [((ROWS, D), BF), ((HD, D), F32), ((ROWS, H * 128), F32), ((ROWS, D), F32)],
        2 * ROWS * 4 * D * D,
    )


def sides(net, count):
    side = (4 * D + 2 * FF) // (4 * net.nz)
    shape = (count // (2 * side), side, D)
    return [(shape, BF, (TILE // (2 * side), side, D), lambda i: (i, 0, 0))] * 2


def rows_call(net, e, kept, back):
    att, h2, g = kept[8], kept[10], kept[12]
    du, ebx = back[0], back[2]
    return call(
        rows_kernel,
        ((D + 2 * FF) // TILE,),
        [att, ebx, du, h2, g, e],
        sides(net, D + 2 * FF),
        2 * ROWS * 9 * D * D,
        [pltpu.VMEM((TILE, D), F32)],
    )


def key_call(flat, norms, maps, cols, kept, back, query, state_grad):
    x, proj, fk = kept[0], kept[2], kept[4]
    dx1 = back[1]
    dq, query_map, dfk, dv = query
    return call(
        key_kernel,
        (1,),
        [
            (proj, (ROWS, D), still(0, 1)),
            (proj, (ROWS, D), still(0, 2)),
            fk,
            state_grad,
            dfk,
            dv,
            dq,
            cols,
            (maps, (1, PAIRS, 256, 256), still(1, 0, 0, 0)),
            (flat[0], (3 * D, D), still(0, 0)),
            x,
            norms[0],
            dx1,
        ],
        [((ROWS, 3 * D), BF), ((HD, D), F32), ((ROWS, D), F32), ((2, D), F32)],
        2 * ROWS * 3 * D * D,
    )


def proj_rows_call(net, kept, dqkv):
    return call(
        proj_rows_kernel,
        (3 * D // TILE,),
        [(dqkv, (ROWS, TILE), lambda i: (0, i)), kept[1]],
        sides(net, 3 * D),
        2 * ROWS * 3 * D * D,
        [pltpu.VMEM((TILE, D), F32)],
    )


def pair_maps(fmap):
    grid = fmap.reshape(LAYERS, 2, HD, PAIRS, 2, HD).transpose(0, 1, 3, 4, 2, 5)
    both = jnp.concatenate([grid, -grid], axis=-1)
    empty = jnp.zeros_like(both[:, :, :, 0])
    top = jnp.concatenate([both[:, :, :, 0], empty], axis=-1)
    bottom = jnp.concatenate([empty, both[:, :, :, 1]], axis=-1)
    return jnp.concatenate(two(jnp.concatenate([top, bottom], axis=3)), axis=3)


def doc_layout(doc_lengths, start, span):
    ends = jnp.cumsum(doc_lengths, axis=1)
    places = start + jnp.arange(span, dtype=jnp.int32)
    documents = jnp.sum((places[None, :, None] >= ends[:, None, :]).astype(jnp.int32), axis=2)
    before = jnp.sum((start - 1 >= ends).astype(jnp.int32), axis=1)
    previous = jnp.where(start > 0, before, -1)
    mark = (documents == previous[:, None]).reshape(-1, 1)
    last = (documents == documents[:, span - 1 :]).reshape(-1, 1)
    lane = jnp.arange(128)[None, :]
    cols = jnp.where(lane == 0, mark, (lane == 1) & last).astype(F32)
    names = (documents + (DOCS + 1) * jnp.arange(documents.shape[0])[:, None]).reshape(-1)
    lower = jnp.arange(names.shape[0])[:, None] >= jnp.arange(names.shape[0])[None, :]
    visible = (lower & (names[:, None] == names[None, :])).astype(F32)
    return cols, visible


def body(tokens, doc_lengths, weights, norm_gain, norm_bias, fmap, cotangent):
    net = Net()
    sequences, span = tokens.shape[:2]
    start = lax.axis_index("seq") * span
    rows = sequences * span
    def prepare(doc_lengths, fmap, norm_gain, norm_bias, tokens, cotangent):
        cols, visible = doc_layout(doc_lengths, start, span)
        last_doc = last_docs(doc_lengths, span)
        gates = [scan_gates(net, last_doc, reverse) for reverse in (False, True)]
        maps = pair_maps(fmap)
        norms = jnp.stack([norm_gain, norm_bias], axis=2)
        x, e = [array.reshape(rows, D).astype(F32) for array in (tokens, cotangent)]
        return cols, visible, gates, maps, norms, x, e

    given = (doc_lengths, fmap, norm_gain, norm_bias, tokens, cotangent)
    steps = len(list(doublings(net.nz)))
    if net.nz == 4 and net.nb == 2 and weights.shape[1] % 32 == 0:
        first, second = [Gather(net, weights[layer]) for layer in range(LAYERS)]
        half = first.half
        own = first.shard[None]
        sides = first.sides(own)
        next_z = [first.along_z(first.shard, step) for step in (1, 3)]
        own, sides, shard = tie(own, sides, first.shard)
        corners = first.corners(first.cuts(sides))
        prepared = prepare(*given)
        own, sides, corners, next_z, shard, prepared = tie(own, sides, corners, next_z, shard, prepared)
        cols, visible, gates, maps, norms, x, e1 = prepared
        far = first.along_z(shard, 2)[None]
        next_z = jnp.stack(next_z)
        next_sides = first.sides(next_z)
        packed = jnp.concatenate([own, *sides, jnp.concatenate(corners, axis=1)], axis=0)
        swapped = net.core(packed)
        next_z, next_sides, far, shard, swapped = tie(next_z, next_sides, far, second.shard, swapped)
        spots = [(0, 0, 0, 0), (0, 0, 1, 0), (0, 1, 0, 0), (0, 1, 1, 0)]
        first.note(swapped, spots, 1)
        for array, spot in zip((own, *sides, *corners), spots + [(0, 1, 1, half)]):
            first.note(array, [spot])

        next_cuts = [cut.reshape(far.shape) for cut in first.cuts(next_sides)]
        cuts = [jnp.concatenate([cut, far], axis=0) for cut in next_cuts]
        cuts, next_z, next_sides = tie(cuts, next_z, next_sides)
        over_y, over_b = first.corners(cuts)
        second_z = [second.along_z(shard, step) for step in (1, 3)]
        packed = jnp.concatenate([next_z, *next_sides], axis=0)
        swapped = net.core(packed)
        over_y, over_b, second_z, swapped, far = tie(over_y, over_b, second_z, swapped, far)
        spots = [(step, *apart, 0) for apart in ((0, 0), (0, 1), (1, 0)) for step in (1, 3)]
        first.note(swapped, spots, 1)
        for index, array in enumerate((next_z, *next_sides)):
            first.note(array, spots[2 * index : 2 * index + 2])

        cuts = over_b[1:, :half], over_y[1:, half:]
        corners = first.corners(cuts)
        swapped = [net.core(array) for array in (over_y, over_b, far)]
        own = shard[None]
        second_z.append(second.along_z(shard, 2))
        corners, swapped = tie(corners, swapped)
        spots = [(1, 1, 1, 0), (3, 1, 1, 0)], [(1, 1, 1, half), (3, 1, 1, half)]
        sides = [(2, 1, 0, 0)], [(2, 0, 1, 0)]
        for index, array in enumerate((over_y, over_b)):
            for kept, apart in ((array, 0), (swapped[index], 1)):
                first.note_pair(kept, spots[index], sides[index], apart)
        first.both(far, swapped[2], [(2, 0, 0, 0)])
        for array, row in zip(corners, (0, half)):
            first.both(array, net.core(array), [(2, 1, 1, row)])

        sides = second.sides(own)
        kept0 = head_call(x, None, norms[0], maps[0], cols, first)
        scan = scan_steps(net, kept0[4], gates[0], False)
        came = next(scan)
        came, own, sides, second_z = tie(came, own, sides, second_z)
        corners = second.corners(second.cuts(sides))
        second_z = jnp.stack(second_z)
        came = scan.send(came)
        came, own, sides, corners, second_z = tie(came, own, sides, corners, second_z)
        second_sides = second.sides(second_z)
        packed = jnp.concatenate([own, *sides, jnp.concatenate(corners, axis=1)], axis=0)
        for _ in range(steps):
            came = scan.send(came)
        rest = first.rows(1, net.nz)
        came, rest = tie(came, rest)
        came = scan.send(came)
        came, second_z, second_sides, packed = tie(came, second_z, second_sides, packed)
        second_corners = second.corners(second.cuts(second_sides))
        swapped = net.core(packed), net.core(jnp.concatenate([second_z, *second_sides], axis=0))
        state = finish(scan, came)
        x1, kept0 = tail_call(x, (None, rest), norms[0], cols, visible, kept0, state)
        x1, second_corners, swapped = tie(x1, second_corners, swapped)
        spots = [(0, 0, 0, 0), (0, 0, 1, 0), (0, 1, 0, 0), (0, 1, 1, 0)]
        second.note(swapped[0], spots, 1)
        for array, spot in zip((own, *sides, *corners), spots + [(0, 1, 1, half)]):
            second.note(array, [spot])
        spots = [(step, *apart, 0) for apart in ((0, 0), (0, 1), (1, 0)) for step in (1, 3, 2)]
        second.note(swapped[1], spots, 1)
        for index, array in enumerate((second_z, *second_sides)):
            second.note(array, spots[3 * index : 3 * index + 3])
        for array, row in zip(second_corners, (0, half)):
            second.both(array, net.core(array), [(step, 1, 1, row) for step in (1, 3, 2)])
        gathered = [rest]
        kept1 = head_call(x1, None, norms[1], maps[1], cols, second)
        scan = scan_steps(net, kept1[4], gates[0], False)
        came = next(scan)
        came, head = tie(came, first.rows(0, 1))
        gathered[0] = (head, rest)
        came = scan.send(came)
        head = second.rows(0, 1)
        came, head = tie(came, head)
        came = scan.send(came)
        for _ in range(1, steps):
            came = scan.send(came)
        rest = second.rows(1, net.nz)
        came, rest = tie(came, rest)
        state = finish(scan, came)
        gathered.append((head, rest))
    else:
        gathered = [lax.all_gather(weights[layer], AXES, axis=0, tiled=True) for layer in range(LAYERS)]
        gathered = [(flat[: 3 * D], flat[3 * D :]) for flat in gathered]
        cols, visible, gates, maps, norms, x, e1 = prepare(*given)
        kept0 = head_call(x, gathered[0], norms[0], maps[0], cols)
        state = finish(scan_steps(net, kept0[4], gates[0], False), None)
        x1, kept0 = tail_call(x, gathered[0], norms[0], cols, visible, kept0, state)
        kept1 = head_call(x1, gathered[1], norms[1], maps[1], cols)
        state = finish(scan_steps(net, kept1[4], gates[0], False), None)
    x, kept1 = tail_call(x1, gathered[1], norms[1], cols, visible, kept1, state)
    result = x.astype(BF).reshape(tokens.shape)
    cut = net.nz * 3 * D // (4 * D + 2 * FF)
    rest_sum = Scatter(net, cut, net.nz, 9)
    both_sum = Scatter(net, 0, net.nz, 9)
    head_sum = Scatter(net, 0, cut)

    back1 = back_call(e1, gathered[1], norms[1], cols, kept1)
    scan = scan_steps(net, back1[5], gates[1], True)
    came = next(scan)
    came, held = tie(came, e1)
    came = scan.send(came)
    keep, send = rows_call(net, held, kept1, back1)
    came, keep, send, back1 = tie(came, keep, send, back1)
    came = scan.send(came)
    swapped = net.core(send)
    query1 = query_call(maps[1], cols, visible, kept1, back1)
    came, query1, keep, swapped = tie(came, query1, keep, swapped)
    for _ in range(1, len(list(doublings(net.nz)))):
        came = scan.send(came)
    tops, bottoms = rest_sum.split([(keep, swapped)])
    came, tops, bottoms = tie(came, tops, bottoms)
    came = scan.send(came)
    came, bottoms = tie(came, bottoms)
    rest1 = rest_sum.first_send((tops, bottoms))
    state_grad = finish(scan, came)
    dqkv1, key_map1, e0, norm_one1 = key_call(
        gathered[1], norms[1], maps[1], cols, kept1, back1, query1, state_grad
    )
    small1 = jnp.concatenate([query1[1], key_map1, norm_one1, back1[6]], axis=0)

    back0 = back_call(e0, gathered[0], norms[0], cols, kept0)
    back0, dqkv1 = tie(back0, dqkv1)
    scan = scan_steps(net, back0[5], gates[1], True)
    came = next(scan)
    keep1, send1 = proj_rows_call(net, kept1, dqkv1)
    came, keep1, send1, held = tie(came, keep1, send1, e0)
    came = scan.send(came)
    swapped1 = net.core(send1)
    keep0, send0 = rows_call(net, held, kept0, back0)
    came, keep0, send0, rest1 = tie(came, keep0, send0, rest1)
    came = scan.send(came)
    swapped0 = net.core(send0)
    rest1 = rest_sum.first_add(rest1)
    came, rest1, keep0, swapped0, keep1, swapped1 = tie(came, rest1, keep0, swapped0, keep1, swapped1)
    for _ in range(1, len(list(doublings(net.nz)))):
        came = scan.send(came)
    rest1 = rest_sum.second_send(rest1)
    tops, bottoms = both_sum.split([(keep1, swapped1), (keep0, swapped0)])
    came, tops, bottoms, back0, rest1 = tie(came, tops, bottoms, back0, rest1)
    came = scan.send(came)
    query0 = query_call(maps[0], cols, visible, kept0, back0)
    rest1 = rest_sum.second_add(rest1)
    came, bottoms, query0, rest1 = tie(came, bottoms, query0, rest1)
    both = both_sum.first_send((tops, bottoms))
    rest1 = rest_sum.z_halves(rest1)
    apart = next(rest1)
    state_grad = finish(scan, came)
    dqkv0, key_map0, e, norm_one0 = key_call(
        gathered[0], norms[0], maps[0], cols, kept0, back0, query0, state_grad
    )

    small0 = jnp.concatenate([query0[1], key_map0, norm_one0, back0[6]], axis=0)
    summing = sum_steps(net, jnp.stack([small0, small1]))
    small = next(summing)
    keep, send = proj_rows_call(net, kept0, dqkv0)
    both, keep, send = tie(both, keep, send)
    both = both_sum.first_add(both)
    both, send, apart, small = tie(both, send, apart, small)
    both = both_sum.second_send(both)
    swapped = net.core(send)
    apart = rest1.send(apart)
    small = summing.send(small)
    head0 = head_sum.split([(keep, swapped)])
    head0, apart = tie(head0, apart)
    both = after(both, head0)
    head0 = head_sum.first_send(head0)
    rest1 = finish(rest1, apart)
    both = both_sum.second_add(both)
    both, small = tie(both, small)
    both = both_sum.z_sum(both)
    far = next(both)
    head0 = head_sum.first_add(head0)
    small = summing.send(after(small, head0))
    small, far = tie(small, far)
    near = both.send(far)
    head0 = head_sum.second_add(head_sum.second_send(head0))
    if cut == 1:
        head0 = head_sum.z_tree(head0)
    else:
        head0 = head_sum.z_sum(head0)
    came = next(head0)
    came, near = tie(came, near)
    both = finish(both, near)
    head0 = finish(head0, came)
    small = finish(summing, small)

    both = add_up(both)
    shards = [
        jnp.where(net.z < cut, add_up(head0), both),
        jnp.where(net.z < cut, both, add_up(rest1)),
    ]
    cut = 2 * HD
    return (
        result,
        e.reshape(tokens.shape),
        jnp.stack(shards),
        small[:, cut::2],
        small[:, cut + 1 :: 2],
        small[:, :cut].reshape(fmap.shape),
    )


def solution(mesh):
    in_specs = (
        P("batch", "seq", None),
        P("batch", None),
        P(None, ("seq", "batch"), None),
        P(),
        P(),
        P(),
        P("batch", "seq", None),
    )
    out_specs = (
        P("batch", "seq", None),
        P("batch", "seq", None),
        P(None, ("seq", "batch"), None),
        P(),
        P(),
        P(),
    )
    return jax.shard_map(body, mesh=mesh, in_specs=in_specs, out_specs=out_specs, check_vma=False)
```

```python
import functools

import jax
import jax.numpy as jnp
from jax import lax
from jax.experimental import pallas as pl
from jax.experimental.pallas import tpu as pltpu
from jax.sharding import PartitionSpec as P

D = 768
H = 12
HD = 64
FF = 3072
LAYERS = 2
DOCS = 4
EPSILON = 1e-05
F32 = jnp.float32
BF = jnp.bfloat16
PAIRS = H // 2
WIDE_LIMIT = 40 * 1024 * 1024


AXES = ("seq", "batch")


class Net:
    def __init__(self):
        self.nz = lax.axis_size("seq") // 4
        self.nb = lax.axis_size("batch")
        place = lax.axis_index("seq")
        self.z = place // 4
        self.y = (place // 2) % 2
        self.c = place % 2
        self.b = lax.axis_index("batch")

    def move(self, array, target):
        pairs = []
        for index in range(self.nz * 4 * self.nb):
            place = index // self.nb
            goal = target(place // 4, (place // 2) % 2, place % 2, index % self.nb)
            if goal is not None:
                z, y, c, b = goal
                pairs.append((index, ((z * 2 + y) * 2 + c) * self.nb + b))
        return lax.ppermute(array, AXES, pairs)

    def core(self, array):
        return self.move(array, lambda z, y, c, b: (z, y, 1 - c, b))

    def flip_y(self, array):
        return self.move(array, lambda z, y, c, b: (z, 1 - y, c, b))

    def turn_b(self, array, step):
        return self.move(array, lambda z, y, c, b: (z, y, c, (b + step) % self.nb))

    def shift_z(self, array, step):
        def target(z, y, c, b):
            return (z + step, y, c, b) if 0 <= z + step < self.nz else None

        return self.move(array, target)


def pick(array, index, axis=0):
    return lax.dynamic_index_in_dim(array, index, axis, False)


def last_docs(doc_lengths, span):
    ends = jnp.cumsum(doc_lengths, axis=1)

    def last_doc(block):
        found = jnp.sum(((block + 1) * span - 1 >= ends).astype(jnp.int32), axis=1)
        return jnp.where(block < 0, -1, found)

    return last_doc


def doublings(count):
    step = 1
    while step < count:
        yield step
        step *= 2


def scan_gates(net, last_doc, reverse):
    base = 4 * net.z
    first = base + 2 * net.y
    if reverse:
        pairs = [(first, first - 1), (base + 1, base - 1), (base + 3, base + 1), (first + 1, first)]
        for step in doublings(net.nz):
            pairs += [(4 * (net.z + step) - 1, base + 3), (4 * (net.z + step) - 1, base - 1)]
    else:
        pairs = [(first, first + 1), (base + 1, base + 3), (base - 1, base + 1), (first - 1, first)]
        for step in doublings(net.nz):
            pairs += [(4 * (net.z - step) + 3, base - 1), (4 * (net.z - step) + 3, base + 3)]
    same = jnp.stack([last_doc(a) == last_doc(b) for a, b in pairs])
    return pick(same, net.c, 1).astype(F32)


def scan_steps(net, packed, gates, reverse):
    wide = F32
    low = F32
    mine = pick(packed, net.c)
    theirs = yield net.core(pick(packed, 1 - net.c))
    zero = jnp.equal(net.c, 0)
    part0 = jnp.where(zero, mine, theirs).astype(wide)
    part1 = jnp.where(zero, theirs, mine).astype(wide)
    if reverse:
        chip = part0 + gates[0] * part1
    else:
        chip = gates[0] * part0 + part1
    chip = chip.astype(low)
    own = pick(chip, net.y)
    other = yield net.flip_y(pick(chip, 1 - net.y))
    down = jnp.equal(net.y, 0)
    row0 = jnp.where(down, own, other).astype(wide)
    row1 = jnp.where(down, other, own).astype(wide)
    if reverse:
        plane = row0 + gates[1] * row1
    else:
        plane = gates[1] * row0 + row1
    entering = jnp.zeros(plane.shape, wide)
    for index, step in enumerate(doublings(net.nz)):
        part = yield net.shift_z(plane, -step if reverse else step)
        entering = entering + gates[4 + 2 * index] * part
        plane = plane + gates[5 + 2 * index] * part
    if reverse:
        row1_in = entering
        row0_in = gates[2] * entering + row1
    else:
        row0_in = entering
        row1_in = gates[2] * entering + row0
    own_in = jnp.where(down, row0_in, row1_in)
    other_in = yield net.flip_y(jnp.where(down, row1_in, row0_in).astype(low))
    other_in = other_in.astype(wide)
    chip_in = jnp.where(down, jnp.stack([own_in, other_in]), jnp.stack([other_in, own_in]))
    if reverse:
        core1_in = chip_in
        core0_in = gates[3] * chip_in + part1
    else:
        core0_in = chip_in
        core1_in = gates[3] * chip_in + part0
    core0_in = core0_in.astype(low)
    core1_in = core1_in.astype(low)
    kept = jnp.where(zero, core0_in, core1_in)
    sent = yield net.core(jnp.where(zero, core1_in, core0_in))
    return jnp.where(zero, jnp.stack([kept, sent]), jnp.stack([sent, kept]))


def finish(steps, value):
    while True:
        try:
            value = steps.send(value)
        except StopIteration as stop:
            return stop.value


def after(value, *conditions):
    return lax.optimization_barrier((value, conditions))[0]


def tie(*groups):
    return lax.optimization_barrier(groups)


class Gather:
    def __init__(self, net, shard):
        self.net = net
        self.shard = shard
        self.half = shard.shape[0] // 2
        self.arrays = []
        self.parts = []

    def along_z(self, shard, step):
        return self.net.move(shard, lambda z, y, c, b: ((z + step) % self.net.nz, y, c, b))

    def sides(self, blocks):
        return self.net.turn_b(blocks, 1), self.net.flip_y(blocks)

    def cuts(self, sides):
        return sides[0][:, : self.half], sides[1][:, self.half :]

    def corners(self, cuts):
        return self.net.flip_y(cuts[0]), self.net.turn_b(cuts[1], 1)

    def note(self, array, spots, apart=0):
        size = array.shape[0] * array.shape[1] // len(spots)
        for number, (below, y, b, row) in enumerate(spots):
            index, start = divmod(number * size, array.shape[1])
            self.parts.append((len(self.arrays), index, start, size, below, y, b, apart, row))
        self.arrays.append(array)

    def note_pair(self, array, halves, block, apart):
        number = len(self.arrays)
        size = 2 * self.half
        for index, (below, y, b, row) in enumerate(halves):
            self.parts.append((number, 0, index * self.half, self.half, below, y, b, apart, row))
        for below, y, b, row in block:
            self.parts.append((number, 1, 0, size, below, y, b, apart, row))
        self.arrays.append(array)

    def both(self, array, swapped, spots):
        self.note(array, spots)
        self.note(swapped, spots, 1)

    def rows(self, first, last):
        size = self.shard.shape[0]
        blocks = (last - first) * 4 * self.net.nb
        return pl.pallas_call(
            functools.partial(place_kernel, self.parts, first, last, size),
            in_specs=[pl.BlockSpec(memory_space=pl.ANY)] * len(self.arrays),
            out_specs=pl.BlockSpec(memory_space=pl.ANY),
            out_shape=jax.ShapeDtypeStruct((blocks * size, D), BF),
            scratch_shapes=[
                pltpu.VMEM((blocks * size, D), BF),
                pltpu.SemaphoreType.DMA((last - first, 10)),
                pltpu.SemaphoreType.DMA((last - first,)),
            ],
            compiler_params=pltpu.CompilerParams(vmem_limit_bytes=60 * 1024 * 1024),
            cost_estimate=pl.CostEstimate(flops=0, bytes_accessed=blocks * size * D * 4, transcendentals=0),
        )(*self.arrays)


def block_copies(parts, first, size, arrays, held, sems):
    place = lax.axis_index("seq")
    z = place // 4
    y = lax.rem(place // 2, 2)
    c = lax.rem(place, 2)
    b = lax.axis_index("batch")

    def each(plane, act):
        for below in range(4):
            chosen = [part for part in parts if part[4] == below]

            @pl.when(lax.rem(z - plane + 4, 4) == below)
            def _(chosen=chosen):
                for number, (array, index, start, rows, _, dy, db, dc, offset) in enumerate(chosen):
                    row = (lax.rem(y + dy, 2) * 2 + lax.rem(c + dc, 2)) * 2 + lax.rem(b + db, 2)
                    goal = pl.multiple_of((plane - first) * 8 * size + row * size + offset, 16)
                    source = arrays[array].at[index, pl.ds(start, rows)]
                    target = held.at[pl.ds(goal, rows)]
                    act(pltpu.make_async_copy(source, target, sems.at[plane - first, number]))

    return each


def place_kernel(parts, first, last, size, *refs):
    arrays, (out, held, in_sems, out_sems) = refs[:-4], refs[-4:]
    each = block_copies(parts, first, size, arrays, held, in_sems)
    plane_rows = 8 * size

    def output(plane):
        rows = pl.ds((plane - first) * plane_rows, plane_rows)
        return pltpu.make_async_copy(held.at[rows], out.at[rows], out_sems.at[plane - first])

    for plane in range(first, last):
        each(plane, lambda copy: copy.start())
    for plane in range(first, last):
        each(plane, lambda copy: copy.wait())
        output(plane).start()
    for plane in range(first, last):
        output(plane).wait()


class Scatter:
    def __init__(self, net, first, last, share=9):
        self.net = net
        self.first = first
        self.last = last
        self.share = share

    def split(self, pairs):
        net = self.net
        if (pairs[0][0].shape[1] // net.nb) % 32 == 0:
            return split_call(net, pairs, self.share)
        total = jnp.concatenate([(a.astype(F32) + b.astype(F32)).astype(BF) for a, b in pairs], axis=0)
        total = total.reshape(self.last - self.first, 2, net.nb, -1, D)
        cut = total.shape[3] * self.share // 18
        top = total[:, :, :, :cut]
        bottom = total[:, :, :, cut:]
        return (
            [pick(top, (net.b + step) % net.nb, 2) for step in range(net.nb)],
            [pick(bottom, net.y, 1), pick(bottom, 1 - net.y, 1)],
        )

    def send_b(self, parts):
        return [parts[0]] + [self.net.turn_b(parts[step], step) for step in range(1, self.net.nb)]

    def send_y(self, parts):
        return [parts[0], self.net.flip_y(parts[1])]

    def first_send(self, buffers):
        return self.send_b(buffers[0]), self.send_y(buffers[1])

    def first_add(self, came):
        net = self.net
        if net.nb == 2 and came[0][0].shape[2] % 16 == 0 and came[1][0].shape[2] % 16 == 0:
            return fold_call(came)
        top = add_up(came[0]).astype(BF)
        bottom = add_up(came[1]).astype(BF)
        return (
            [pick(top, net.y, 1), pick(top, 1 - net.y, 1)],
            [pick(bottom, (net.b + step) % net.nb, 1) for step in range(net.nb)],
        )

    def second_send(self, buffers):
        return self.send_y(buffers[0]), self.send_b(buffers[1])

    def second_add(self, came):
        return jnp.concatenate([add_up(part).astype(BF) for part in came], axis=1)

    def z_send(self, rows, steps):
        net = self.net
        limit = self.last - self.first - 1
        came = []
        for step in steps:
            part = pick(rows, jnp.clip((net.z + step) % net.nz - self.first, 0, limit))

            def target(z, y, c, b, step=step):
                goal = (z + step) % net.nz
                return (goal, y, c, b) if self.first <= goal < self.last else None

            came.append(net.move(part, target) if step else part)
        return came

    def z_halves(self, rows):
        net = self.net
        empty = [jnp.zeros((count,) + rows.shape[1:], BF) for count in (self.first, net.nz - self.last)]
        rows = jnp.concatenate([empty[0], rows, empty[1]], axis=0)
        step = net.nz // 2
        while step:
            upper = (net.z // step) % 2
            halves = rows.reshape((2, step) + rows.shape[1:])
            kept = pick(halves, upper)
            came = yield net.move(pick(halves, 1 - upper), lambda z, y, c, b, step=step: (z ^ step, y, c, b))
            rows = (kept.astype(F32) + came.astype(F32)).astype(BF)
            step //= 2
        return [rows[0]]

    def z_tree(self, rows):
        total = rows[0]
        for step in doublings(self.net.nz):

            def target(z, y, c, b, step=step):
                far = (z - self.first) % self.net.nz
                return ((z - step) % self.net.nz, y, c, b) if far % (2 * step) == step else None

            came = yield self.net.move(total, target)
            total = (total.astype(F32) + came.astype(F32)).astype(BF)
        return [total]

    def z_sum(self, rows):
        half = self.net.nz // 2
        came = yield self.z_send(rows, [half])
        rest = yield self.z_send(rows, [step for step in range(1, self.net.nz) if step != half])
        return came + rest + self.z_send(rows, [0])


def add_up(parts):
    return sum(part.astype(F32) for part in parts)


def sum_steps(net, array):
    targets = []
    for step in doublings(net.nz):
        targets.append(lambda z, y, c, b, step=step: (z ^ step, y, c, b))
    for step in doublings(net.nb):
        targets.append(lambda z, y, c, b, step=step: (z, y, c, b ^ step))
    targets.append(lambda z, y, c, b: (z, y, 1 - c, b))
    targets.append(lambda z, y, c, b: (z, 1 - y, c, b))
    for target in targets:
        array = array.astype(BF)
        came = yield net.move(array, target)
        array = array.astype(F32) + came.astype(F32)
    return array


def nn(a, b):
    return lax.dot_general(a, b, (((1,), (0,)), ((), ())), preferred_element_type=F32)


def nt(a, b):
    return lax.dot_general(a, b, (((1,), (1,)), ((), ())), preferred_element_type=F32)


def tn(a, b):
    return lax.dot_general(a, b, (((0,), (0,)), ((), ())), preferred_element_type=F32)


def two(a):
    high = a.astype(BF)
    return high, (a - high.astype(F32)).astype(BF)


def left_half(shape):
    return lax.broadcasted_iota(jnp.int32, shape, 1) < 64


def normed(values, gain, bias):
    mean = jnp.mean(values, axis=1, keepdims=True)
    centred = values - mean
    variance = jnp.mean(centred * centred, axis=1, keepdims=True)
    return centred * lax.rsqrt(variance + EPSILON) * gain + bias


def normed_back(values, gain, upstream):
    mean = jnp.mean(values, axis=1, keepdims=True)
    centred = values - mean
    variance = jnp.mean(centred * centred, axis=1, keepdims=True)
    scale = lax.rsqrt(variance + EPSILON)
    unit = centred * scale
    inner = upstream * gain
    grad = scale * (
        inner
        - jnp.mean(inner, axis=1, keepdims=True)
        - unit * jnp.mean(inner * unit, axis=1, keepdims=True)
    )
    return grad, jnp.sum(upstream * unit, axis=0, keepdims=True), jnp.sum(upstream, axis=0, keepdims=True)


def softmax_halves(values):
    left = left_half(values.shape)
    low = jnp.float32(-jnp.inf)
    top0 = jnp.max(jnp.where(left, values, low), axis=1, keepdims=True)
    top1 = jnp.max(jnp.where(left, low, values), axis=1, keepdims=True)
    raised = jnp.exp(values - jnp.where(left, top0, top1))
    sum0 = jnp.sum(jnp.where(left, raised, 0.0), axis=1, keepdims=True)
    sum1 = jnp.sum(jnp.where(left, 0.0, raised), axis=1, keepdims=True)
    return raised / jnp.where(left, sum0, sum1)


def softmax_halves_back(weights, upstream):
    left = left_half(weights.shape)
    product = weights * upstream
    sum0 = jnp.sum(jnp.where(left, product, 0.0), axis=1, keepdims=True)
    sum1 = jnp.sum(jnp.where(left, 0.0, product), axis=1, keepdims=True)
    return product - weights * jnp.where(left, sum0, sum1)


def lanes(ref, head):
    return ref[:, head * 128 : (head + 1) * 128]


def state_at(ref, seq, pair):
    start = pair % 3 * 128
    return ref[seq, pair // 3, start : start + 128, :]


def normaliser_at(ref, head):
    row = H // 2 * HD + head % 6
    parts = [ref[seq, head // 6, row : row + 1, :] for seq in range(2)]
    return jnp.concatenate([jnp.broadcast_to(part, (64, 128)) for part in parts], axis=0)


def store_state(ref, seq, pair, block, row):
    half = pair // 3
    start = pair % 3 * 128
    ref[seq, half, start : start + 64, :] = block[:64, :128]
    ref[seq, half, start + 64 : start + 128, :] = block[64:, 128:]
    tail = H // 2 * HD + pair % 3 * 2
    ref[seq, half, tail : tail + 1, :] = row[:, :128]
    ref[seq, half, tail + 1 : tail + 2, :] = row[:, 128:]


def clear_tail(ref):
    for seq in range(2):
        for half in range(2):
            ref[seq, half, 390:400, :] = jnp.zeros((10, 128), F32)


def head_kernel(gather, x_ref, norm_ref, map_ref, cols_ref, *refs):
    step = pl.program_id(0)
    if gather is None:
        w_ref, h_ref, proj_ref, fq_ref, fk_ref, state_ref = refs
    else:
        arrays, (h_ref, proj_ref, fq_ref, fk_ref, state_ref, held, sems) = refs[:-7], refs[-7:]
        each = block_copies(gather[0], 0, gather[1], arrays, held, sems)

    @pl.when(step == 0)
    def _():
        if gather is not None:
            each(0, lambda copy: copy.start())
        h_ref[...] = normed(x_ref[...], norm_ref[0:1, :], norm_ref[1:2, :]).astype(BF)
        if gather is not None:
            each(0, lambda copy: copy.wait())

    weights = w_ref[...] if gather is None else held[pl.ds(pl.multiple_of(step * D, D), D), :]
    proj_ref[...] = nt(h_ref[...], weights).astype(BF)

    def features(out_ref):
        for pair in range(PAIRS):
            part = lanes(proj_ref, pair)
            before = nn(jnp.concatenate([part, part], axis=1), map_ref[0, pair])
            for side in range(2):
                head = pair * 2 + side
                out_ref[:, head * 128 : (head + 1) * 128] = softmax_halves(
                    before[:, side * 128 : (side + 1) * 128]
                )

    @pl.when(step == 0)
    def _():
        features(fq_ref)

    @pl.when(step == 1)
    def _():
        features(fk_ref)

    @pl.when(step == 2)
    def _():
        clear_tail(state_ref)
        for seq in range(2):
            rows = slice(seq * 64, seq * 64 + 64)
            last = cols_ref[rows, 1:2]
            for pair in range(PAIRS):
                feats = fk_ref[rows, pair * 256 : (pair + 1) * 256].astype(BF).astype(F32) * last
                block = tn(proj_ref[rows, pair * 128 : (pair + 1) * 128], feats.astype(BF))
                store_state(state_ref, seq, pair, block, jnp.sum(feats, axis=0, keepdims=True))


def tail_kernel(
    x_ref, v_ref, fq_ref, fk_ref, state_ref, cols_ref, vis_ref, norm_ref, wo_ref, wu_ref, wd_ref,
    o_ref, rden_ref, att_ref, x1_ref, h2_ref, u_ref, g_ref, out_ref,
):
    @pl.when(pl.program_id(0) == 0)
    def _():
        visible = vis_ref[...]
        mark = cols_ref[:, 0:1]
        left = left_half((128, 128))
        for pair in range(PAIRS):
            value = lanes(v_ref, pair)
            nothing = jnp.zeros_like(value)
            state = [jnp.concatenate(two(state_at(state_ref, seq, pair)), axis=1) for seq in range(2)]
            weights = []
            totals = []
            carried = []
            for side in range(2):
                head = pair * 2 + side
                query = lanes(fq_ref, head).astype(BF)
                score = nt(query, lanes(fk_ref, head).astype(BF)) * visible
                weights.append(score.astype(BF))
                wide = query.astype(F32) * normaliser_at(state_ref, head) * mark
                totals.append(jnp.sum(score + wide, axis=1, keepdims=True))
                twice = jnp.concatenate([query, query], axis=1)
                carried.append(
                    jnp.concatenate([nt(twice[:64], state[0]), nt(twice[64:], state[1])], axis=0)
                )
            number = nn(
                jnp.concatenate(weights, axis=1),
                jnp.concatenate([jnp.where(left, value, nothing), jnp.where(left, nothing, value)], axis=0),
            )
            number = number + mark * jnp.where(left, carried[0], carried[1])
            inverse = 1.0 / jnp.where(left, totals[0], totals[1])
            output = number * inverse
            cut = slice(pair * 128, (pair + 1) * 128)
            o_ref[:, cut] = output
            rden_ref[:, cut] = inverse
            att_ref[:, cut] = output.astype(BF)
        x1 = x_ref[...] + nn(att_ref[...], wo_ref[...])
        x1_ref[...] = x1
        h2_ref[...] = normed(x1, norm_ref[0:1, :], norm_ref[1:2, :]).astype(BF)
        out_ref[...] = x1

    u = nt(h2_ref[...], wu_ref[...])
    u_ref[...] = u
    inner = jnp.tanh(0.7978845608028654 * (u + 0.044715 * (u * u * u)))
    g = (0.5 * u * (1.0 + inner)).astype(BF)
    g_ref[...] = g
    out_ref[...] += nn(g, wd_ref[...])


def back_kernel(
    e_ref, u_ref, x1_ref, norm_ref, wd_ref, wu_ref, wo_ref, o_ref, rden_ref, fq_ref, cols_ref,
    du_ref, dx1_ref, ebx_ref, dn_ref, dd_ref, state_ref, gn_ref, total,
):
    step = pl.program_id(0)
    dg = nt(e_ref[...].astype(BF), wd_ref[...])
    u = u_ref[...]
    inner = jnp.tanh(0.7978845608028654 * (u + 0.044715 * (u * u * u)))
    slope = 0.5 * (1.0 + inner) + (0.5 * u) * (1.0 - inner * inner) * (
        0.7978845608028654 * (1.0 + 0.134145 * (u * u))
    )
    du = (dg * slope).astype(BF)
    du_ref[...] = du
    part = nn(du, wu_ref[...])

    @pl.when(step == 0)
    def _():
        total[...] = part

    @pl.when(step > 0)
    def _():
        total[...] += part

    @pl.when(step == pl.num_programs(0) - 1)
    def _():
        grad, gain, bias = normed_back(x1_ref[...], norm_ref[0:1, :], total[...])
        gn_ref[0:1, :] = gain
        gn_ref[1:2, :] = bias
        dx1 = e_ref[...] + grad
        dx1_ref[...] = dx1
        low = dx1.astype(BF)
        ebx_ref[...] = low
        dn_ref[...] = nt(low, wo_ref[...]).astype(BF).astype(F32) * rden_ref[...]
        left = left_half((128, 128))
        lane = lax.broadcasted_iota(jnp.int32, (128, 128), 1)
        clear_tail(state_ref)
        columns = jnp.zeros((128, 128), F32)
        for pair in range(PAIRS):
            dn = lanes(dn_ref, pair)
            product = dn * lanes(o_ref, pair)
            d0 = -jnp.sum(jnp.where(left, product, 0.0), axis=1, keepdims=True)
            d1 = -jnp.sum(jnp.where(left, 0.0, product), axis=1, keepdims=True)
            columns = jnp.where(lane == pair * 2, d0, jnp.where(lane == pair * 2 + 1, d1, columns))
            for seq in range(2):
                rows = slice(seq * 64, seq * 64 + 64)
                mark = cols_ref[rows, 0:1]
                high, rest = two(dn[rows] * mark)
                feats = fq_ref[rows, pair * 256 : (pair + 1) * 256].astype(BF)
                block = tn(jnp.concatenate([high, rest], axis=0), jnp.concatenate([feats, feats], axis=0))
                wide = feats.astype(F32)
                row = jnp.concatenate(
                    [
                        jnp.sum(wide[:, :128] * (d0[rows] * mark), axis=0, keepdims=True),
                        jnp.sum(wide[:, 128:] * (d1[rows] * mark), axis=0, keepdims=True),
                    ],
                    axis=1,
                )
                store_state(state_ref, seq, pair, block, row)
        dd_ref[...] = columns


def fold_map(pair_weights, low_q):
    left = left_half((128, 128))
    folded = [weight - pltpu.roll(weight, 64, 1) for weight in pair_weights]
    grad = jnp.where(left, folded[0], pltpu.roll(folded[1], 64, 1))
    high, rest = two(grad)
    twice = jnp.concatenate([low_q, low_q], axis=0)
    table = tn(twice, jnp.concatenate([high, rest], axis=0))
    return jnp.where(left[:64], table[:64], table[64:])


def query_kernel(
    q_ref, v_ref, fq_ref, fk_ref, state_ref, dn_ref, dd_ref, cols_ref, vis_ref, map_ref,
    dq_ref, dmap_ref, dfk_ref, dv_ref,
):
    visible = vis_ref[...]
    low_visible = visible.astype(BF)
    mark = cols_ref[:, 0:1]
    left = left_half((128, 128))
    for pair in range(PAIRS):
        value = lanes(v_ref, pair)
        dn = lanes(dn_ref, pair)
        twice = jnp.concatenate([value, value], axis=1)
        state = [two(state_at(state_ref, seq, pair)) for seq in range(2)]
        weights = []
        shifts = []
        turned = []
        for side in range(2):
            head = pair * 2 + side
            wide = lanes(fq_ref, head)
            query = wide.astype(BF)
            key = lanes(fk_ref, head).astype(BF)
            score = (nt(query, key) * visible).astype(BF)
            mine = jnp.where(left, dn, 0.0) if side == 0 else jnp.where(left, 0.0, dn)
            high, rest = two(mine)
            dd = dd_ref[:, head : head + 1]
            shift = (nt(jnp.concatenate([high, rest], axis=1), twice) + dd).astype(BF) * low_visible
            carried = jnp.concatenate(
                [
                    nn(
                        jnp.concatenate([high[rows], high[rows], rest[rows]], axis=1),
                        jnp.concatenate([state[seq][0], state[seq][1], state[seq][0]], axis=0),
                    )
                    for seq, rows in ((0, slice(0, 64)), (1, slice(64, 128)))
                ],
                axis=0,
            )
            dfq = nn(shift, key) + mark * (carried + dd * normaliser_at(state_ref, head))
            dfk_ref[:, head * 128 : (head + 1) * 128] = tn(shift, query)
            weights.append(softmax_halves_back(wide, dfq))
            shifts.append(score)
            turned.append(high)
        cut = slice(pair * 128, (pair + 1) * 128)
        dv_ref[:, cut] = tn(jnp.concatenate(shifts, axis=0), jnp.concatenate(turned, axis=0))
        low = jnp.concatenate(weights, axis=1).astype(BF)
        dq_ref[:, cut] = nt(low, map_ref[0, pair, :128, :]).astype(BF)
        dmap_ref[:, cut] = fold_map(weights, lanes(q_ref, pair))


def key_kernel(
    k_ref, v_ref, fk_ref, state_ref, dfk_ref, dv_ref, dq_ref, cols_ref, map_ref, w_ref, x_ref, norm_ref, dx1_ref,
    dqkv_ref, dmap_ref, e_ref, gn_ref,
):
    last = cols_ref[:, 1:2]
    left = left_half((128, 128))
    dqkv_ref[:, :D] = dq_ref[...]
    for pair in range(PAIRS):
        value = lanes(v_ref, pair)
        nothing = jnp.zeros_like(value)
        state = [two(state_at(state_ref, seq, pair)) for seq in range(2)]
        weights = []
        grads = []
        for side in range(2):
            head = pair * 2 + side
            wide = lanes(fk_ref, head)
            key = wide.astype(BF)
            mine = jnp.where(left, value, nothing) if side == 0 else jnp.where(left, nothing, value)
            carried = []
            turned = []
            for seq, rows in ((0, slice(0, 64)), (1, slice(64, 128))):
                high, rest = state[seq]
                carried.append(
                    nn(
                        jnp.concatenate([mine[rows], mine[rows]], axis=1),
                        jnp.concatenate([high, rest], axis=0),
                    )
                )
                turned.append(nt(key[rows], high))
            carried = jnp.concatenate(carried, axis=0)
            dfk = lanes(dfk_ref, head) + last * (carried + normaliser_at(state_ref, head))
            weights.append(softmax_halves_back(wide, dfk))
            grads.append(jnp.concatenate(turned, axis=0))
        cut = slice(pair * 128, (pair + 1) * 128)
        dv = lanes(dv_ref, pair) + last * jnp.where(left, grads[0], grads[1])
        dqkv_ref[:, 2 * D + pair * 128 : 2 * D + (pair + 1) * 128] = dv.astype(BF)
        low = jnp.concatenate(weights, axis=1).astype(BF)
        dqkv_ref[:, D + pair * 128 : D + (pair + 1) * 128] = nt(low, map_ref[0, pair, :128, :]).astype(BF)
        dmap_ref[:, cut] = fold_map(weights, lanes(k_ref, pair))
    upstream = nn(dqkv_ref[...], w_ref[...])
    grad, gain, bias = normed_back(x_ref[...], norm_ref[0:1, :], upstream)
    gn_ref[0:1, :] = gain
    gn_ref[1:2, :] = bias
    e_ref[...] = dx1_ref[...] + grad


def store_sides(block, keep_ref, send_ref):
    zero = lax.rem(lax.axis_index("seq"), 2) == 0
    groups, size = keep_ref.shape[:2]
    for group in range(groups):
        low = block[group * 2 * size : group * 2 * size + size]
        high = block[group * 2 * size + size : group * 2 * size + 2 * size]
        keep_ref[group] = jnp.where(zero, low, high).astype(BF)
        send_ref[group] = jnp.where(zero, high, low).astype(BF)


def rows_kernel(att_ref, ebx_ref, du_ref, h2_ref, g_ref, e_ref, keep_ref, send_ref, held):
    terms = ((0, D, att_ref, ebx_ref), (D, D + FF, du_ref, h2_ref), (D + FF, D + 2 * FF, g_ref, e_ref))
    for step in range((D + 2 * FF) // TILE):
        start = step * TILE

        @pl.when(pl.program_id(0) == step)
        def _(start=start):
            for first, last, left, right in terms:
                low = max(start, first)
                high = min(start + TILE, last)
                if low < high:
                    held[low - start : high - start, :] = tn(
                        left[:, low - first : high - first], right[...].astype(BF)
                    )
            store_sides(held, keep_ref, send_ref)


def proj_rows_kernel(dqkv_ref, h_ref, keep_ref, send_ref, held):
    held[...] = tn(dqkv_ref[...], h_ref[...])
    store_sides(held, keep_ref, send_ref)


def split_kernel(runs, nb, *refs):
    tops = refs[2 * len(runs) : 2 * len(runs) + nb]
    bottoms = refs[2 * len(runs) + nb :]
    upper, lower = tops[0].shape[2], bottoms[0].shape[2]
    y = lax.rem(lax.axis_index("seq") // 2, 2)
    b = lax.axis_index("batch")
    start = 0
    for index, count in enumerate(runs):
        keep, came = refs[2 * index : 2 * index + 2]

        @pl.when((pl.program_id(0) >= start) & (pl.program_id(0) < start + count))
        def _(keep=keep, came=came):
            def rows(row_y, row_b, offset, count):
                at = pl.ds(pl.multiple_of(row_b * (upper + lower) + offset, 16), count)
                return (keep[row_y, at, :].astype(F32) + came[row_y, at, :].astype(F32)).astype(BF)

            for step, top in enumerate(tops):
                for side in range(2):
                    top[0, side] = rows(side, lax.rem(b + step, nb), 0, upper)
            for step, bottom in enumerate(bottoms):
                for side in range(nb):
                    bottom[0, side] = rows(lax.rem(y + step, 2), side, upper, lower)

        start += count


def split_call(net, pairs, share):
    size = pairs[0][0].shape[1]
    upper = size // net.nb * share // 18
    lower = size // net.nb - upper
    runs = [keep.shape[0] // 2 for keep, _ in pairs]
    planes = sum(runs)
    operands = []
    start = 0
    for pair, count in zip(pairs, runs):

        def index(i, start=start, count=count):
            return (jnp.clip(i - start, 0, count - 1), 0, 0)

        operands += [(array, (2, size, D), index) for array in pair]
        start += count
    outputs = [((planes, 2, upper, D), BF, (1, 2, upper, D), lambda i: (i, 0, 0, 0))] * net.nb
    outputs += [((planes, net.nb, lower, D), BF, (1, net.nb, lower, D), lambda i: (i, 0, 0, 0))] * 2
    parts = call(functools.partial(split_kernel, runs, net.nb), (planes,), operands, outputs, 0)
    return parts[: net.nb], parts[net.nb :]


def fold_kernel(top_keep, top_came, bottom_keep, bottom_came, *outs):
    y = lax.rem(lax.axis_index("seq") // 2, 2)
    b = lax.axis_index("batch")
    for step in range(2):
        at = lax.rem(y + step, 2)
        outs[step][0] = (top_keep[0, at].astype(F32) + top_came[0, at].astype(F32)).astype(BF)
        at = lax.rem(b + step, 2)
        outs[2 + step][0] = (bottom_keep[0, at].astype(F32) + bottom_came[0, at].astype(F32)).astype(BF)


def fold_call(came):
    operands = []
    outputs = []
    for pair in came:
        shape = pair[0].shape
        operands += [(array, (1,) + shape[1:], lambda i: (i, 0, 0, 0)) for array in pair]
        outputs += [((shape[0],) + shape[2:], BF, (1,) + shape[2:], lambda i: (i, 0, 0))] * 2
    parts = call(fold_kernel, (shape[0],), operands, outputs, 0)
    return parts[:2], parts[2:]


def whole(array):
    rank = array.ndim
    return pl.BlockSpec(array.shape, lambda *_: (0,) * rank)


def call(kernel, grid, operands, outputs, flops, scratch=(), free=(), limit=WIDE_LIMIT):
    arrays = []
    in_specs = []
    for operand in operands:
        if isinstance(operand, tuple):
            arrays.append(operand[0])
            in_specs.append(pl.BlockSpec(operand[1], operand[2]))
        else:
            arrays.append(operand)
            in_specs.append(whole(operand))
    arrays += free
    in_specs += [pl.BlockSpec(memory_space=pl.ANY)] * len(free)
    shapes = [jax.ShapeDtypeStruct(out[0], out[1]) for out in outputs]
    out_specs = []
    for out, shape in zip(outputs, shapes):
        out_specs.append(pl.BlockSpec(out[2], out[3]) if len(out) > 2 else whole(shape))
    moved = sum(a.size * a.dtype.itemsize for a in shapes)
    for spec, a in zip(in_specs, arrays):
        moved += a.size * a.dtype.itemsize if a.shape[0] < 6000 else 6 * D * D
    return pl.pallas_call(
        kernel,
        grid=grid,
        in_specs=in_specs,
        out_specs=out_specs,
        out_shape=shapes,
        scratch_shapes=list(scratch),
        compiler_params=pltpu.CompilerParams(vmem_limit_bytes=limit),
        cost_estimate=pl.CostEstimate(flops=flops, bytes_accessed=moved, transcendentals=0),
    )(*arrays)


STATE = (2, 2, H // 2 * HD + 16, 128)
ROWS = 128
CHUNK = D
TILE = 3 * D // 2
CHUNKS = FF // CHUNK


def still(*index):
    return lambda i: index


def head_call(x, flat, norms, maps, cols, gather=None):
    operands = [
        x,
        norms[0],
        (maps, (1, PAIRS, 256, 256), lambda i: (jnp.minimum(i, 1), 0, 0, 0)),
        cols,
    ]
    outputs = [
        ((ROWS, D), BF),
        ((ROWS, 3 * D), BF, (ROWS, D), lambda i: (0, i)),
        ((ROWS, H * 128), F32),
        ((ROWS, H * 128), F32),
        (STATE, F32),
    ]
    flops = 2 * ROWS * 3 * D * D
    if gather is None:
        operands.append((flat[0], (D, D), lambda i: (i, 0)))
        return call(functools.partial(head_kernel, None), (3,), operands, outputs, flops)
    plan = (gather.parts, gather.shard.shape[0])
    scratch = [pltpu.VMEM((3 * D, D), BF), pltpu.SemaphoreType.DMA((1, 10))]
    return call(
        functools.partial(head_kernel, plan), (3,), operands, outputs, flops, scratch, gather.arrays, 60 * 1024 * 1024
    )


def tail_call(x, flat, norms, cols, visible, head, state):
    h1, proj, fq, fk, local = head
    o, rden, att, x1, h2, u, g, result = call(
        tail_kernel,
        (CHUNKS,),
        [
            x,
            (proj, (ROWS, D), still(0, 2)),
            fq,
            fk,
            state,
            cols,
            visible,
            norms[1],
            (flat[1], (D, D), still(0, 0)),
            (flat[1], (CHUNK, D), lambda i: (1 + i, 0)),
            (flat[1], (CHUNK, D), lambda i: (1 + CHUNKS + i, 0)),
        ],
        [
            ((ROWS, D), F32),
            ((ROWS, D), F32),
            ((ROWS, D), BF),
            ((ROWS, D), F32),
            ((ROWS, D), BF),
            ((ROWS, FF), F32, (ROWS, CHUNK), lambda i: (0, i)),
            ((ROWS, FF), BF, (ROWS, CHUNK), lambda i: (0, i)),
            ((ROWS, D), F32),
        ],
        2 * ROWS * 9 * D * D,
    )
    return result, (x, h1, proj, fq, fk, state, o, rden, att, x1, h2, u, g)


def back_call(e, flat, norms, cols, kept):
    x, h1, proj, fq, fk, state, o, rden, att, x1, h2, u, g = kept
    return call(
        back_kernel,
        (CHUNKS,),
        [
            e,
            (u, (ROWS, CHUNK), lambda i: (0, i)),
            x1,
            norms[1],
            (flat[1], (CHUNK, D), lambda i: (1 + CHUNKS + i, 0)),
            (flat[1], (CHUNK, D), lambda i: (1 + i, 0)),
            (flat[1], (D, D), still(0, 0)),
            o,
            rden,
            fq,
            cols,
        ],
        [
            ((ROWS, FF), BF, (ROWS, CHUNK), lambda i: (0, i)),
            ((ROWS, D), F32),
            ((ROWS, D), BF),
            ((ROWS, D), F32),
            ((ROWS, 128), F32),
            (STATE, F32),
            ((2, D), F32),
        ],
        2 * ROWS * 9 * D * D,
        [pltpu.VMEM((ROWS, D), F32)],
    )


def query_call(maps, cols, visible, kept, back):
    proj, fq, fk, state = kept[2:6]
    dn, dd = back[3:5]
    return call(
        query_kernel,
        (1,),
        [
            (proj, (ROWS, D), still(0, 0)),
            (proj, (ROWS, D), still(0, 2)),
            fq,
            fk,
            state,
            dn,
            dd,
            cols,
            visible,
            (maps, (1, PAIRS, 256, 256), still(0, 0, 0, 0)),
        ],
        [((ROWS, D), BF), ((HD, D), F32), ((ROWS, H * 128), F32), ((ROWS, D), F32)],
        2 * ROWS * 4 * D * D,
    )


def sides(net, count):
    side = (4 * D + 2 * FF) // (4 * net.nz)
    shape = (count // (2 * side), side, D)
    return [(shape, BF, (TILE // (2 * side), side, D), lambda i: (i, 0, 0))] * 2


def rows_call(net, e, kept, back):
    att, h2, g = kept[8], kept[10], kept[12]
    du, ebx = back[0], back[2]
    return call(
        rows_kernel,
        ((D + 2 * FF) // TILE,),
        [att, ebx, du, h2, g, e],
        sides(net, D + 2 * FF),
        2 * ROWS * 9 * D * D,
        [pltpu.VMEM((TILE, D), F32)],
    )


def key_call(flat, norms, maps, cols, kept, back, query, state_grad):
    x, proj, fk = kept[0], kept[2], kept[4]
    dx1 = back[1]
    dq, query_map, dfk, dv = query
    return call(
        key_kernel,
        (1,),
        [
            (proj, (ROWS, D), still(0, 1)),
            (proj, (ROWS, D), still(0, 2)),
            fk,
            state_grad,
            dfk,
            dv,
            dq,
            cols,
            (maps, (1, PAIRS, 256, 256), still(1, 0, 0, 0)),
            (flat[0], (3 * D, D), still(0, 0)),
            x,
            norms[0],
            dx1,
        ],
        [((ROWS, 3 * D), BF), ((HD, D), F32), ((ROWS, D), F32), ((2, D), F32)],
        2 * ROWS * 3 * D * D,
    )


def proj_rows_call(net, kept, dqkv):
    return call(
        proj_rows_kernel,
        (3 * D // TILE,),
        [(dqkv, (ROWS, TILE), lambda i: (0, i)), kept[1]],
        sides(net, 3 * D),
        2 * ROWS * 3 * D * D,
        [pltpu.VMEM((TILE, D), F32)],
    )


def pair_maps(fmap):
    grid = fmap.reshape(LAYERS, 2, HD, PAIRS, 2, HD).transpose(0, 1, 3, 4, 2, 5)
    both = jnp.concatenate([grid, -grid], axis=-1)
    empty = jnp.zeros_like(both[:, :, :, 0])
    top = jnp.concatenate([both[:, :, :, 0], empty], axis=-1)
    bottom = jnp.concatenate([empty, both[:, :, :, 1]], axis=-1)
    return jnp.concatenate(two(jnp.concatenate([top, bottom], axis=3)), axis=3)


def doc_layout(doc_lengths, start, span):
    ends = jnp.cumsum(doc_lengths, axis=1)
    places = start + jnp.arange(span, dtype=jnp.int32)
    documents = jnp.sum((places[None, :, None] >= ends[:, None, :]).astype(jnp.int32), axis=2)
    before = jnp.sum((start - 1 >= ends).astype(jnp.int32), axis=1)
    previous = jnp.where(start > 0, before, -1)
    mark = (documents == previous[:, None]).reshape(-1, 1)
    last = (documents == documents[:, span - 1 :]).reshape(-1, 1)
    lane = jnp.arange(128)[None, :]
    cols = jnp.where(lane == 0, mark, (lane == 1) & last).astype(F32)
    names = (documents + (DOCS + 1) * jnp.arange(documents.shape[0])[:, None]).reshape(-1)
    lower = jnp.arange(names.shape[0])[:, None] >= jnp.arange(names.shape[0])[None, :]
    visible = (lower & (names[:, None] == names[None, :])).astype(F32)
    return cols, visible


def body(tokens, doc_lengths, weights, norm_gain, norm_bias, fmap, cotangent):
    net = Net()
    sequences, span = tokens.shape[:2]
    start = lax.axis_index("seq") * span
    rows = sequences * span
    def prepare(doc_lengths, fmap, norm_gain, norm_bias, tokens, cotangent):
        cols, visible = doc_layout(doc_lengths, start, span)
        last_doc = last_docs(doc_lengths, span)
        gates = [scan_gates(net, last_doc, reverse) for reverse in (False, True)]
        maps = pair_maps(fmap)
        norms = jnp.stack([norm_gain, norm_bias], axis=2)
        x, e = [array.reshape(rows, D).astype(F32) for array in (tokens, cotangent)]
        return cols, visible, gates, maps, norms, x, e

    given = (doc_lengths, fmap, norm_gain, norm_bias, tokens, cotangent)
    steps = len(list(doublings(net.nz)))
    if net.nz == 4 and net.nb == 2 and weights.shape[1] % 32 == 0:
        first, second = [Gather(net, weights[layer]) for layer in range(LAYERS)]
        half = first.half
        own = first.shard[None]
        sides = first.sides(own)
        next_z = [first.along_z(first.shard, step) for step in (1, 3)]
        own, sides, shard = tie(own, sides, first.shard)
        corners = first.corners(first.cuts(sides))
        prepared = prepare(*given)
        own, sides, corners, next_z, shard, prepared = tie(own, sides, corners, next_z, shard, prepared)
        cols, visible, gates, maps, norms, x, e1 = prepared
        far = first.along_z(shard, 2)[None]
        next_z = jnp.stack(next_z)
        next_sides = first.sides(next_z)
        packed = jnp.concatenate([own, *sides, jnp.concatenate(corners, axis=1)], axis=0)
        swapped = net.core(packed)
        next_z, next_sides, far, shard, swapped = tie(next_z, next_sides, far, second.shard, swapped)
        spots = [(0, 0, 0, 0), (0, 0, 1, 0), (0, 1, 0, 0), (0, 1, 1, 0)]
        first.note(swapped, spots, 1)
        for array, spot in zip((own, *sides, *corners), spots + [(0, 1, 1, half)]):
            first.note(array, [spot])

        next_cuts = [cut.reshape(far.shape) for cut in first.cuts(next_sides)]
        cuts = [jnp.concatenate([cut, far], axis=0) for cut in next_cuts]
        cuts, next_z, next_sides = tie(cuts, next_z, next_sides)
        over_y, over_b = first.corners(cuts)
        second_z = [second.along_z(shard, step) for step in (1, 3)]
        packed = jnp.concatenate([next_z, *next_sides], axis=0)
        swapped = net.core(packed)
        over_y, over_b, second_z, swapped, far = tie(over_y, over_b, second_z, swapped, far)
        spots = [(step, *apart, 0) for apart in ((0, 0), (0, 1), (1, 0)) for step in (1, 3)]
        first.note(swapped, spots, 1)
        for index, array in enumerate((next_z, *next_sides)):
            first.note(array, spots[2 * index : 2 * index + 2])

        cuts = over_b[1:, :half], over_y[1:, half:]
        corners = first.corners(cuts)
        swapped = [net.core(array) for array in (over_y, over_b, far)]
        own = shard[None]
        second_z.append(second.along_z(shard, 2))
        corners, swapped = tie(corners, swapped)
        spots = [(1, 1, 1, 0), (3, 1, 1, 0)], [(1, 1, 1, half), (3, 1, 1, half)]
        sides = [(2, 1, 0, 0)], [(2, 0, 1, 0)]
        for index, array in enumerate((over_y, over_b)):
            for kept, apart in ((array, 0), (swapped[index], 1)):
                first.note_pair(kept, spots[index], sides[index], apart)
        first.both(far, swapped[2], [(2, 0, 0, 0)])
        for array, row in zip(corners, (0, half)):
            first.both(array, net.core(array), [(2, 1, 1, row)])

        sides = second.sides(own)
        kept0 = head_call(x, None, norms[0], maps[0], cols, first)
        scan = scan_steps(net, kept0[4], gates[0], False)
        came = next(scan)
        came, own, sides, second_z = tie(came, own, sides, second_z)
        corners = second.corners(second.cuts(sides))
        second_z = jnp.stack(second_z)
        came = scan.send(came)
        came, own, sides, corners, second_z = tie(came, own, sides, corners, second_z)
        second_sides = second.sides(second_z)
        packed = jnp.concatenate([own, *sides, jnp.concatenate(corners, axis=1)], axis=0)
        for _ in range(steps):
            came = scan.send(came)
        rest = first.rows(1, net.nz)
        came, rest = tie(came, rest)
        came = scan.send(came)
        came, second_z, second_sides, packed = tie(came, second_z, second_sides, packed)
        second_corners = second.corners(second.cuts(second_sides))
        swapped = net.core(packed), net.core(jnp.concatenate([second_z, *second_sides], axis=0))
        state = finish(scan, came)
        x1, kept0 = tail_call(x, (None, rest), norms[0], cols, visible, kept0, state)
        x1, second_corners, swapped = tie(x1, second_corners, swapped)
        spots = [(0, 0, 0, 0), (0, 0, 1, 0), (0, 1, 0, 0), (0, 1, 1, 0)]
        second.note(swapped[0], spots, 1)
        for array, spot in zip((own, *sides, *corners), spots + [(0, 1, 1, half)]):
            second.note(array, [spot])
        spots = [(step, *apart, 0) for apart in ((0, 0), (0, 1), (1, 0)) for step in (1, 3, 2)]
        second.note(swapped[1], spots, 1)
        for index, array in enumerate((second_z, *second_sides)):
            second.note(array, spots[3 * index : 3 * index + 3])
        for array, row in zip(second_corners, (0, half)):
            second.both(array, net.core(array), [(step, 1, 1, row) for step in (1, 3, 2)])
        gathered = [rest]
        kept1 = head_call(x1, None, norms[1], maps[1], cols, second)
        scan = scan_steps(net, kept1[4], gates[0], False)
        came = scan.send(next(scan))
        came, head = tie(came, first.rows(0, 1))
        gathered[0] = (head, rest)
        came = scan.send(came)
        head = second.rows(0, 1)
        came, head = tie(came, head)
        for _ in range(1, steps):
            came = scan.send(came)
        rest = second.rows(1, net.nz)
        came, rest = tie(came, rest)
        state = finish(scan, came)
        gathered.append((head, rest))
    else:
        gathered = [lax.all_gather(weights[layer], AXES, axis=0, tiled=True) for layer in range(LAYERS)]
        gathered = [(flat[: 3 * D], flat[3 * D :]) for flat in gathered]
        cols, visible, gates, maps, norms, x, e1 = prepare(*given)
        kept0 = head_call(x, gathered[0], norms[0], maps[0], cols)
        state = finish(scan_steps(net, kept0[4], gates[0], False), None)
        x1, kept0 = tail_call(x, gathered[0], norms[0], cols, visible, kept0, state)
        kept1 = head_call(x1, gathered[1], norms[1], maps[1], cols)
        state = finish(scan_steps(net, kept1[4], gates[0], False), None)
    x, kept1 = tail_call(x1, gathered[1], norms[1], cols, visible, kept1, state)
    result = x.astype(BF).reshape(tokens.shape)
    cut = net.nz * 3 * D // (4 * D + 2 * FF)
    rest_sum = Scatter(net, cut, net.nz, 10)
    both_sum = Scatter(net, 0, net.nz, 9)
    head_sum = Scatter(net, 0, cut)

    back1 = back_call(e1, gathered[1], norms[1], cols, kept1)
    scan = scan_steps(net, back1[5], gates[1], True)
    came = next(scan)
    came, held = tie(came, e1)
    came = scan.send(came)
    keep, send = rows_call(net, held, kept1, back1)
    came, keep, send, back1 = tie(came, keep, send, back1)
    came = scan.send(came)
    swapped = net.core(send)
    query1 = query_call(maps[1], cols, visible, kept1, back1)
    came, query1, keep, swapped = tie(came, query1, keep, swapped)
    for _ in range(1, len(list(doublings(net.nz)))):
        came = scan.send(came)
    tops, bottoms = rest_sum.split([(keep, swapped)])
    came, tops, bottoms = tie(came, tops, bottoms)
    came = scan.send(came)
    came, bottoms = tie(came, bottoms)
    rest1 = rest_sum.first_send((tops, bottoms))
    state_grad = finish(scan, came)
    dqkv1, key_map1, e0, norm_one1 = key_call(
        gathered[1], norms[1], maps[1], cols, kept1, back1, query1, state_grad
    )
    small1 = jnp.concatenate([query1[1], key_map1, norm_one1, back1[6]], axis=0)

    back0 = back_call(e0, gathered[0], norms[0], cols, kept0)
    back0, dqkv1 = tie(back0, dqkv1)
    scan = scan_steps(net, back0[5], gates[1], True)
    came = next(scan)
    keep1, send1 = proj_rows_call(net, kept1, dqkv1)
    came, keep1, send1, held = tie(came, keep1, send1, e0)
    came = scan.send(came)
    swapped1 = net.core(send1)
    keep0, send0 = rows_call(net, held, kept0, back0)
    came, keep0, send0, rest1 = tie(came, keep0, send0, rest1)
    came = scan.send(came)
    swapped0 = net.core(send0)
    rest1 = rest_sum.first_add(rest1)
    came, rest1, keep0, swapped0, keep1, swapped1 = tie(came, rest1, keep0, swapped0, keep1, swapped1)
    for _ in range(1, len(list(doublings(net.nz)))):
        came = scan.send(came)
    rest1 = rest_sum.second_send(rest1)
    tops, bottoms = both_sum.split([(keep1, swapped1), (keep0, swapped0)])
    came, tops, bottoms, back0, rest1 = tie(came, tops, bottoms, back0, rest1)
    came = scan.send(came)
    query0 = query_call(maps[0], cols, visible, kept0, back0)
    rest1 = rest_sum.second_add(rest1)
    came, bottoms, query0, rest1 = tie(came, bottoms, query0, rest1)
    both = both_sum.first_send((tops, bottoms))
    rest1 = rest_sum.z_halves(rest1)
    apart = next(rest1)
    state_grad = finish(scan, came)
    dqkv0, key_map0, e, norm_one0 = key_call(
        gathered[0], norms[0], maps[0], cols, kept0, back0, query0, state_grad
    )

    small0 = jnp.concatenate([query0[1], key_map0, norm_one0, back0[6]], axis=0)
    summing = sum_steps(net, jnp.stack([small0, small1]))
    small = next(summing)
    keep, send = proj_rows_call(net, kept0, dqkv0)
    both, keep, send = tie(both, keep, send)
    both = both_sum.first_add(both)
    both, send, apart, small = tie(both, send, apart, small)
    both = both_sum.second_send(both)
    swapped = net.core(send)
    apart = rest1.send(apart)
    small = summing.send(small)
    head0 = head_sum.split([(keep, swapped)])
    head0, apart = tie(head0, apart)
    both = after(both, head0)
    head0 = head_sum.first_send(head0)
    rest1 = finish(rest1, apart)
    both = both_sum.second_add(both)
    both, small = tie(both, small)
    both = both_sum.z_sum(both)
    far = next(both)
    head0 = head_sum.first_add(head0)
    small = summing.send(after(small, head0))
    small, far = tie(small, far)
    near = both.send(far)
    head0 = head_sum.second_add(head_sum.second_send(head0))
    if cut == 1:
        head0 = head_sum.z_tree(head0)
    else:
        head0 = head_sum.z_sum(head0)
    came = next(head0)
    came, near = tie(came, near)
    both = finish(both, near)
    head0 = finish(head0, came)
    small = finish(summing, small)

    both = add_up(both)
    shards = [
        jnp.where(net.z < cut, add_up(head0), both),
        jnp.where(net.z < cut, both, add_up(rest1)),
    ]
    cut = 2 * HD
    return (
        result,
        e.reshape(tokens.shape),
        jnp.stack(shards),
        small[:, cut::2],
        small[:, cut + 1 :: 2],
        small[:, :cut].reshape(fmap.shape),
    )


def solution(mesh):
    in_specs = (
        P("batch", "seq", None),
        P("batch", None),
        P(None, ("seq", "batch"), None),
        P(),
        P(),
        P(),
        P("batch", "seq", None),
    )
    out_specs = (
        P("batch", "seq", None),
        P("batch", "seq", None),
        P(None, ("seq", "batch"), None),
        P(),
        P(),
        P(),
    )
    return jax.shard_map(body, mesh=mesh, in_specs=in_specs, out_specs=out_specs, check_vma=False)
```

```python
import functools

import jax
import jax.numpy as jnp
from jax import lax
from jax.experimental import pallas as pl
from jax.experimental.pallas import tpu as pltpu
from jax.sharding import PartitionSpec as P

D = 768
H = 12
HD = 64
FF = 3072
LAYERS = 2
DOCS = 4
EPSILON = 1e-05
F32 = jnp.float32
BF = jnp.bfloat16
PAIRS = H // 2
WIDE_LIMIT = 40 * 1024 * 1024


AXES = ("seq", "batch")


class Net:
    def __init__(self):
        self.nz = lax.axis_size("seq") // 4
        self.nb = lax.axis_size("batch")
        place = lax.axis_index("seq")
        self.z = place // 4
        self.y = (place // 2) % 2
        self.c = place % 2
        self.b = lax.axis_index("batch")

    def move(self, array, target):
        pairs = []
        for index in range(self.nz * 4 * self.nb):
            place = index // self.nb
            goal = target(place // 4, (place // 2) % 2, place % 2, index % self.nb)
            if goal is not None:
                z, y, c, b = goal
                pairs.append((index, ((z * 2 + y) * 2 + c) * self.nb + b))
        return lax.ppermute(array, AXES, pairs)

    def core(self, array):
        return self.move(array, lambda z, y, c, b: (z, y, 1 - c, b))

    def flip_y(self, array):
        return self.move(array, lambda z, y, c, b: (z, 1 - y, c, b))

    def turn_b(self, array, step):
        return self.move(array, lambda z, y, c, b: (z, y, c, (b + step) % self.nb))

    def shift_z(self, array, step):
        def target(z, y, c, b):
            return (z + step, y, c, b) if 0 <= z + step < self.nz else None

        return self.move(array, target)


def pick(array, index, axis=0):
    return lax.dynamic_index_in_dim(array, index, axis, False)


def last_docs(doc_lengths, span):
    ends = jnp.cumsum(doc_lengths, axis=1)

    def last_doc(block):
        found = jnp.sum(((block + 1) * span - 1 >= ends).astype(jnp.int32), axis=1)
        return jnp.where(block < 0, -1, found)

    return last_doc


def doublings(count):
    step = 1
    while step < count:
        yield step
        step *= 2


def scan_gates(net, last_doc, reverse):
    base = 4 * net.z
    first = base + 2 * net.y
    if reverse:
        pairs = [(first, first - 1), (base + 1, base - 1), (base + 3, base + 1), (first + 1, first)]
        for step in doublings(net.nz):
            pairs += [(4 * (net.z + step) - 1, base + 3), (4 * (net.z + step) - 1, base - 1)]
    else:
        pairs = [(first, first + 1), (base + 1, base + 3), (base - 1, base + 1), (first - 1, first)]
        for step in doublings(net.nz):
            pairs += [(4 * (net.z - step) + 3, base - 1), (4 * (net.z - step) + 3, base + 3)]
    same = jnp.stack([last_doc(a) == last_doc(b) for a, b in pairs])
    return pick(same, net.c, 1).astype(F32)


def scan_steps(net, packed, gates, reverse):
    wide = F32
    low = F32
    mine = pick(packed, net.c)
    theirs = yield net.core(pick(packed, 1 - net.c))
    zero = jnp.equal(net.c, 0)
    part0 = jnp.where(zero, mine, theirs).astype(wide)
    part1 = jnp.where(zero, theirs, mine).astype(wide)
    if reverse:
        chip = part0 + gates[0] * part1
    else:
        chip = gates[0] * part0 + part1
    chip = chip.astype(low)
    own = pick(chip, net.y)
    other = yield net.flip_y(pick(chip, 1 - net.y))
    down = jnp.equal(net.y, 0)
    row0 = jnp.where(down, own, other).astype(wide)
    row1 = jnp.where(down, other, own).astype(wide)
    if reverse:
        plane = row0 + gates[1] * row1
    else:
        plane = gates[1] * row0 + row1
    entering = jnp.zeros(plane.shape, wide)
    for index, step in enumerate(doublings(net.nz)):
        part = yield net.shift_z(plane, -step if reverse else step)
        entering = entering + gates[4 + 2 * index] * part
        plane = plane + gates[5 + 2 * index] * part
    if reverse:
        row1_in = entering
        row0_in = gates[2] * entering + row1
    else:
        row0_in = entering
        row1_in = gates[2] * entering + row0
    own_in = jnp.where(down, row0_in, row1_in)
    other_in = yield net.flip_y(jnp.where(down, row1_in, row0_in).astype(low))
    other_in = other_in.astype(wide)
    chip_in = jnp.where(down, jnp.stack([own_in, other_in]), jnp.stack([other_in, own_in]))
    if reverse:
        core1_in = chip_in
        core0_in = gates[3] * chip_in + part1
    else:
        core0_in = chip_in
        core1_in = gates[3] * chip_in + part0
    core0_in = core0_in.astype(low)
    core1_in = core1_in.astype(low)
    kept = jnp.where(zero, core0_in, core1_in)
    sent = yield net.core(jnp.where(zero, core1_in, core0_in))
    return jnp.where(zero, jnp.stack([kept, sent]), jnp.stack([sent, kept]))


def finish(steps, value):
    while True:
        try:
            value = steps.send(value)
        except StopIteration as stop:
            return stop.value


def after(value, *conditions):
    return lax.optimization_barrier((value, conditions))[0]


def tie(*groups):
    return lax.optimization_barrier(groups)


class Gather:
    def __init__(self, net, shard):
        self.net = net
        self.shard = shard
        self.half = shard.shape[0] // 2
        self.arrays = []
        self.parts = []

    def along_z(self, shard, step):
        return self.net.move(shard, lambda z, y, c, b: ((z + step) % self.net.nz, y, c, b))

    def sides(self, blocks):
        return self.net.turn_b(blocks, 1), self.net.flip_y(blocks)

    def cuts(self, sides):
        return sides[0][:, : self.half], sides[1][:, self.half :]

    def corners(self, cuts):
        return self.net.flip_y(cuts[0]), self.net.turn_b(cuts[1], 1)

    def note(self, array, spots, apart=0):
        size = array.shape[0] * array.shape[1] // len(spots)
        for number, (below, y, b, row) in enumerate(spots):
            index, start = divmod(number * size, array.shape[1])
            self.parts.append((len(self.arrays), index, start, size, below, y, b, apart, row))
        self.arrays.append(array)

    def note_pair(self, array, halves, block, apart):
        number = len(self.arrays)
        size = 2 * self.half
        for index, (below, y, b, row) in enumerate(halves):
            self.parts.append((number, 0, index * self.half, self.half, below, y, b, apart, row))
        for below, y, b, row in block:
            self.parts.append((number, 1, 0, size, below, y, b, apart, row))
        self.arrays.append(array)

    def both(self, array, swapped, spots):
        self.note(array, spots)
        self.note(swapped, spots, 1)

    def rows(self, first, last):
        size = self.shard.shape[0]
        blocks = (last - first) * 4 * self.net.nb
        return pl.pallas_call(
            functools.partial(place_kernel, self.parts, first, last, size),
            in_specs=[pl.BlockSpec(memory_space=pl.ANY)] * len(self.arrays),
            out_specs=pl.BlockSpec(memory_space=pl.ANY),
            out_shape=jax.ShapeDtypeStruct((blocks * size, D), BF),
            scratch_shapes=[
                pltpu.VMEM((blocks * size, D), BF),
                pltpu.SemaphoreType.DMA((last - first, 10)),
                pltpu.SemaphoreType.DMA((last - first,)),
            ],
            compiler_params=pltpu.CompilerParams(vmem_limit_bytes=60 * 1024 * 1024),
            cost_estimate=pl.CostEstimate(flops=0, bytes_accessed=blocks * size * D * 4, transcendentals=0),
        )(*self.arrays)


def block_copies(parts, first, size, arrays, held, sems):
    place = lax.axis_index("seq")
    z = place // 4
    y = lax.rem(place // 2, 2)
    c = lax.rem(place, 2)
    b = lax.axis_index("batch")

    def each(plane, act):
        for below in range(4):
            chosen = [part for part in parts if part[4] == below]

            @pl.when(lax.rem(z - plane + 4, 4) == below)
            def _(chosen=chosen):
                for number, (array, index, start, rows, _, dy, db, dc, offset) in enumerate(chosen):
                    row = (lax.rem(y + dy, 2) * 2 + lax.rem(c + dc, 2)) * 2 + lax.rem(b + db, 2)
                    goal = pl.multiple_of((plane - first) * 8 * size + row * size + offset, 16)
                    source = arrays[array].at[index, pl.ds(start, rows)]
                    target = held.at[pl.ds(goal, rows)]
                    act(pltpu.make_async_copy(source, target, sems.at[plane - first, number]))

    return each


def place_kernel(parts, first, last, size, *refs):
    arrays, (out, held, in_sems, out_sems) = refs[:-4], refs[-4:]
    each = block_copies(parts, first, size, arrays, held, in_sems)
    plane_rows = 8 * size

    def output(plane):
        rows = pl.ds((plane - first) * plane_rows, plane_rows)
        return pltpu.make_async_copy(held.at[rows], out.at[rows], out_sems.at[plane - first])

    for plane in range(first, last):
        each(plane, lambda copy: copy.start())
    for plane in range(first, last):
        each(plane, lambda copy: copy.wait())
        output(plane).start()
    for plane in range(first, last):
        output(plane).wait()


class Scatter:
    def __init__(self, net, first, last, share=9):
        self.net = net
        self.first = first
        self.last = last
        self.share = share

    def split(self, pairs):
        net = self.net
        if (pairs[0][0].shape[1] // net.nb) % 32 == 0:
            return split_call(net, pairs, self.share)
        total = jnp.concatenate([(a.astype(F32) + b.astype(F32)).astype(BF) for a, b in pairs], axis=0)
        total = total.reshape(self.last - self.first, 2, net.nb, -1, D)
        cut = total.shape[3] * self.share // 18
        top = total[:, :, :, :cut]
        bottom = total[:, :, :, cut:]
        return (
            [pick(top, (net.b + step) % net.nb, 2) for step in range(net.nb)],
            [pick(bottom, net.y, 1), pick(bottom, 1 - net.y, 1)],
        )

    def send_b(self, parts):
        return [parts[0]] + [self.net.turn_b(parts[step], step) for step in range(1, self.net.nb)]

    def send_y(self, parts):
        return [parts[0], self.net.flip_y(parts[1])]

    def first_send(self, buffers):
        return self.send_b(buffers[0]), self.send_y(buffers[1])

    def first_add(self, came):
        net = self.net
        if net.nb == 2 and came[0][0].shape[2] % 16 == 0 and came[1][0].shape[2] % 16 == 0:
            return fold_call(came)
        top = add_up(came[0]).astype(BF)
        bottom = add_up(came[1]).astype(BF)
        return (
            [pick(top, net.y, 1), pick(top, 1 - net.y, 1)],
            [pick(bottom, (net.b + step) % net.nb, 1) for step in range(net.nb)],
        )

    def second_send(self, buffers):
        return self.send_y(buffers[0]), self.send_b(buffers[1])

    def second_add(self, came):
        return jnp.concatenate([add_up(part).astype(BF) for part in came], axis=1)

    def z_send(self, rows, steps):
        net = self.net
        limit = self.last - self.first - 1
        came = []
        for step in steps:
            part = pick(rows, jnp.clip((net.z + step) % net.nz - self.first, 0, limit))

            def target(z, y, c, b, step=step):
                goal = (z + step) % net.nz
                return (goal, y, c, b) if self.first <= goal < self.last else None

            came.append(net.move(part, target) if step else part)
        return came

    def z_halves(self, rows):
        net = self.net
        empty = [jnp.zeros((count,) + rows.shape[1:], BF) for count in (self.first, net.nz - self.last)]
        rows = jnp.concatenate([empty[0], rows, empty[1]], axis=0)
        step = net.nz // 2
        while step:
            upper = (net.z // step) % 2
            halves = rows.reshape((2, step) + rows.shape[1:])
            kept = pick(halves, upper)
            came = yield net.move(pick(halves, 1 - upper), lambda z, y, c, b, step=step: (z ^ step, y, c, b))
            rows = (kept.astype(F32) + came.astype(F32)).astype(BF)
            step //= 2
        return [rows[0]]

    def z_tree(self, rows):
        total = rows[0]
        for step in doublings(self.net.nz):

            def target(z, y, c, b, step=step):
                far = (z - self.first) % self.net.nz
                return ((z - step) % self.net.nz, y, c, b) if far % (2 * step) == step else None

            came = yield self.net.move(total, target)
            total = (total.astype(F32) + came.astype(F32)).astype(BF)
        return [total]

    def z_sum(self, rows):
        half = self.net.nz // 2
        came = yield self.z_send(rows, [half])
        rest = yield self.z_send(rows, [step for step in range(1, self.net.nz) if step != half])
        return came + rest + self.z_send(rows, [0])


def add_up(parts):
    return sum(part.astype(F32) for part in parts)


def sum_steps(net, array):
    targets = []
    for step in doublings(net.nz):
        targets.append(lambda z, y, c, b, step=step: (z ^ step, y, c, b))
    for step in doublings(net.nb):
        targets.append(lambda z, y, c, b, step=step: (z, y, c, b ^ step))
    targets.append(lambda z, y, c, b: (z, y, 1 - c, b))
    targets.append(lambda z, y, c, b: (z, 1 - y, c, b))
    for target in targets:
        array = array.astype(BF)
        came = yield net.move(array, target)
        array = array.astype(F32) + came.astype(F32)
    return array


def nn(a, b):
    return lax.dot_general(a, b, (((1,), (0,)), ((), ())), preferred_element_type=F32)


def nt(a, b):
    return lax.dot_general(a, b, (((1,), (1,)), ((), ())), preferred_element_type=F32)


def tn(a, b):
    return lax.dot_general(a, b, (((0,), (0,)), ((), ())), preferred_element_type=F32)


def two(a):
    high = a.astype(BF)
    return high, (a - high.astype(F32)).astype(BF)


def left_half(shape):
    return lax.broadcasted_iota(jnp.int32, shape, 1) < 64


def normed(values, gain, bias):
    mean = jnp.mean(values, axis=1, keepdims=True)
    centred = values - mean
    variance = jnp.mean(centred * centred, axis=1, keepdims=True)
    return centred * lax.rsqrt(variance + EPSILON) * gain + bias


def normed_back(values, gain, upstream):
    mean = jnp.mean(values, axis=1, keepdims=True)
    centred = values - mean
    variance = jnp.mean(centred * centred, axis=1, keepdims=True)
    scale = lax.rsqrt(variance + EPSILON)
    unit = centred * scale
    inner = upstream * gain
    grad = scale * (
        inner
        - jnp.mean(inner, axis=1, keepdims=True)
        - unit * jnp.mean(inner * unit, axis=1, keepdims=True)
    )
    return grad, jnp.sum(upstream * unit, axis=0, keepdims=True), jnp.sum(upstream, axis=0, keepdims=True)


def softmax_halves(values):
    left = left_half(values.shape)
    low = jnp.float32(-jnp.inf)
    top0 = jnp.max(jnp.where(left, values, low), axis=1, keepdims=True)
    top1 = jnp.max(jnp.where(left, low, values), axis=1, keepdims=True)
    raised = jnp.exp(values - jnp.where(left, top0, top1))
    sum0 = jnp.sum(jnp.where(left, raised, 0.0), axis=1, keepdims=True)
    sum1 = jnp.sum(jnp.where(left, 0.0, raised), axis=1, keepdims=True)
    return raised / jnp.where(left, sum0, sum1)


def softmax_halves_back(weights, upstream):
    left = left_half(weights.shape)
    product = weights * upstream
    sum0 = jnp.sum(jnp.where(left, product, 0.0), axis=1, keepdims=True)
    sum1 = jnp.sum(jnp.where(left, 0.0, product), axis=1, keepdims=True)
    return product - weights * jnp.where(left, sum0, sum1)


def lanes(ref, head):
    return ref[:, head * 128 : (head + 1) * 128]


def state_at(ref, seq, pair):
    start = pair % 3 * 128
    return ref[seq, pair // 3, start : start + 128, :]


def normaliser_at(ref, head):
    row = H // 2 * HD + head % 6
    parts = [ref[seq, head // 6, row : row + 1, :] for seq in range(2)]
    return jnp.concatenate([jnp.broadcast_to(part, (64, 128)) for part in parts], axis=0)


def store_state(ref, seq, pair, block, row):
    half = pair // 3
    start = pair % 3 * 128
    ref[seq, half, start : start + 64, :] = block[:64, :128]
    ref[seq, half, start + 64 : start + 128, :] = block[64:, 128:]
    tail = H // 2 * HD + pair % 3 * 2
    ref[seq, half, tail : tail + 1, :] = row[:, :128]
    ref[seq, half, tail + 1 : tail + 2, :] = row[:, 128:]


def clear_tail(ref):
    for seq in range(2):
        for half in range(2):
            ref[seq, half, 390:400, :] = jnp.zeros((10, 128), F32)


def head_kernel(gather, x_ref, norm_ref, map_ref, cols_ref, *refs):
    step = pl.program_id(0)
    if gather is None:
        w_ref, h_ref, proj_ref, fq_ref, fk_ref, state_ref = refs
    else:
        arrays, (h_ref, proj_ref, fq_ref, fk_ref, state_ref, held, sems) = refs[:-7], refs[-7:]
        each = block_copies(gather[0], 0, gather[1], arrays, held, sems)

    @pl.when(step == 0)
    def _():
        if gather is not None:
            each(0, lambda copy: copy.start())
        h_ref[...] = normed(x_ref[...], norm_ref[0:1, :], norm_ref[1:2, :]).astype(BF)
        if gather is not None:
            each(0, lambda copy: copy.wait())

    weights = w_ref[...] if gather is None else held[pl.ds(pl.multiple_of(step * D, D), D), :]
    proj_ref[...] = nt(h_ref[...], weights).astype(BF)

    def features(out_ref):
        for pair in range(PAIRS):
            part = lanes(proj_ref, pair)
            before = nn(jnp.concatenate([part, part], axis=1), map_ref[0, pair])
            for side in range(2):
                head = pair * 2 + side
                out_ref[:, head * 128 : (head + 1) * 128] = softmax_halves(
                    before[:, side * 128 : (side + 1) * 128]
                )

    @pl.when(step == 0)
    def _():
        features(fq_ref)

    @pl.when(step == 1)
    def _():
        features(fk_ref)

    @pl.when(step == 2)
    def _():
        clear_tail(state_ref)
        for seq in range(2):
            rows = slice(seq * 64, seq * 64 + 64)
            last = cols_ref[rows, 1:2]
            for pair in range(PAIRS):
                feats = fk_ref[rows, pair * 256 : (pair + 1) * 256].astype(BF).astype(F32) * last
                block = tn(proj_ref[rows, pair * 128 : (pair + 1) * 128], feats.astype(BF))
                store_state(state_ref, seq, pair, block, jnp.sum(feats, axis=0, keepdims=True))


def tail_kernel(
    x_ref, v_ref, fq_ref, fk_ref, state_ref, cols_ref, vis_ref, norm_ref, wo_ref, wu_ref, wd_ref,
    o_ref, rden_ref, att_ref, x1_ref, h2_ref, u_ref, g_ref, out_ref,
):
    @pl.when(pl.program_id(0) == 0)
    def _():
        visible = vis_ref[...]
        mark = cols_ref[:, 0:1]
        left = left_half((128, 128))
        for pair in range(PAIRS):
            value = lanes(v_ref, pair)
            nothing = jnp.zeros_like(value)
            state = [jnp.concatenate(two(state_at(state_ref, seq, pair)), axis=1) for seq in range(2)]
            weights = []
            totals = []
            carried = []
            for side in range(2):
                head = pair * 2 + side
                query = lanes(fq_ref, head).astype(BF)
                score = nt(query, lanes(fk_ref, head).astype(BF)) * visible
                weights.append(score.astype(BF))
                wide = query.astype(F32) * normaliser_at(state_ref, head) * mark
                totals.append(jnp.sum(score + wide, axis=1, keepdims=True))
                twice = jnp.concatenate([query, query], axis=1)
                carried.append(
                    jnp.concatenate([nt(twice[:64], state[0]), nt(twice[64:], state[1])], axis=0)
                )
            number = nn(
                jnp.concatenate(weights, axis=1),
                jnp.concatenate([jnp.where(left, value, nothing), jnp.where(left, nothing, value)], axis=0),
            )
            number = number + mark * jnp.where(left, carried[0], carried[1])
            inverse = 1.0 / jnp.where(left, totals[0], totals[1])
            output = number * inverse
            cut = slice(pair * 128, (pair + 1) * 128)
            o_ref[:, cut] = output
            rden_ref[:, cut] = inverse
            att_ref[:, cut] = output.astype(BF)
        x1 = x_ref[...] + nn(att_ref[...], wo_ref[...])
        x1_ref[...] = x1
        h2_ref[...] = normed(x1, norm_ref[0:1, :], norm_ref[1:2, :]).astype(BF)
        out_ref[...] = x1

    u = nt(h2_ref[...], wu_ref[...])
    u_ref[...] = u
    inner = jnp.tanh(0.7978845608028654 * (u + 0.044715 * (u * u * u)))
    g = (0.5 * u * (1.0 + inner)).astype(BF)
    g_ref[...] = g
    out_ref[...] += nn(g, wd_ref[...])


def back_kernel(
    e_ref, u_ref, x1_ref, norm_ref, wd_ref, wu_ref, wo_ref, o_ref, rden_ref, fq_ref, cols_ref,
    du_ref, dx1_ref, ebx_ref, dn_ref, dd_ref, state_ref, gn_ref, total,
):
    step = pl.program_id(0)
    dg = nt(e_ref[...].astype(BF), wd_ref[...])
    u = u_ref[...]
    inner = jnp.tanh(0.7978845608028654 * (u + 0.044715 * (u * u * u)))
    slope = 0.5 * (1.0 + inner) + (0.5 * u) * (1.0 - inner * inner) * (
        0.7978845608028654 * (1.0 + 0.134145 * (u * u))
    )
    du = (dg * slope).astype(BF)
    du_ref[...] = du
    part = nn(du, wu_ref[...])

    @pl.when(step == 0)
    def _():
        total[...] = part

    @pl.when(step > 0)
    def _():
        total[...] += part

    @pl.when(step == pl.num_programs(0) - 1)
    def _():
        grad, gain, bias = normed_back(x1_ref[...], norm_ref[0:1, :], total[...])
        gn_ref[0:1, :] = gain
        gn_ref[1:2, :] = bias
        dx1 = e_ref[...] + grad
        dx1_ref[...] = dx1
        low = dx1.astype(BF)
        ebx_ref[...] = low
        dn_ref[...] = nt(low, wo_ref[...]).astype(BF).astype(F32) * rden_ref[...]
        left = left_half((128, 128))
        lane = lax.broadcasted_iota(jnp.int32, (128, 128), 1)
        clear_tail(state_ref)
        columns = jnp.zeros((128, 128), F32)
        for pair in range(PAIRS):
            dn = lanes(dn_ref, pair)
            product = dn * lanes(o_ref, pair)
            d0 = -jnp.sum(jnp.where(left, product, 0.0), axis=1, keepdims=True)
            d1 = -jnp.sum(jnp.where(left, 0.0, product), axis=1, keepdims=True)
            columns = jnp.where(lane == pair * 2, d0, jnp.where(lane == pair * 2 + 1, d1, columns))
            for seq in range(2):
                rows = slice(seq * 64, seq * 64 + 64)
                mark = cols_ref[rows, 0:1]
                high, rest = two(dn[rows] * mark)
                feats = fq_ref[rows, pair * 256 : (pair + 1) * 256].astype(BF)
                block = tn(jnp.concatenate([high, rest], axis=0), jnp.concatenate([feats, feats], axis=0))
                wide = feats.astype(F32)
                row = jnp.concatenate(
                    [
                        jnp.sum(wide[:, :128] * (d0[rows] * mark), axis=0, keepdims=True),
                        jnp.sum(wide[:, 128:] * (d1[rows] * mark), axis=0, keepdims=True),
                    ],
                    axis=1,
                )
                store_state(state_ref, seq, pair, block, row)
        dd_ref[...] = columns


def fold_map(pair_weights, low_q):
    left = left_half((128, 128))
    folded = [weight - pltpu.roll(weight, 64, 1) for weight in pair_weights]
    grad = jnp.where(left, folded[0], pltpu.roll(folded[1], 64, 1))
    high, rest = two(grad)
    twice = jnp.concatenate([low_q, low_q], axis=0)
    table = tn(twice, jnp.concatenate([high, rest], axis=0))
    return jnp.where(left[:64], table[:64], table[64:])


def query_kernel(
    q_ref, v_ref, fq_ref, fk_ref, state_ref, dn_ref, dd_ref, cols_ref, vis_ref, map_ref,
    dq_ref, dmap_ref, dfk_ref, dv_ref,
):
    visible = vis_ref[...]
    low_visible = visible.astype(BF)
    mark = cols_ref[:, 0:1]
    left = left_half((128, 128))
    for pair in range(PAIRS):
        value = lanes(v_ref, pair)
        dn = lanes(dn_ref, pair)
        twice = jnp.concatenate([value, value], axis=1)
        state = [two(state_at(state_ref, seq, pair)) for seq in range(2)]
        weights = []
        shifts = []
        turned = []
        for side in range(2):
            head = pair * 2 + side
            wide = lanes(fq_ref, head)
            query = wide.astype(BF)
            key = lanes(fk_ref, head).astype(BF)
            score = (nt(query, key) * visible).astype(BF)
            mine = jnp.where(left, dn, 0.0) if side == 0 else jnp.where(left, 0.0, dn)
            high, rest = two(mine)
            dd = dd_ref[:, head : head + 1]
            shift = (nt(jnp.concatenate([high, rest], axis=1), twice) + dd).astype(BF) * low_visible
            carried = jnp.concatenate(
                [
                    nn(
                        jnp.concatenate([high[rows], high[rows], rest[rows]], axis=1),
                        jnp.concatenate([state[seq][0], state[seq][1], state[seq][0]], axis=0),
                    )
                    for seq, rows in ((0, slice(0, 64)), (1, slice(64, 128)))
                ],
                axis=0,
            )
            dfq = nn(shift, key) + mark * (carried + dd * normaliser_at(state_ref, head))
            dfk_ref[:, head * 128 : (head + 1) * 128] = tn(shift, query)
            weights.append(softmax_halves_back(wide, dfq))
            shifts.append(score)
            turned.append(high)
        cut = slice(pair * 128, (pair + 1) * 128)
        dv_ref[:, cut] = tn(jnp.concatenate(shifts, axis=0), jnp.concatenate(turned, axis=0))
        low = jnp.concatenate(weights, axis=1).astype(BF)
        dq_ref[:, cut] = nt(low, map_ref[0, pair, :128, :]).astype(BF)
        dmap_ref[:, cut] = fold_map(weights, lanes(q_ref, pair))


def key_kernel(
    k_ref, v_ref, fk_ref, state_ref, dfk_ref, dv_ref, dq_ref, cols_ref, map_ref, w_ref, x_ref, norm_ref, dx1_ref,
    dqkv_ref, dmap_ref, e_ref, gn_ref,
):
    last = cols_ref[:, 1:2]
    left = left_half((128, 128))
    dqkv_ref[:, :D] = dq_ref[...]
    for pair in range(PAIRS):
        value = lanes(v_ref, pair)
        nothing = jnp.zeros_like(value)
        state = [two(state_at(state_ref, seq, pair)) for seq in range(2)]
        weights = []
        grads = []
        for side in range(2):
            head = pair * 2 + side
            wide = lanes(fk_ref, head)
            key = wide.astype(BF)
            mine = jnp.where(left, value, nothing) if side == 0 else jnp.where(left, nothing, value)
            carried = []
            turned = []
            for seq, rows in ((0, slice(0, 64)), (1, slice(64, 128))):
                high, rest = state[seq]
                carried.append(
                    nn(
                        jnp.concatenate([mine[rows], mine[rows]], axis=1),
                        jnp.concatenate([high, rest], axis=0),
                    )
                )
                turned.append(nt(key[rows], high))
            carried = jnp.concatenate(carried, axis=0)
            dfk = lanes(dfk_ref, head) + last * (carried + normaliser_at(state_ref, head))
            weights.append(softmax_halves_back(wide, dfk))
            grads.append(jnp.concatenate(turned, axis=0))
        cut = slice(pair * 128, (pair + 1) * 128)
        dv = lanes(dv_ref, pair) + last * jnp.where(left, grads[0], grads[1])
        dqkv_ref[:, 2 * D + pair * 128 : 2 * D + (pair + 1) * 128] = dv.astype(BF)
        low = jnp.concatenate(weights, axis=1).astype(BF)
        dqkv_ref[:, D + pair * 128 : D + (pair + 1) * 128] = nt(low, map_ref[0, pair, :128, :]).astype(BF)
        dmap_ref[:, cut] = fold_map(weights, lanes(k_ref, pair))
    upstream = nn(dqkv_ref[...], w_ref[...])
    grad, gain, bias = normed_back(x_ref[...], norm_ref[0:1, :], upstream)
    gn_ref[0:1, :] = gain
    gn_ref[1:2, :] = bias
    e_ref[...] = dx1_ref[...] + grad


def store_sides(block, keep_ref, send_ref):
    zero = lax.rem(lax.axis_index("seq"), 2) == 0
    groups, size = keep_ref.shape[:2]
    for group in range(groups):
        low = block[group * 2 * size : group * 2 * size + size]
        high = block[group * 2 * size + size : group * 2 * size + 2 * size]
        keep_ref[group] = jnp.where(zero, low, high).astype(BF)
        send_ref[group] = jnp.where(zero, high, low).astype(BF)


def rows_kernel(att_ref, ebx_ref, du_ref, h2_ref, g_ref, e_ref, keep_ref, send_ref, held):
    terms = ((0, D, att_ref, ebx_ref), (D, D + FF, du_ref, h2_ref), (D + FF, D + 2 * FF, g_ref, e_ref))
    for step in range((D + 2 * FF) // TILE):
        start = step * TILE

        @pl.when(pl.program_id(0) == step)
        def _(start=start):
            for first, last, left, right in terms:
                low = max(start, first)
                high = min(start + TILE, last)
                if low < high:
                    held[low - start : high - start, :] = tn(
                        left[:, low - first : high - first], right[...].astype(BF)
                    )
            store_sides(held, keep_ref, send_ref)


def proj_rows_kernel(dqkv_ref, h_ref, keep_ref, send_ref, held):
    held[...] = tn(dqkv_ref[...], h_ref[...])
    store_sides(held, keep_ref, send_ref)


def split_kernel(runs, nb, *refs):
    tops = refs[2 * len(runs) : 2 * len(runs) + nb]
    bottoms = refs[2 * len(runs) + nb :]
    upper, lower = tops[0].shape[2], bottoms[0].shape[2]
    y = lax.rem(lax.axis_index("seq") // 2, 2)
    b = lax.axis_index("batch")
    start = 0
    for index, count in enumerate(runs):
        keep, came = refs[2 * index : 2 * index + 2]

        @pl.when((pl.program_id(0) >= start) & (pl.program_id(0) < start + count))
        def _(keep=keep, came=came):
            def rows(row_y, row_b, offset, count):
                at = pl.ds(pl.multiple_of(row_b * (upper + lower) + offset, 16), count)
                return (keep[row_y, at, :].astype(F32) + came[row_y, at, :].astype(F32)).astype(BF)

            for step, top in enumerate(tops):
                for side in range(2):
                    top[0, side] = rows(side, lax.rem(b + step, nb), 0, upper)
            for step, bottom in enumerate(bottoms):
                for side in range(nb):
                    bottom[0, side] = rows(lax.rem(y + step, 2), side, upper, lower)

        start += count


def split_call(net, pairs, share):
    size = pairs[0][0].shape[1]
    upper = size // net.nb * share // 18
    lower = size // net.nb - upper
    runs = [keep.shape[0] // 2 for keep, _ in pairs]
    planes = sum(runs)
    operands = []
    start = 0
    for pair, count in zip(pairs, runs):

        def index(i, start=start, count=count):
            return (jnp.clip(i - start, 0, count - 1), 0, 0)

        operands += [(array, (2, size, D), index) for array in pair]
        start += count
    outputs = [((planes, 2, upper, D), BF, (1, 2, upper, D), lambda i: (i, 0, 0, 0))] * net.nb
    outputs += [((planes, net.nb, lower, D), BF, (1, net.nb, lower, D), lambda i: (i, 0, 0, 0))] * 2
    parts = call(functools.partial(split_kernel, runs, net.nb), (planes,), operands, outputs, 0)
    return parts[: net.nb], parts[net.nb :]


def fold_kernel(top_keep, top_came, bottom_keep, bottom_came, *outs):
    y = lax.rem(lax.axis_index("seq") // 2, 2)
    b = lax.axis_index("batch")
    for step in range(2):
        at = lax.rem(y + step, 2)
        outs[step][0] = (top_keep[0, at].astype(F32) + top_came[0, at].astype(F32)).astype(BF)
        at = lax.rem(b + step, 2)
        outs[2 + step][0] = (bottom_keep[0, at].astype(F32) + bottom_came[0, at].astype(F32)).astype(BF)


def fold_call(came):
    operands = []
    outputs = []
    for pair in came:
        shape = pair[0].shape
        operands += [(array, (1,) + shape[1:], lambda i: (i, 0, 0, 0)) for array in pair]
        outputs += [((shape[0],) + shape[2:], BF, (1,) + shape[2:], lambda i: (i, 0, 0))] * 2
    parts = call(fold_kernel, (shape[0],), operands, outputs, 0)
    return parts[:2], parts[2:]


def whole(array):
    rank = array.ndim
    return pl.BlockSpec(array.shape, lambda *_: (0,) * rank)


def call(kernel, grid, operands, outputs, flops, scratch=(), free=(), limit=WIDE_LIMIT):
    arrays = []
    in_specs = []
    for operand in operands:
        if isinstance(operand, tuple):
            arrays.append(operand[0])
            in_specs.append(pl.BlockSpec(operand[1], operand[2]))
        else:
            arrays.append(operand)
            in_specs.append(whole(operand))
    arrays += free
    in_specs += [pl.BlockSpec(memory_space=pl.ANY)] * len(free)
    shapes = [jax.ShapeDtypeStruct(out[0], out[1]) for out in outputs]
    out_specs = []
    for out, shape in zip(outputs, shapes):
        out_specs.append(pl.BlockSpec(out[2], out[3]) if len(out) > 2 else whole(shape))
    moved = sum(a.size * a.dtype.itemsize for a in shapes)
    for spec, a in zip(in_specs, arrays):
        moved += a.size * a.dtype.itemsize if a.shape[0] < 6000 else 6 * D * D
    return pl.pallas_call(
        kernel,
        grid=grid,
        in_specs=in_specs,
        out_specs=out_specs,
        out_shape=shapes,
        scratch_shapes=list(scratch),
        compiler_params=pltpu.CompilerParams(vmem_limit_bytes=limit),
        cost_estimate=pl.CostEstimate(flops=flops, bytes_accessed=moved, transcendentals=0),
    )(*arrays)


STATE = (2, 2, H // 2 * HD + 16, 128)
ROWS = 128
CHUNK = D
TILE = 3 * D // 2
CHUNKS = FF // CHUNK


def still(*index):
    return lambda i: index


def head_call(x, flat, norms, maps, cols, gather=None):
    operands = [
        x,
        norms[0],
        (maps, (1, PAIRS, 256, 256), lambda i: (jnp.minimum(i, 1), 0, 0, 0)),
        cols,
    ]
    outputs = [
        ((ROWS, D), BF),
        ((ROWS, 3 * D), BF, (ROWS, D), lambda i: (0, i)),
        ((ROWS, H * 128), F32),
        ((ROWS, H * 128), F32),
        (STATE, F32),
    ]
    flops = 2 * ROWS * 3 * D * D
    if gather is None:
        operands.append((flat[0], (D, D), lambda i: (i, 0)))
        return call(functools.partial(head_kernel, None), (3,), operands, outputs, flops)
    plan = (gather.parts, gather.shard.shape[0])
    scratch = [pltpu.VMEM((3 * D, D), BF), pltpu.SemaphoreType.DMA((1, 10))]
    return call(
        functools.partial(head_kernel, plan), (3,), operands, outputs, flops, scratch, gather.arrays, 60 * 1024 * 1024
    )


def tail_call(x, flat, norms, cols, visible, head, state):
    h1, proj, fq, fk, local = head
    o, rden, att, x1, h2, u, g, result = call(
        tail_kernel,
        (CHUNKS,),
        [
            x,
            (proj, (ROWS, D), still(0, 2)),
            fq,
            fk,
            state,
            cols,
            visible,
            norms[1],
            (flat[1], (D, D), still(0, 0)),
            (flat[1], (CHUNK, D), lambda i: (1 + i, 0)),
            (flat[1], (CHUNK, D), lambda i: (1 + CHUNKS + i, 0)),
        ],
        [
            ((ROWS, D), F32),
            ((ROWS, D), F32),
            ((ROWS, D), BF),
            ((ROWS, D), F32),
            ((ROWS, D), BF),
            ((ROWS, FF), F32, (ROWS, CHUNK), lambda i: (0, i)),
            ((ROWS, FF), BF, (ROWS, CHUNK), lambda i: (0, i)),
            ((ROWS, D), F32),
        ],
        2 * ROWS * 9 * D * D,
    )
    return result, (x, h1, proj, fq, fk, state, o, rden, att, x1, h2, u, g)


def back_call(e, flat, norms, cols, kept):
    x, h1, proj, fq, fk, state, o, rden, att, x1, h2, u, g = kept
    return call(
        back_kernel,
        (CHUNKS,),
        [
            e,
            (u, (ROWS, CHUNK), lambda i: (0, i)),
            x1,
            norms[1],
            (flat[1], (CHUNK, D), lambda i: (1 + CHUNKS + i, 0)),
            (flat[1], (CHUNK, D), lambda i: (1 + i, 0)),
            (flat[1], (D, D), still(0, 0)),
            o,
            rden,
            fq,
            cols,
        ],
        [
            ((ROWS, FF), BF, (ROWS, CHUNK), lambda i: (0, i)),
            ((ROWS, D), F32),
            ((ROWS, D), BF),
            ((ROWS, D), F32),
            ((ROWS, 128), F32),
            (STATE, F32),
            ((2, D), F32),
        ],
        2 * ROWS * 9 * D * D,
        [pltpu.VMEM((ROWS, D), F32)],
    )


def query_call(maps, cols, visible, kept, back):
    proj, fq, fk, state = kept[2:6]
    dn, dd = back[3:5]
    return call(
        query_kernel,
        (1,),
        [
            (proj, (ROWS, D), still(0, 0)),
            (proj, (ROWS, D), still(0, 2)),
            fq,
            fk,
            state,
            dn,
            dd,
            cols,
            visible,
            (maps, (1, PAIRS, 256, 256), still(0, 0, 0, 0)),
        ],
        [((ROWS, D), BF), ((HD, D), F32), ((ROWS, H * 128), F32), ((ROWS, D), F32)],
        2 * ROWS * 4 * D * D,
    )


def sides(net, count):
    side = (4 * D + 2 * FF) // (4 * net.nz)
    shape = (count // (2 * side), side, D)
    return [(shape, BF, (TILE // (2 * side), side, D), lambda i: (i, 0, 0))] * 2


def rows_call(net, e, kept, back):
    att, h2, g = kept[8], kept[10], kept[12]
    du, ebx = back[0], back[2]
    return call(
        rows_kernel,
        ((D + 2 * FF) // TILE,),
        [att, ebx, du, h2, g, e],
        sides(net, D + 2 * FF),
        2 * ROWS * 9 * D * D,
        [pltpu.VMEM((TILE, D), F32)],
    )


def key_call(flat, norms, maps, cols, kept, back, query, state_grad):
    x, proj, fk = kept[0], kept[2], kept[4]
    dx1 = back[1]
    dq, query_map, dfk, dv = query
    return call(
        key_kernel,
        (1,),
        [
            (proj, (ROWS, D), still(0, 1)),
            (proj, (ROWS, D), still(0, 2)),
            fk,
            state_grad,
            dfk,
            dv,
            dq,
            cols,
            (maps, (1, PAIRS, 256, 256), still(1, 0, 0, 0)),
            (flat[0], (3 * D, D), still(0, 0)),
            x,
            norms[0],
            dx1,
        ],
        [((ROWS, 3 * D), BF), ((HD, D), F32), ((ROWS, D), F32), ((2, D), F32)],
        2 * ROWS * 3 * D * D,
    )


def proj_rows_call(net, kept, dqkv):
    return call(
        proj_rows_kernel,
        (3 * D // TILE,),
        [(dqkv, (ROWS, TILE), lambda i: (0, i)), kept[1]],
        sides(net, 3 * D),
        2 * ROWS * 3 * D * D,
        [pltpu.VMEM((TILE, D), F32)],
    )


def pair_maps(fmap):
    grid = fmap.reshape(LAYERS, 2, HD, PAIRS, 2, HD).transpose(0, 1, 3, 4, 2, 5)
    both = jnp.concatenate([grid, -grid], axis=-1)
    empty = jnp.zeros_like(both[:, :, :, 0])
    top = jnp.concatenate([both[:, :, :, 0], empty], axis=-1)
    bottom = jnp.concatenate([empty, both[:, :, :, 1]], axis=-1)
    return jnp.concatenate(two(jnp.concatenate([top, bottom], axis=3)), axis=3)


def doc_layout(doc_lengths, start, span):
    ends = jnp.cumsum(doc_lengths, axis=1)
    places = start + jnp.arange(span, dtype=jnp.int32)
    documents = jnp.sum((places[None, :, None] >= ends[:, None, :]).astype(jnp.int32), axis=2)
    before = jnp.sum((start - 1 >= ends).astype(jnp.int32), axis=1)
    previous = jnp.where(start > 0, before, -1)
    mark = (documents == previous[:, None]).reshape(-1, 1)
    last = (documents == documents[:, span - 1 :]).reshape(-1, 1)
    lane = jnp.arange(128)[None, :]
    cols = jnp.where(lane == 0, mark, (lane == 1) & last).astype(F32)
    names = (documents + (DOCS + 1) * jnp.arange(documents.shape[0])[:, None]).reshape(-1)
    lower = jnp.arange(names.shape[0])[:, None] >= jnp.arange(names.shape[0])[None, :]
    visible = (lower & (names[:, None] == names[None, :])).astype(F32)
    return cols, visible


def body(tokens, doc_lengths, weights, norm_gain, norm_bias, fmap, cotangent):
    net = Net()
    sequences, span = tokens.shape[:2]
    start = lax.axis_index("seq") * span
    rows = sequences * span
    def prepare(doc_lengths, fmap, norm_gain, norm_bias, tokens, cotangent):
        cols, visible = doc_layout(doc_lengths, start, span)
        last_doc = last_docs(doc_lengths, span)
        gates = [scan_gates(net, last_doc, reverse) for reverse in (False, True)]
        maps = pair_maps(fmap)
        norms = jnp.stack([norm_gain, norm_bias], axis=2)
        x, e = [array.reshape(rows, D).astype(F32) for array in (tokens, cotangent)]
        return cols, visible, gates, maps, norms, x, e

    given = (doc_lengths, fmap, norm_gain, norm_bias, tokens, cotangent)
    steps = len(list(doublings(net.nz)))
    if net.nz == 4 and net.nb == 2 and weights.shape[1] % 32 == 0:
        first, second = [Gather(net, weights[layer]) for layer in range(LAYERS)]
        half = first.half
        own = first.shard[None]
        sides = first.sides(own)
        next_z = [first.along_z(first.shard, step) for step in (1, 3)]
        own, sides, shard = tie(own, sides, first.shard)
        corners = first.corners(first.cuts(sides))
        prepared = prepare(*given)
        own, sides, corners, next_z, shard, prepared = tie(own, sides, corners, next_z, shard, prepared)
        cols, visible, gates, maps, norms, x, e1 = prepared
        far = first.along_z(shard, 2)[None]
        next_z = jnp.stack(next_z)
        next_sides = first.sides(next_z)
        packed = jnp.concatenate([own, *sides, jnp.concatenate(corners, axis=1)], axis=0)
        swapped = net.core(packed)
        next_z, next_sides, far, shard, swapped = tie(next_z, next_sides, far, second.shard, swapped)
        spots = [(0, 0, 0, 0), (0, 0, 1, 0), (0, 1, 0, 0), (0, 1, 1, 0)]
        first.note(swapped, spots, 1)
        for array, spot in zip((own, *sides, *corners), spots + [(0, 1, 1, half)]):
            first.note(array, [spot])

        next_cuts = [cut.reshape(far.shape) for cut in first.cuts(next_sides)]
        cuts = [jnp.concatenate([cut, far], axis=0) for cut in next_cuts]
        cuts, next_z, next_sides = tie(cuts, next_z, next_sides)
        over_y, over_b = first.corners(cuts)
        second_z = [second.along_z(shard, step) for step in (1, 3)]
        packed = jnp.concatenate([next_z, *next_sides], axis=0)
        swapped = net.core(packed)
        over_y, over_b, second_z, swapped, far = tie(over_y, over_b, second_z, swapped, far)
        spots = [(step, *apart, 0) for apart in ((0, 0), (0, 1), (1, 0)) for step in (1, 3)]
        first.note(swapped, spots, 1)
        for index, array in enumerate((next_z, *next_sides)):
            first.note(array, spots[2 * index : 2 * index + 2])

        cuts = over_b[1:, :half], over_y[1:, half:]
        corners = first.corners(cuts)
        swapped = [net.core(array) for array in (over_y, over_b, far)]
        own = shard[None]
        second_z.append(second.along_z(shard, 2))
        corners, swapped = tie(corners, swapped)
        spots = [(1, 1, 1, 0), (3, 1, 1, 0)], [(1, 1, 1, half), (3, 1, 1, half)]
        sides = [(2, 1, 0, 0)], [(2, 0, 1, 0)]
        for index, array in enumerate((over_y, over_b)):
            for kept, apart in ((array, 0), (swapped[index], 1)):
                first.note_pair(kept, spots[index], sides[index], apart)
        first.both(far, swapped[2], [(2, 0, 0, 0)])
        for array, row in zip(corners, (0, half)):
            first.both(array, net.core(array), [(2, 1, 1, row)])

        sides = second.sides(own)
        kept0 = head_call(x, None, norms[0], maps[0], cols, first)
        scan = scan_steps(net, kept0[4], gates[0], False)
        came = next(scan)
        came, own, sides, second_z = tie(came, own, sides, second_z)
        corners = second.corners(second.cuts(sides))
        second_z = jnp.stack(second_z)
        came = scan.send(came)
        came, own, sides, corners, second_z = tie(came, own, sides, corners, second_z)
        second_sides = second.sides(second_z)
        packed = jnp.concatenate([own, *sides, jnp.concatenate(corners, axis=1)], axis=0)
        for _ in range(steps):
            came = scan.send(came)
        rest = first.rows(1, net.nz)
        came, rest = tie(came, rest)
        came = scan.send(came)
        came, second_z, second_sides, packed = tie(came, second_z, second_sides, packed)
        second_corners = second.corners(second.cuts(second_sides))
        swapped = net.core(packed), net.core(jnp.concatenate([second_z, *second_sides], axis=0))
        state = finish(scan, came)
        x1, kept0 = tail_call(x, (None, rest), norms[0], cols, visible, kept0, state)
        x1, second_corners, swapped = tie(x1, second_corners, swapped)
        spots = [(0, 0, 0, 0), (0, 0, 1, 0), (0, 1, 0, 0), (0, 1, 1, 0)]
        second.note(swapped[0], spots, 1)
        for array, spot in zip((own, *sides, *corners), spots + [(0, 1, 1, half)]):
            second.note(array, [spot])
        spots = [(step, *apart, 0) for apart in ((0, 0), (0, 1), (1, 0)) for step in (1, 3, 2)]
        second.note(swapped[1], spots, 1)
        for index, array in enumerate((second_z, *second_sides)):
            second.note(array, spots[3 * index : 3 * index + 3])
        for array, row in zip(second_corners, (0, half)):
            second.both(array, net.core(array), [(step, 1, 1, row) for step in (1, 3, 2)])
        gathered = [rest]
        kept1 = head_call(x1, None, norms[1], maps[1], cols, second)
        scan = scan_steps(net, kept1[4], gates[0], False)
        came = scan.send(next(scan))
        came, head = tie(came, first.rows(0, 1))
        gathered[0] = (head, rest)
        came = scan.send(came)
        head = second.rows(0, 1)
        came, head = tie(came, head)
        for _ in range(1, steps):
            came = scan.send(came)
        rest = second.rows(1, net.nz)
        came, rest = tie(came, rest)
        state = finish(scan, came)
        gathered.append((head, rest))
    else:
        gathered = [lax.all_gather(weights[layer], AXES, axis=0, tiled=True) for layer in range(LAYERS)]
        gathered = [(flat[: 3 * D], flat[3 * D :]) for flat in gathered]
        cols, visible, gates, maps, norms, x, e1 = prepare(*given)
        kept0 = head_call(x, gathered[0], norms[0], maps[0], cols)
        state = finish(scan_steps(net, kept0[4], gates[0], False), None)
        x1, kept0 = tail_call(x, gathered[0], norms[0], cols, visible, kept0, state)
        kept1 = head_call(x1, gathered[1], norms[1], maps[1], cols)
        state = finish(scan_steps(net, kept1[4], gates[0], False), None)
    x, kept1 = tail_call(x1, gathered[1], norms[1], cols, visible, kept1, state)
    result = x.astype(BF).reshape(tokens.shape)
    cut = net.nz * 3 * D // (4 * D + 2 * FF)
    rest_sum = Scatter(net, cut, net.nz, 10)
    both_sum = Scatter(net, 0, net.nz, 10)
    head_sum = Scatter(net, 0, cut)

    back1 = back_call(e1, gathered[1], norms[1], cols, kept1)
    scan = scan_steps(net, back1[5], gates[1], True)
    came = next(scan)
    came, held = tie(came, e1)
    came = scan.send(came)
    keep, send = rows_call(net, held, kept1, back1)
    came, keep, send, back1 = tie(came, keep, send, back1)
    came = scan.send(came)
    swapped = net.core(send)
    query1 = query_call(maps[1], cols, visible, kept1, back1)
    came, query1, keep, swapped = tie(came, query1, keep, swapped)
    for _ in range(1, len(list(doublings(net.nz)))):
        came = scan.send(came)
    tops, bottoms = rest_sum.split([(keep, swapped)])
    came, tops, bottoms = tie(came, tops, bottoms)
    came = scan.send(came)
    came, bottoms = tie(came, bottoms)
    rest1 = rest_sum.first_send((tops, bottoms))
    state_grad = finish(scan, came)
    dqkv1, key_map1, e0, norm_one1 = key_call(
        gathered[1], norms[1], maps[1], cols, kept1, back1, query1, state_grad
    )
    small1 = jnp.concatenate([query1[1], key_map1, norm_one1, back1[6]], axis=0)

    back0 = back_call(e0, gathered[0], norms[0], cols, kept0)
    back0, dqkv1 = tie(back0, dqkv1)
    scan = scan_steps(net, back0[5], gates[1], True)
    came = next(scan)
    keep1, send1 = proj_rows_call(net, kept1, dqkv1)
    came, keep1, send1, held = tie(came, keep1, send1, e0)
    came = scan.send(came)
    swapped1 = net.core(send1)
    keep0, send0 = rows_call(net, held, kept0, back0)
    came, keep0, send0, rest1 = tie(came, keep0, send0, rest1)
    came = scan.send(came)
    swapped0 = net.core(send0)
    rest1 = rest_sum.first_add(rest1)
    came, rest1, keep0, swapped0, keep1, swapped1 = tie(came, rest1, keep0, swapped0, keep1, swapped1)
    for _ in range(1, len(list(doublings(net.nz)))):
        came = scan.send(came)
    rest1 = rest_sum.second_send(rest1)
    tops, bottoms = both_sum.split([(keep1, swapped1), (keep0, swapped0)])
    came, tops, bottoms, back0, rest1 = tie(came, tops, bottoms, back0, rest1)
    came = scan.send(came)
    query0 = query_call(maps[0], cols, visible, kept0, back0)
    rest1 = rest_sum.second_add(rest1)
    came, bottoms, query0, rest1 = tie(came, bottoms, query0, rest1)
    both = both_sum.first_send((tops, bottoms))
    rest1 = rest_sum.z_halves(rest1)
    apart = next(rest1)
    state_grad = finish(scan, came)
    dqkv0, key_map0, e, norm_one0 = key_call(
        gathered[0], norms[0], maps[0], cols, kept0, back0, query0, state_grad
    )

    small0 = jnp.concatenate([query0[1], key_map0, norm_one0, back0[6]], axis=0)
    summing = sum_steps(net, jnp.stack([small0, small1]))
    small = next(summing)
    keep, send = proj_rows_call(net, kept0, dqkv0)
    both, keep, send = tie(both, keep, send)
    both = both_sum.first_add(both)
    both, send, apart, small = tie(both, send, apart, small)
    both = both_sum.second_send(both)
    swapped = net.core(send)
    apart = rest1.send(apart)
    small = summing.send(small)
    head0 = head_sum.split([(keep, swapped)])
    head0, apart = tie(head0, apart)
    both = after(both, head0)
    head0 = head_sum.first_send(head0)
    rest1 = finish(rest1, apart)
    both = both_sum.second_add(both)
    both, small = tie(both, small)
    both = both_sum.z_sum(both)
    far = next(both)
    head0 = head_sum.first_add(head0)
    small = summing.send(after(small, head0))
    small, far = tie(small, far)
    near = both.send(far)
    head0 = head_sum.second_add(head_sum.second_send(head0))
    if cut == 1:
        head0 = head_sum.z_tree(head0)
    else:
        head0 = head_sum.z_sum(head0)
    came = next(head0)
    came, near = tie(came, near)
    both = finish(both, near)
    head0 = finish(head0, came)
    small = finish(summing, small)

    both = add_up(both)
    shards = [
        jnp.where(net.z < cut, add_up(head0), both),
        jnp.where(net.z < cut, both, add_up(rest1)),
    ]
    cut = 2 * HD
    return (
        result,
        e.reshape(tokens.shape),
        jnp.stack(shards),
        small[:, cut::2],
        small[:, cut + 1 :: 2],
        small[:, :cut].reshape(fmap.shape),
    )


def solution(mesh):
    in_specs = (
        P("batch", "seq", None),
        P("batch", None),
        P(None, ("seq", "batch"), None),
        P(),
        P(),
        P(),
        P("batch", "seq", None),
    )
    out_specs = (
        P("batch", "seq", None),
        P("batch", "seq", None),
        P(None, ("seq", "batch"), None),
        P(),
        P(),
        P(),
    )
    return jax.shard_map(body, mesh=mesh, in_specs=in_specs, out_specs=out_specs, check_vma=False)
```
